32 devices in a mesh: dp: 8 (over y, x, core), tensor: 4 (over z).
Axes of the slice: x: 2, y: 2, z: 4, core: 2. Of those that a mesh axis runs over, the one named last changes fastest.
Arguments:
- activations: bfloat16 [4096, 768], P('dp'), may hold values from -6 to 6
- noise_times: float32 [16], P('dp'), may hold values from 0 to 1
- cath_labels: int32 [16], P('dp'), may hold values from 0 to 3
- class_table: bfloat16 [4, 256], replicated, may hold values from -6 to 6
- ada_weight: bfloat16 [256, 6, 768], replicated, may hold values from -0.375 to 0.375
- qkvg_weight: bfloat16 [768, 4, 768], P(None, None, 'tensor'), may hold values from -0.21875 to 0.21875
- out_weight: bfloat16 [768, 768], P('tensor'), may hold values from -1.75 to 1.75
- pair_weight: bfloat16 [256, 12], P('tensor'), may hold values from -2 to 2
- gateup_weight: bfloat16 [768, 2, 3072], P(None, None, 'tensor'), may hold values from -0.21875 to 0.21875
- down_weight: bfloat16 [3072, 768], P('tensor'), may hold values from -0.21875 to 0.21875
- pair_features: bfloat16 [16, 256, 256, 256], P('dp', 'tensor'), may hold values from -6 to 6
- cotangent: bfloat16 [4096, 768], P('dp'), may hold values from -6 to 6
Outputs:
- output: bfloat16 [4096, 768], P('dp')
- activations_grad: bfloat16 [4096, 768], P('dp')
- pair_features_grad: bfloat16 [16, 256, 256, 256], P('dp', 'tensor')
- class_table_grad: float32 [4, 256], P(None, 'dp')
- ada_weight_grad: float32 [256, 6, 768], P('dp')
- qkvg_weight_grad: float32 [768, 4, 768], P('dp', None, 'tensor')
- out_weight_grad: float32 [768, 768], P('tensor', 'dp')
- pair_weight_grad: float32 [256, 12], P('tensor')
- gateup_weight_grad: float32 [768, 2, 3072], P('dp', None, 'tensor')
- down_weight_grad: float32 [3072, 768], P('tensor', 'dp')
The draws below stay inside these ranges and needn't reach their ends.
All inputs are finite; a program needn't handle non-finite values.
Results may differ from the reference program's by a relative error of at most 0.024.
Values may be sent and summed in bfloat16 or wider, within the bound.
A program may use at most 192 MiB of HBM per device.

```python
import math
import jax
import jax.numpy as jnp
from jax import lax

D = 768
HEADS = 12
HD = 64
FF = 3072
PAIR = 256
DC = 256
NCLASS = 4
L = 256
CHAINS = 16
TOKENS = 4096


def draw_pair_features(key, part):
    key = jax.random.fold_in(key, 11)
    noise_key, spike_key, order_key = jax.random.split(key, 3)
    quarter_width = PAIR // 4
    full_shape = (CHAINS, 4, quarter_width, L, L)
    background = jnp.clip(jax.random.normal(noise_key, full_shape, jnp.float32), -6.0, 6.0)
    spike_values = jax.random.uniform(spike_key, full_shape, jnp.float32, 2.5, 3.5)
    chain_keys = jax.random.split(order_key, CHAINS * 4)
    targets = jax.vmap(lambda single_key: jax.random.permutation(single_key, L))(chain_keys)
    targets = targets.reshape(CHAINS, 4, L).astype(jnp.int32)
    landing = targets[:, :, :, None] == jnp.arange(L, dtype=jnp.int32)[None, None, None, :]
    values = jnp.where(landing[:, :, None], spike_values, background)
    return values.reshape(CHAINS, PAIR, L, L).astype(jnp.bfloat16)


def draw_pair_weight(key, part):
    key = jax.random.fold_in(key, 23)
    noise_key, offset_key = jax.random.split(key, 2)
    spread = PAIR ** (-0.5)
    random_part = jnp.clip(jax.random.normal(noise_key, (PAIR, HEADS), jnp.float32), -4.0, 4.0)
    offsets = jax.random.uniform(offset_key, (4, HEADS), jnp.float32, 0.4, 0.8)
    quarter_index = jnp.arange(PAIR, dtype=jnp.int32) // (PAIR // 4)
    return (spread * (random_part + offsets[quarter_index])).astype(jnp.bfloat16)


def place_ends(entries, key, least, top_value):
    longest = entries.shape.index(max(entries.shape))
    spots = []
    for shift in (0, 1):
        where = [jax.random.randint(jax.random.fold_in(key, axis), (), 0, length) for axis, length in enumerate(entries.shape)]
        where[longest] = (where[longest] + shift) % entries.shape[longest]
        spots.append(tuple(where))
    return entries.at[spots[0]].set(least).at[spots[1]].set(top_value)


def with_spikes(entries, key, source, target, parts, factor):
    owner, partner = [(jnp.arange(entries.shape[axis_at]) // (entries.shape[axis_at] // parts)).reshape([-1 if axis == axis_at else 1 for axis in range(entries.ndim)]) for axis_at in (source, target)]
    chosen = jax.random.permutation(key, parts)[partner]
    strong = (owner == chosen) | (owner == (partner + parts // 2) % parts)
    return jnp.where(strong, factor * entries, entries)


def levels(key, shape, shards, low, high):
    loudness, own = 1.0, jax.random.fold_in(key, 6)
    for position, shards_of in shards:
        steps = jnp.exp(jax.random.uniform(jax.random.fold_in(own, position), (shards_of,), jnp.float32, low / len(shards), high / len(shards)))
        loudness = loudness * jnp.repeat(steps, shape[position] // shards_of).reshape([-1 if axis == position else 1 for axis in range(len(shape))])
    return loudness


def bell_draw(own_key, dims, width, most, cuts=(), held_as=jnp.bfloat16):
    entries = width * jax.random.normal(own_key, dims, jnp.float32)
    if cuts:
        entries = entries * levels(own_key, dims, cuts, -0.22, 0.18)
    return jnp.clip(entries, -most, most).astype(held_as)


def heavy_noise(rng, extent, width, reach, cuts, heavy, kind=jnp.bfloat16):
    entries = width * jax.random.normal(rng, extent, jnp.float32)
    if cuts:
        entries = entries * levels(rng, extent, cuts, -0.22, 0.18)
    return jnp.clip(with_spikes(entries, jax.random.fold_in(rng, 3), *heavy), -reach, reach).astype(kind)


def setup_inputs(seed: int = 0) -> dict:
    streams_of = jax.random.split(jax.random.key(seed), 13)
    activations = heavy_noise(streams_of[0], (TOKENS, D), 1.0, 6.0, ((0, 8),), (0, 1, 8, 2.0))
    noise_times = jnp.clip(1.0 * jax.random.uniform(streams_of[1], (CHAINS,), jnp.float32) ** levels(streams_of[1], (CHAINS,), ((0, 8),), -0.2, 0.2), 0.0, 1.0)
    cath_labels = place_ends(jax.random.randint(streams_of[2], (CHAINS,), 0, NCLASS), jax.random.fold_in(streams_of[2], 1), 0, NCLASS - 1).astype(jnp.int32)
    class_table = bell_draw(streams_of[3], (NCLASS, DC), 1.0, 6.0)
    ada_weight = bell_draw(streams_of[4], (DC, 6, D), DC ** -0.5, 0.375)
    qkvg_weight = bell_draw(streams_of[5], (D, 4, D), D ** -0.5, 0.21875, ((2, 4),))
    out_weight = bell_draw(streams_of[6], (D, D), (max(D // 64, 4)) ** -0.5, 1.75, ((0, 4),))
    pair_weight = draw_pair_weight(jax.random.fold_in(streams_of[12], 71), 0)
    gateup_weight = bell_draw(streams_of[8], (D, 2, FF), D ** -0.5, 0.21875, ((2, 4),))
    down_weight = bell_draw(streams_of[9], (FF, D), (FF // 4) ** -0.5, 0.21875, ((0, 4),))
    pair_features = draw_pair_features(jax.random.fold_in(streams_of[12], 71), 0)
    cotangent = heavy_noise(streams_of[11], (TOKENS, D), 1.0, 6.0, ((0, 8),), (0, 1, 8, 2.0))
    return dict(activations=activations, noise_times=noise_times, cath_labels=cath_labels, class_table=class_table, ada_weight=ada_weight, qkvg_weight=qkvg_weight, out_weight=out_weight, pair_weight=pair_weight, gateup_weight=gateup_weight, down_weight=down_weight, pair_features=pair_features, cotangent=cotangent)


@jax.custom_vjp
def low(v):
    return lax.optimization_barrier(v.astype(jnp.bfloat16)).astype(jnp.float32)

@jax.custom_vjp
def low_back(v):
    return v

def low_keep(v):
    return (low(v), None)

def low_pass(kept, grad):
    return (grad,)

def back_keep(v):
    return (v, None)

def back_low(kept, grad):
    return (low(grad),)
low.defvjp(low_keep, low_pass)
low_back.defvjp(back_keep, back_low)
highest = lax.Precision.HIGHEST

def timestep_embedding(time_points, count_of_features):
    width_halved = count_of_features // 2
    wave_frequency = jnp.exp(jnp.arange(width_halved).astype(time_points.dtype) * (math.log(1000.0) / width_halved))
    phase_angles = 2.0 * math.pi * time_points[:, None] * wave_frequency[None, :]
    return jnp.concatenate([jnp.cos(phase_angles), jnp.sin(phase_angles)], axis=1)

def layer_normalizer(values):
    centred = values - lax.optimization_barrier(jnp.mean(values, axis=-1, keepdims=True))
    return centred * lax.rsqrt(lax.optimization_barrier(jnp.mean(centred * centred, axis=-1, keepdims=True)) + 1e-05)

def forward(inputs, pair_block, label_rows, time_rows, class_param, ada_param, qkvg_param, out_param, pair_param, gateup_param, down_param):
    chains = pair_block.shape[0]
    length = pair_block.shape[2]
    condition = time_rows + jnp.dot(label_rows, class_param, precision=highest)
    modulation = jnp.einsum('bc,cmd->bmd', jax.nn.silu(condition), ada_param, precision=highest)
    shaped = inputs.reshape(chains, length, D)
    normed = low(layer_normalizer(shaped) * (1.0 + modulation[:, None, 0]) + modulation[:, None, 1])
    projected = jnp.einsum('bld,dke->blke', normed, qkvg_param, precision=highest)
    queries = low(low_back(projected[:, :, 0])).reshape(chains, length, HEADS, HD)
    key_heads = low(low_back(projected[:, :, 1])).reshape(chains, length, HEADS, HD)
    value_heads = low(low_back(projected[:, :, 2])).reshape(chains, length, HEADS, HD)
    gate_pre = low_back(projected[:, :, 3])
    pair_bias = jnp.einsum('bcij,ch->bhij', pair_block, pair_param, precision=highest)
    scores = low_back(jnp.einsum('bihe,bjhe->bhij', queries, key_heads, precision=highest) * 0.125 + pair_bias)
    attention = jax.nn.softmax(scores, axis=-1)
    attended = low_back(jnp.einsum('bhij,bjhe->bihe', low(attention), value_heads, precision=highest)).reshape(chains, length, D)
    gated = low(attended * jax.nn.sigmoid(gate_pre))
    branch = low_back(jnp.einsum('ble,ed->bld', gated, out_param, precision=highest))
    middle = shaped + jax.nn.sigmoid(modulation[:, None, 2]) * branch
    normed_two = low(layer_normalizer(middle) * (1.0 + modulation[:, None, 3]) + modulation[:, None, 4])
    hidden = jnp.einsum('bld,dkf->blkf', normed_two, gateup_param, precision=highest)
    gate_part = low_back(hidden[:, :, 0])
    up_part = low_back(hidden[:, :, 1])
    swish = low(jax.nn.silu(gate_part) * up_part)
    feedforward = low_back(jnp.einsum('blf,fd->bld', swish, down_param, precision=highest))
    result = middle + jax.nn.sigmoid(modulation[:, None, 5]) * feedforward
    return result.reshape(chains * length, D)

def reference(activations, noise_times, cath_labels, class_table, ada_weight, qkvg_weight, out_weight, pair_weight, gateup_weight, down_weight, pair_features, cotangent):
    floats = jnp.float32
    weights = tuple((weight_arg.astype(floats) for weight_arg in (class_table, ada_weight, qkvg_weight, out_weight, pair_weight, gateup_weight, down_weight)))
    chains = pair_features.shape[0]
    length = pair_features.shape[2]
    group_size = math.gcd(chains, max(1, 1024 // length))
    features = timestep_embedding(noise_times.astype(floats), DC)
    onehot = (cath_labels[:, None] == jnp.arange(NCLASS, dtype=jnp.int32)[None, :]).astype(floats)

    def one_group(totals, block_index):
        chain_start = (block_index * group_size).astype(jnp.int32)
        token_start = (block_index * group_size * length).astype(jnp.int32)
        inputs = lax.dynamic_slice_in_dim(activations, token_start, group_size * length, 0).astype(floats)
        upstream = lax.dynamic_slice_in_dim(cotangent, token_start, group_size * length, 0).astype(floats)
        pair_block = lax.dynamic_slice_in_dim(pair_features, chain_start, group_size, 0).astype(floats)
        label_rows = lax.dynamic_slice_in_dim(onehot, chain_start, group_size, 0)
        time_rows = lax.dynamic_slice_in_dim(features, chain_start, group_size, 0)

        def apply_layer(inputs_in, pairs_in, *params):
            return forward(inputs_in, pairs_in, label_rows, time_rows, *params)
        result, pullback = jax.vjp(apply_layer, inputs, pair_block, *weights)
        gradients = pullback(upstream)
        totals = tuple((running + update for running, update in zip(totals, gradients[2:])))
        return (totals, (result.astype(jnp.bfloat16), gradients[0].astype(jnp.bfloat16), gradients[1].astype(jnp.bfloat16)))
    initial = tuple((jnp.zeros_like(weight_arg) for weight_arg in weights))
    totals, stacked = lax.scan(one_group, initial, jnp.arange(chains // group_size, dtype=jnp.int32))
    output = stacked[0].reshape(chains * length, D)
    inputs_grad = stacked[1].reshape(chains * length, D)
    pairs_grad = stacked[2].reshape(chains, PAIR, length, length)
    class_grad, ada_grad, qkvg_grad, out_grad, pairw_grad, gateup_grad, down_grad = totals
    return (output, inputs_grad, pairs_grad, class_grad, ada_grad, qkvg_grad, out_grad, pairw_grad, gateup_grad, down_grad)
```

```python
import functools
import math

import jax
import jax.numpy as jnp
from jax import lax
from jax.experimental import pallas as pl
from jax.experimental.pallas import tpu as pltpu
from jax.sharding import PartitionSpec as P

D = 768
HD = 64
DC = 256
NCLASS = 4
L = 256
RC = 64
NRC = L // RC
LH = 3
LW = LH * HD
MESH = pl.DeviceIdType.MESH
F32 = jnp.float32
BF16 = jnp.bfloat16
VMEM_LIMIT = 63 * 2**20

highest = lax.Precision.HIGHEST


def timestep_embedding(time_points, count_of_features):
    width_halved = count_of_features // 2
    wave_frequency = jnp.exp(
        jnp.arange(width_halved).astype(jnp.float32) * (math.log(1000.0) / width_halved)
    )
    phase_angles = 2.0 * math.pi * time_points[:, None] * wave_frequency[None, :]
    return jnp.concatenate([jnp.cos(phase_angles), jnp.sin(phase_angles)], axis=1)


def normalize(values):
    centred = values - jnp.mean(values, axis=-1, keepdims=True)
    inverse = lax.rsqrt(jnp.mean(centred * centred, axis=-1, keepdims=True) + 1e-05)
    return (centred * inverse, inverse)


def norm_back(grad_unit, unit_rows, inverse):
    mean_grad = jnp.mean(grad_unit, axis=-1, keepdims=True)
    mean_proj = jnp.mean(grad_unit * unit_rows, axis=-1, keepdims=True)
    return inverse * (grad_unit - mean_grad - unit_rows * mean_proj)


def nn(a, b, precision=None):
    return lax.dot_general(
        a, b, (((1,), (0,)), ((), ())), preferred_element_type=F32, precision=precision
    )


def nt(a, b, precision=None):
    return lax.dot_general(
        a, b, (((1,), (1,)), ((), ())), preferred_element_type=F32, precision=precision
    )


def tn(a, b, precision=None):
    return lax.dot_general(
        a, b, (((0,), (0,)), ((), ())), preferred_element_type=F32, precision=precision
    )


def remote(src, dst, ssem, rsem, device):
    return pltpu.make_async_remote_copy(
        src_ref=src, dst_ref=dst, send_sem=ssem, recv_sem=rsem, device_id=device, device_id_type=MESH
    )


def iota(shape, axis):
    return lax.broadcasted_iota(jnp.int32, shape, axis)


class Place:
    def __init__(self, ndp):
        self.ndp = ndp
        self.dp = dp = lax.axis_index("dp")
        self.t = t = lax.axis_index("tensor")
        self.near_t, self.skip_t, self.far_t = t + 1 - 2 * lax.rem(t, 2), lax.rem(t + 2, 4), 3 - t
        self.near, self.skip, self.far = (dp, self.near_t), (dp, self.skip_t), (dp, self.far_t)
        self.inner = (t == 1) | (t == 2)
        self.outer = (t == 0) | (t == 3)

    def peer(self, step):
        return lax.rem(self.dp + step, self.ndp)

    def barrier(self):
        sem = pltpu.get_barrier_semaphore()
        for device in (self.near, self.skip, self.far):
            pl.semaphore_signal(sem, inc=1, device_id=device, device_id_type=MESH)

        @pl.loop(1, self.ndp)
        def _(step):
            pl.semaphore_signal(
                sem, inc=1, device_id=(self.peer(step), self.t), device_id_type=MESH
            )

        pl.semaphore_wait(sem, 3 + self.ndp - 1)


class Spread:
    def __init__(self, place, source, target, ssem, rsem):
        self.place, self.source, self.target, self.ssem, self.rsem = place, source, target, ssem, rsem

    def copy(self, step):
        there = self.place.peer(step)
        return remote(
            self.source(there),
            self.target.at[self.place.dp],
            self.ssem.at[step],
            self.rsem.at[self.place.dp],
            (there, self.place.t),
        )

    def arrival(self, step):
        there = self.place.peer(step)
        return remote(
            self.source(there),
            self.target.at[there],
            self.ssem.at[step],
            self.rsem.at[there],
            (there, self.place.t),
        )

    def own(self):
        here = self.place.dp
        return pltpu.make_async_copy(self.source(here), self.target.at[here], self.ssem.at[0])

    def start(self):
        self.own().start()

        @pl.loop(1, self.place.ndp)
        def _(step):
            self.copy(step).start()

    def wait(self):
        self.own().wait()

        @pl.loop(1, self.place.ndp)
        def _(step):
            self.copy(step).wait_send()
            self.arrival(step).wait_recv()


class LineSum:
    def __init__(self, place, part, in1, in2, total, sems):
        self.place, self.part, self.in1, self.in2, self.total, self.sems = place, part, in1, in2, total, sems

    def copy(self, stage, i):
        src = (self.part, self.part, self.total)[stage].at[i]
        dst = (self.in1, self.in2, self.total)[stage].at[i]
        device = (self.place.near, self.place.far, self.place.near)[stage]
        return remote(src, dst, self.sems.at[2 * stage, i], self.sems.at[2 * stage + 1, i], device)

    def start(self, i):
        @pl.when(self.place.outer)
        def _():
            self.copy(0, i).start()

    def cross(self, i):
        @pl.when(self.place.inner)
        def _():
            self.copy(0, i).wait_recv()
            self.part[i] = (self.part[i].astype(F32) + self.in1[i].astype(F32)).astype(BF16)
            self.copy(1, i).start()

    def back(self, i):
        @pl.when(self.place.inner)
        def _():
            self.copy(1, i).wait_recv()
            self.total[i] = (self.part[i].astype(F32) + self.in2[i].astype(F32)).astype(BF16)
            self.copy(2, i).start()

    def finish(self, i):
        @pl.when(self.place.outer)
        def _():
            self.copy(2, i).wait_recv()

    def drain(self, i):
        @pl.when(self.place.outer)
        def _():
            self.copy(0, i).wait_send()

        @pl.when(self.place.inner)
        def _():
            self.copy(1, i).wait_send()
            self.copy(2, i).wait_send()

    def value(self, b):
        return jnp.concatenate([self.total[2 * b], self.total[2 * b + 1]], axis=0).astype(F32)


def layer_kernel(
    nb, ndp,
    cond, aux, ada, act_in, cot_in, wq_in, wo_in, wgu_in, wd_in, pw, pf,
    sg, out_o, in_o, wff_o, watt_o, mg_o, pw_o, aux_o,
    act, cot, wq, wo, wgu, wd, isem, kw, mod, pbuf, psem,
    send1, keep, recv1, send2, recv2, bsem,
    qs, ks, vs, probs, gate, att, normed_t,
    part1, in1a, in1b, total1, sem1,
    part2, in2a, in2b, total2, sem2,
    part3, in3a, in3b, total3, sem3,
    part4, in4a, in4b, total4, sem4,
    norm2_t, fgrad, fgrad_t, swish, hgrad, bgrad_t, gated_s, pgrad, mgrad_mid,
    gsem, acc, wff, watt, mgs, pws, xsem,
):
    place = Place(ndp)
    nch = nb * NRC
    slots = pbuf.shape[0]
    rows_per = D // ndp

    def fetch(k, slot):
        b, r = k // NRC, k % NRC
        return pltpu.make_async_copy(pf.at[b, :, pl.ds(r * RC, RC), :], pbuf.at[slot], psem.at[slot])

    for k in range(slots):
        fetch(k, k).start()
    loads = [
        pltpu.make_async_copy(src, dst, isem.at[n])
        for n, (src, dst) in enumerate(
            ((act_in, act), (wq_in, wq), (wo_in, wo), (cot_in, cot), (wgu_in, wgu), (wd_in, wd))
        )
    ]
    for load in loads:
        load.start()

    row, col = iota((192, 12), 0), iota((192, 12), 1)
    group, head = row // 48, lax.rem(row // 16, 3)
    owner = jnp.where(
        group == 0,
        place.far_t,
        jnp.where(group == 1, place.near_t, jnp.where(group == 2, place.skip_t, place.t)),
    )
    pick = (col == owner * 3 + head).astype(F32).astype(BF16)
    chosen = nt(pick, pw[...]).astype(BF16)
    channels = pw.shape[0]
    widen = (iota((channels, channels * 16), 1) // 16 == iota((channels, channels * 16), 0)).astype(F32)
    wide = nn(chosen, widen.astype(BF16))
    diagonal = lax.rem(iota(wide.shape, 0), 16) == lax.rem(iota(wide.shape, 1), 16)
    kw[...] = jnp.where(diagonal, wide, 0.0).astype(BF16)

    place.barrier()

    aux_spread = Spread(place, lambda j: aux.at[j], aux_o, xsem.at[0], xsem.at[1])
    aux_spread.start()

    def first(k, n):
        return remote(
            send1.at[k, n], recv1.at[k, n], bsem.at[2 * n, k], bsem.at[2 * n + 1, k], place.near
        )

    def second(k):
        return remote(send2.at[k], recv2.at[k], bsem.at[4, k], bsem.at[5, k], place.skip)

    def bias(k):
        slot = k % slots
        fetch(k, slot).wait()
        for s in range(RC // 16):
            rows = pbuf[slot, :, pl.ds(s * 16, 16), :].reshape(-1, L)
            out = nn(kw[...], rows)
            half = out.shape[0] // 2
            send1[k, :, :, pl.ds(s * 16, 16), :] = out[:half].reshape(2, -1, 16, L).astype(BF16)
            keep[k, :, :, pl.ds(s * 16, 16), :] = out[half:].reshape(2, -1, 16, L)
        for n in range(2):
            first(k, n).start()
        if k + slots < nch:
            fetch(k + slots, slot).start()

    def relay(k):
        first(k, 0).wait_recv()
        send2[k] = (keep[k, 0] + recv1[k, 0].astype(F32)).astype(BF16)
        second(k).start()

    def modulate():
        def scoped(rows, sem):
            load = pltpu.make_async_copy(ada, rows, sem)
            load.start()
            load.wait()

            def step(c, sums):
                row = rows[c].astype(F32)
                return tuple(sums[b] + cond[b, c] * row for b in range(nb))

            sums = lax.fori_loop(0, DC, step, tuple(jnp.zeros((6, D), F32) for _ in range(nb)), unroll=8)
            for b in range(nb):
                mod[b] = sums[b]

        pl.run_scoped(scoped, pltpu.VMEM(ada.shape, BF16), pltpu.SemaphoreType.DMA)

    def project(b):
        if b == 0:
            loads[0].wait()
            loads[1].wait()
        unit, _ = normalize(act[pl.ds(b * L, L)].astype(F32))
        m = mod[b]
        low = (unit * (1.0 + m[0:1]) + m[1:2]).astype(BF16)
        normed_t[:, pl.ds(b * L, L)] = low.T
        for piece in range(2):
            out = nn(low, wq[:, pl.ds(piece * 384, 384)])
            for n in range(6):
                which, h = piece * 2 + n // 3, n % 3
                column = out[:, n * HD : (n + 1) * HD]
                if which == 0:
                    qs[b, h] = (column.astype(BF16).astype(F32) * 0.125).astype(BF16)
                elif which == 1:
                    ks[b, h] = column.astype(BF16)
                elif which == 2:
                    vs[b, h] = column.astype(BF16)
            if piece == 1:
                gate[b] = jax.nn.sigmoid(out[:, LW:])

    sum1 = LineSum(place, part1, in1a, in1b, total1, sem1)
    sum2 = LineSum(place, part2, in2a, in2b, total2, sem2)
    sum3 = LineSum(place, part3, in3a, in3b, total3, sem3)
    sum4 = LineSum(place, part4, in4a, in4b, total4, sem4)

    def attend(b):
        if b == 0:
            loads[2].wait()
        for r in range(NRC):
            k = b * NRC + r
            first(k, 1).wait_recv()
            second(k).wait_recv()
        heads = []
        for h in range(LH):
            bias_rows = jnp.concatenate(
                [
                    keep[b * NRC + r, 1, h]
                    + recv1[b * NRC + r, 1, h].astype(F32)
                    + recv2[b * NRC + r, h].astype(F32)
                    for r in range(NRC)
                ],
                axis=0,
            )
            scores = nt(qs[b, h], ks[b, h]) + bias_rows
            e = jnp.exp(scores - jnp.max(scores, axis=-1, keepdims=True))
            p = (e * (1.0 / jnp.sum(e, axis=-1, keepdims=True))).astype(BF16)
            probs[b, h] = p
            heads.append(nn(p, vs[b, h]))
        attended = jnp.concatenate(heads, axis=1)
        att[b] = attended
        gated = (attended * gate[b]).astype(BF16)
        gated_s[pl.ds(b * L, L)] = gated
        for half in range(2):
            part1[b * 2 + half] = nn(gated[half * 128 : (half + 1) * 128], wo[...]).astype(BF16)
            sum1.start(b * 2 + half)

    def prepare():
        loads[3].wait()
        for b in range(nb):
            low = (cot[pl.ds(b * L, L)].astype(F32) * jax.nn.sigmoid(mod[b, 5:6])).astype(BF16)
            fgrad[pl.ds(b * L, L)] = low
            fgrad_t[:, pl.ds(b * L, L)] = low.T

    def middle_of(b):
        rows = act[pl.ds(b * L, L)].astype(F32)
        return rows + jax.nn.sigmoid(mod[b, 2:3]) * sum1.value(b)

    def feedforward(b):
        if b == 0:
            loads[4].wait()
            loads[5].wait()
        here = pl.ds(b * L, L)
        unit, _ = normalize(middle_of(b))
        low = (unit * (1.0 + mod[b, 3:4]) + mod[b, 4:5]).astype(BF16)
        norm2_t[:, here] = low.T
        for f in range(3):
            tile, tile_up = pl.ds(f * 256, 256), pl.ds(D + f * 256, 256)
            g = nn(low, wgu[:, tile])
            up = nn(low, wgu[:, tile_up])
            back = nt(fgrad[here], wd[tile, :])
            s = jax.nn.sigmoid(g)
            silu = g * s
            swish[here, tile] = (silu * up).astype(BF16)
            hgrad[here, tile_up] = (back * silu).astype(BF16)
            hgrad[here, tile] = (back * up * s * (1.0 + g * (1.0 - s))).astype(BF16)
        for half in range(2):
            some = pl.ds(b * L + half * 128, 128)
            for d in range(3):
                tile = pl.ds(d * 256, 256)
                part2[b * 2 + half, :, tile] = nt(hgrad[some, :], wgu[tile, :]).astype(BF16)
            sum2.start(b * 2 + half)
        for half in range(2):
            some = pl.ds(b * L + half * 128, 128)
            for d in range(3):
                tile = pl.ds(d * 256, 256)
                part3[b * 2 + half, :, tile] = nn(swish[some, :], wd[:, tile]).astype(BF16)
            sum3.start(b * 2 + half)

    def put_rows(target, tile, values):
        low = values.astype(BF16)
        for j in range(ndp):
            target[j, :, tile] = low[j * rows_per : (j + 1) * rows_per]

    wff_spread = Spread(place, lambda j: wff.at[j], wff_o, xsem.at[2], xsem.at[3])
    watt_spread = Spread(place, lambda j: watt.at[j], watt_o, xsem.at[4], xsem.at[5])

    def weights_ff():
        for f in range(6):
            tile = pl.ds(f * 256, 256)
            put_rows(wff, tile, nn(norm2_t[...], hgrad[:, tile]))
        for f in range(3):
            put_rows(wff, pl.ds(2 * D + f * 256, 256), nn(fgrad_t[...], swish[:, pl.ds(f * 256, 256)]))
        wff_spread.start()

    def weights_att():
        for f in range(3):
            tile = pl.ds(f * 256, 256)
            put_rows(watt, tile, nn(normed_t[...], pgrad[:, tile]))
        put_rows(watt, pl.ds(D, LW), nn(bgrad_t[...], gated_s[...]))
        watt_spread.start()

    def share(k, n):
        return remote(
            sg.at[2 if n == 0 else 3, k],
            sg.at[n, k],
            gsem.at[2 * n, k],
            gsem.at[2 * n + 1, k],
            place.skip if n == 2 else place.near,
        )

    def attend_back(b):
        here = pl.ds(b * L, L)
        m = mod[b]
        gate_one = jax.nn.sigmoid(m[2:3])
        middle = middle_of(b)
        unit, inverse = normalize(middle)
        two = sum2.value(b)
        up = cot[here].astype(F32)
        mid_grad = up + norm_back(two * (1.0 + m[3:4]), unit, inverse)
        mgrad_mid[here] = mid_grad
        low = (mid_grad * gate_one).astype(BF16)
        bgrad_t[:, here] = low.T
        mgs[b, 2:3] = (
            jnp.sum(mid_grad * sum1.value(b), axis=0, keepdims=True) * gate_one * (1.0 - gate_one)
        )
        mgs[b, 3:4] = jnp.sum(two * unit, axis=0, keepdims=True)
        mgs[b, 4:5] = jnp.sum(two, axis=0, keepdims=True)
        gated_grad = nt(low, wo[...])
        opened = gate[b]
        att_grad = (gated_grad * opened).astype(BF16)
        attended = att[b]
        pgrad[here, pl.ds(3 * LW, LW)] = (gated_grad * attended * opened * (1.0 - opened)).astype(BF16)
        product = att_grad.astype(F32) * attended
        dq, dk, dv = [], [], []
        for h in range(LH):
            cols = slice(h * HD, (h + 1) * HD)
            head_grad = att_grad[:, cols]
            delta = jnp.sum(product[:, cols], axis=-1, keepdims=True)
            p = probs[b, h]
            score_grad = (p.astype(F32) * (nt(head_grad, vs[b, h]) - delta)).astype(BF16)
            for r in range(NRC):
                sg[3, b * NRC + r, h] = score_grad[r * RC : (r + 1) * RC]
            dq.append(nn(score_grad, ks[b, h]) * 0.125)
            dk.append(tn(score_grad, qs[b, h]))
            dv.append(tn(p, head_grad))
        for r in range(NRC):
            share(b * NRC + r, 2).start()
        for r in range(NRC):
            share(b * NRC + r, 1).start()
        pgrad[here, pl.ds(0, 3 * LW)] = jnp.concatenate(dq + dk + dv, axis=1).astype(BF16)
        for half in range(2):
            some = pl.ds(b * L + half * 128, 128)
            for d in range(3):
                tile = pl.ds(d * 256, 256)
                part4[b * 2 + half, :, tile] = nt(pgrad[some, :], wq[tile, :]).astype(BF16)
            sum4.start(b * 2 + half)

    def forward_share(k):
        share(k, 2).wait_recv()
        share(k, 0).start()

    def pair_weight(k):
        slot = k % slots
        share(k, 0).wait_recv()
        share(k, 1).wait_recv()
        fetch(k, slot).wait()
        total = None
        for s in range(RC // 16):
            rows = pbuf[slot, :, pl.ds(s * 16, 16), :].reshape(-1, L)
            grads = sg[:, k, :, pl.ds(s * 16, 16), :].reshape(-1, L)
            out = nt(rows, grads)
            total = out if total is None else total + out
        if k == 0:
            acc[...] = total
        else:
            acc[...] += total
        if k + slots < nch:
            fetch(k + slots, slot).start()

    def pair_weight_end():
        values = acc[...].reshape(channels, 16, 192)
        mask = iota((16, 192), 0) == lax.rem(iota((16, 192), 1), 16)
        picked = jnp.sum(jnp.where(mask[None], values, 0.0), axis=1)
        row, col = iota((192, 128), 0), iota((192, 128), 1)
        group, head = row // 48, lax.rem(row // 16, 3)
        owner = jnp.where(
            group == 0,
            place.far_t,
            jnp.where(group == 1, place.near_t, jnp.where(group == 2, place.skip_t, place.t)),
        )
        pws[...] = nn(picked, (col == owner * 3 + head).astype(F32), precision=highest)

    def finish_rows(b):
        here = pl.ds(b * L, L)
        m = mod[b]
        gate_two = jax.nn.sigmoid(m[5:6])
        ffn = sum3.value(b)
        out_o[here] = (middle_of(b) + gate_two * ffn).astype(BF16)
        mgs[b, 5:6] = (
            jnp.sum(cot[here].astype(F32) * ffn, axis=0, keepdims=True) * gate_two * (1.0 - gate_two)
        )
        unit, inverse = normalize(act[here].astype(F32))
        one = sum4.value(b)
        mgs[b, 0:1] = jnp.sum(one * unit, axis=0, keepdims=True)
        mgs[b, 1:2] = jnp.sum(one, axis=0, keepdims=True)
        in_o[here] = (mgrad_mid[here] + norm_back(one * (1.0 + m[0:1]), unit, inverse)).astype(BF16)

    def refetch():
        for k in range(slots):
            fetch(k, k).start()

    mg_spread = Spread(place, lambda j: mgs, mg_o, xsem.at[6], xsem.at[7])
    pw_spread = Spread(place, lambda j: pws, pw_o, xsem.at[8], xsem.at[9])

    def both(step, b):
        step(2 * b)
        step(2 * b + 1)

    bias(0)
    modulate()
    bias(1)
    project(0)
    relay(0)
    bias(2)
    relay(1)
    bias(3)
    relay(2)
    project(1)
    bias(4)
    relay(3)
    prepare()
    bias(5)
    attend(0)
    relay(4)
    bias(6)
    relay(5)
    both(sum1.cross, 0)
    bias(7)
    refetch()
    relay(6)
    both(sum1.back, 0)
    relay(7)
    both(sum1.finish, 0)
    feedforward(0)
    attend(1)
    both(sum2.cross, 0)
    both(sum1.cross, 1)
    both(sum2.back, 0)
    both(sum1.back, 1)
    both(sum2.finish, 0)
    attend_back(0)
    both(sum1.finish, 1)
    feedforward(1)
    for k in range(4):
        forward_share(k)
    both(sum2.cross, 1)
    both(sum3.cross, 0)
    both(sum2.back, 1)
    both(sum4.cross, 0)
    weights_ff()
    both(sum2.finish, 1)
    attend_back(1)
    both(sum3.back, 0)
    both(sum4.back, 0)
    for k in range(4):
        pair_weight(k)
        forward_share(k + 4)
    both(sum4.cross, 1)
    both(sum3.cross, 1)
    weights_att()
    both(sum4.back, 1)
    both(sum3.back, 1)
    both(sum3.finish, 0)
    both(sum4.finish, 0)
    finish_rows(0)
    pair_weight(4)
    pair_weight(5)
    both(sum3.finish, 1)
    both(sum4.finish, 1)
    finish_rows(1)
    mg_spread.start()
    pair_weight(6)
    pair_weight(7)
    pair_weight_end()
    pw_spread.start()

    for k in range(nch):
        for n in range(2):
            first(k, n).wait_send()
        second(k).wait_send()
        for n in range(3):
            share(k, n).wait_send()
    for total in (sum1, sum2, sum3, sum4):
        for i in range(2 * nb):
            total.drain(i)
    for spread in (aux_spread, wff_spread, watt_spread, mg_spread, pw_spread):
        spread.wait()


def vmem_specs(n):
    return [pl.BlockSpec(memory_space=pltpu.VMEM)] * n


def any_specs(n):
    return [pl.BlockSpec(memory_space=pl.ANY)] * n


def layer_call(nb, ndp, cond, aux, ada, act, cot, wq, wo, wgu, wd, pw, pf):
    nch = nb * NRC
    rows = nb * L
    rows_per = D // ndp
    channels = pf.shape[1]
    hidden = wd.shape[0]
    shapes = [
        ((4, nch, LH, RC, L), BF16),
        ((rows, D), BF16),
        ((rows, D), BF16),
        ((ndp, rows_per, 3 * hidden), BF16),
        ((ndp, rows_per, 5 * LW), BF16),
        ((ndp, nb, 6, D), F32),
        ((ndp, channels, 128), F32),
        (aux.shape, F32),
    ]
    dma = pltpu.SemaphoreType.DMA

    def line():
        return [pltpu.VMEM((2 * nb, 128, D), BF16)] * 4 + [dma((6, 2 * nb))]

    scratch = [
        pltpu.VMEM((rows, D), BF16),
        pltpu.VMEM((rows, D), BF16),
        pltpu.VMEM(wq.shape, BF16),
        pltpu.VMEM(wo.shape, BF16),
        pltpu.VMEM(wgu.shape, BF16),
        pltpu.VMEM(wd.shape, BF16),
        dma((6,)),
        pltpu.VMEM((192, channels * 16), BF16),
        pltpu.VMEM((nb, 6, D), F32),
        pltpu.VMEM((3, channels, RC, L), BF16),
        dma((3,)),
        pltpu.VMEM((nch, 2, LH, RC, L), BF16),
        pltpu.VMEM((nch, 2, LH, RC, L), F32),
        pltpu.VMEM((nch, 2, LH, RC, L), BF16),
        pltpu.VMEM((nch, LH, RC, L), BF16),
        pltpu.VMEM((nch, LH, RC, L), BF16),
        dma((6, nch)),
        pltpu.VMEM((nb, LH, L, HD), BF16),
        pltpu.VMEM((nb, LH, L, HD), BF16),
        pltpu.VMEM((nb, LH, L, HD), BF16),
        pltpu.VMEM((nb, LH, L, L), BF16),
        pltpu.VMEM((nb, L, LW), F32),
        pltpu.VMEM((nb, L, LW), F32),
        pltpu.VMEM((D, rows), BF16),
        *line(),
        *line(),
        *line(),
        *line(),
        pltpu.VMEM((D, rows), BF16),
        pltpu.VMEM((rows, D), BF16),
        pltpu.VMEM((D, rows), BF16),
        pltpu.VMEM((rows, hidden), BF16),
        pltpu.VMEM((rows, 2 * hidden), BF16),
        pltpu.VMEM((D, rows), BF16),
        pltpu.VMEM((rows, LW), BF16),
        pltpu.VMEM((rows, 4 * LW), BF16),
        pltpu.VMEM((rows, D), F32),
        dma((6, nch)),
        pltpu.VMEM((channels * 16, 192), F32),
        pltpu.VMEM((ndp, rows_per, 3 * hidden), BF16),
        pltpu.VMEM((ndp, rows_per, 5 * LW), BF16),
        pltpu.VMEM((nb, 6, D), F32),
        pltpu.VMEM((channels, 128), F32),
        dma((10, ndp)),
    ]
    return pl.pallas_call(
        functools.partial(layer_kernel, nb, ndp),
        out_shape=[jax.ShapeDtypeStruct(*s) for s in shapes],
        in_specs=[pl.BlockSpec(memory_space=pltpu.SMEM)] + any_specs(8) + vmem_specs(1) + any_specs(1),
        out_specs=vmem_specs(3) + any_specs(5),
        scratch_shapes=scratch,
        compiler_params=pltpu.CompilerParams(
            collective_id=0, has_side_effects=True, vmem_limit_bytes=VMEM_LIMIT
        ),
        name="layer",
    )(cond, aux, ada, act, cot, wq, wo, wgu, wd, pw, pf)


def ending_kernel(
    nb, ndp,
    sg, pw, mg, aux, ada, out_i, in_i, wff, watt, pwi,
    pg, out_o, in_o, ada_o, class_o, wgu_o, wd_o, wq_o, wo_o, pw_o,
    obuf, osem, psem,
):
    t = lax.axis_index("tensor")
    nch = nb * NRC
    hidden = wd_o.shape[1]
    slots = obuf.shape[0]
    passing = [
        pltpu.make_async_copy(out_i, out_o, psem.at[0]),
        pltpu.make_async_copy(in_i, in_o, psem.at[1]),
    ]
    for copy in passing:
        copy.start()
    channels = pw.shape[0]
    row, col = iota((12, 192), 0), iota((12, 192), 1)
    group, head = col // 48, lax.rem(col // 16, 3)
    near_t, skip_t, far_t = t + 1 - 2 * lax.rem(t, 2), lax.rem(t + 2, 4), 3 - t
    owner = jnp.where(
        group == 0, far_t, jnp.where(group == 1, near_t, jnp.where(group == 2, skip_t, t))
    )
    pick = (row == owner * 3 + head).astype(F32).astype(BF16)
    chosen = nn(pw[...], pick).astype(BF16)
    widen = (iota((channels * 16, channels), 0) // 16 == iota((channels * 16, channels), 1)).astype(F32)
    wide = nn(widen.astype(BF16), chosen)
    diagonal = lax.rem(iota(wide.shape, 0), 16) == lax.rem(iota(wide.shape, 1), 16)
    spread = jnp.where(diagonal, wide, 0.0).astype(BF16)

    def store(k):
        b, r = k // NRC, k % NRC
        return pltpu.make_async_copy(
            obuf.at[k % slots], pg.at[b, :, pl.ds(r * RC, RC), :], osem.at[k % slots]
        )

    def pair_grad(k):
        if k >= slots:
            store(k - slots).wait()
        for s in range(RC // 16):
            grads = sg[:, k, :, pl.ds(s * 16, 16), :].reshape(-1, L)
            obuf[k % slots, :, pl.ds(s * 16, 16), :] = (
                nn(spread, grads).reshape(channels, 16, L).astype(BF16)
            )
        store(k).start()

    def add(source, tile):
        total = source[0, :, tile].astype(F32)
        for j in range(1, ndp):
            total += source[j, :, tile].astype(F32)
        return total

    def weight_sums():
        total = add(wff, pl.ds(0, 3 * hidden))
        wgu_o[...] = total[:, : 2 * hidden]
        wd_o[...] = total[:, 2 * hidden :]
        total = add(watt, pl.ds(0, 5 * LW))
        wq_o[...] = total[:, : 4 * LW]
        wo_o[...] = total[:, 4 * LW :]
        total = pwi[0]
        for j in range(1, ndp):
            total += pwi[j]
        pw_o[...] = total[:, : pw_o.shape[1]]

    def condition():
        def rows(kind):
            return jnp.concatenate([aux[j, kind * nb : (kind + 1) * nb] for j in range(ndp)], axis=0)

        silu, factor, hot = rows(0), rows(1), rows(2)
        back = None
        for m in range(6):
            grads = mg[:, m, :]
            ada_o[:, m, :] = tn(silu, grads, precision=highest)
            part = nt(grads, ada[:, m, :].astype(F32), precision=highest)
            back = part if back is None else back + part
        class_o[...] = tn(hot, back * factor, precision=highest)[:NCLASS]

    for k in range(nch):
        pair_grad(k)
        if k == 1:
            weight_sums()
        if k == 3:
            condition()
    for k in range(max(nch - slots, 0), nch):
        store(k).wait()
    for copy in passing:
        copy.wait()


def ending_call(nb, ndp, sg, pw, mg, aux, ada, out, inputs_grad, wff, watt, pwi, pair_shape):
    rows_per = D // ndp
    hidden = wff.shape[2] // 3
    width = DC // ndp
    channels = pair_shape[1]
    shapes = [
        (pair_shape, BF16),
        (out.shape, BF16),
        (out.shape, BF16),
        ((width, 6, D), F32),
        ((NCLASS, width), F32),
        ((rows_per, 2 * hidden), F32),
        ((rows_per, hidden), F32),
        ((rows_per, 4 * LW), F32),
        ((rows_per, LW), F32),
        ((channels, 12), F32),
    ]
    return pl.pallas_call(
        functools.partial(ending_kernel, nb, ndp),
        out_shape=[jax.ShapeDtypeStruct(*s) for s in shapes],
        in_specs=vmem_specs(5) + any_specs(2) + vmem_specs(3),
        out_specs=any_specs(3) + vmem_specs(7),
        scratch_shapes=[
            pltpu.VMEM((3, channels, RC, L), BF16),
            pltpu.SemaphoreType.DMA((3,)),
            pltpu.SemaphoreType.DMA((2,)),
        ],
        compiler_params=pltpu.CompilerParams(vmem_limit_bytes=VMEM_LIMIT),
        name="ending",
    )(sg, pw, mg, aux, ada, out, inputs_grad, wff, watt, pwi)


def shards(
    ndp,
    activations,
    noise_times,
    cath_labels,
    class_table,
    ada_weight,
    qkvg_weight,
    out_weight,
    pair_weight,
    gateup_weight,
    down_weight,
    pair_features,
    cotangent,
):
    chains = pair_features.shape[0]
    width = DC // ndp
    onehot = (cath_labels[:, None] == jnp.arange(NCLASS, dtype=jnp.int32)[None, :]).astype(F32)
    condition = timestep_embedding(noise_times, DC) + jnp.dot(
        onehot, class_table.astype(F32), precision=highest
    )
    cond_sigmoid = jax.nn.sigmoid(condition)
    cond_silu = condition * cond_sigmoid
    factor = cond_sigmoid * (1.0 + condition * (1.0 - cond_sigmoid))
    hot = jnp.broadcast_to(jnp.pad(onehot, ((0, 0), (0, width - NCLASS)))[:, None], (chains, ndp, width))
    aux = jnp.stack(
        [cond_silu.reshape(chains, ndp, width), factor.reshape(chains, ndp, width), hot]
    )
    aux = jnp.moveaxis(aux, 2, 0).reshape(ndp, 3 * chains, width)
    wq = qkvg_weight.reshape(D, -1)
    wgu = gateup_weight.reshape(D, -1)
    sg, out, inputs_grad, wff, watt, mg, pwi, aux_all = layer_call(
        chains, ndp, cond_silu, aux, ada_weight, activations, cotangent, wq, out_weight, wgu,
        down_weight, pair_weight, pair_features,
    )
    here = lax.axis_index("dp")
    ada_rows = lax.dynamic_slice_in_dim(ada_weight, here * width, width, 0)
    pair_grad, out, inputs_grad, ada_sum, class_sum, gateup, down, qkvg, outw, pair_sum = ending_call(
        chains, ndp, sg, pair_weight, mg.reshape(-1, 6, D), aux_all, ada_rows, out, inputs_grad,
        wff, watt, pwi, pair_features.shape,
    )
    return (
        out,
        inputs_grad,
        pair_grad,
        class_sum,
        ada_sum,
        qkvg.reshape(-1, 4, LW),
        outw.T,
        pair_sum,
        gateup.reshape(gateup.shape[0], 2, -1),
        down.T,
    )


def solution(mesh):
    placed = (
        P("dp", None),
        P("dp"),
        P("dp"),
        P(),
        P(),
        P(None, None, "tensor"),
        P("tensor", None),
        P("tensor", None),
        P(None, None, "tensor"),
        P("tensor", None),
        P("dp", "tensor", None, None),
        P("dp", None),
    )
    return jax.shard_map(
        functools.partial(shards, mesh.shape["dp"]),
        mesh=mesh,
        in_specs=placed,
        out_specs=(
            P("dp", None),
            P("dp", None),
            P("dp", "tensor", None, None),
            P(None, "dp"),
            P("dp", None, None),
            P("dp", None, "tensor"),
            P("tensor", "dp"),
            P("tensor", None),
            P("dp", None, "tensor"),
            P("tensor", "dp"),
        ),
        check_vma=False,
    )
```

```python
import functools
import math

import jax
import jax.numpy as jnp
import numpy as np
from jax import lax
from jax.experimental import pallas as pl
from jax.experimental.pallas import tpu as pltpu
from jax.sharding import PartitionSpec as P

D = 768
HD = 64
DC = 256
NCLASS = 4
L = 256
RC = 64
NRC = L // RC
LH = 3
LW = LH * HD
PARTS = 4
PR = L // PARTS
RING = 4
MESH = pl.DeviceIdType.MESH
F32 = jnp.float32
BF16 = jnp.bfloat16
VMEM_LIMIT = 63 * 2**20

highest = lax.Precision.HIGHEST


def normalize(values):
    centred = values - jnp.mean(values, axis=-1, keepdims=True)
    inverse = lax.rsqrt(jnp.mean(centred * centred, axis=-1, keepdims=True) + 1e-05)
    return (centred * inverse, inverse)


def norm_back(grad_unit, unit_rows, inverse):
    mean_grad = jnp.mean(grad_unit, axis=-1, keepdims=True)
    mean_proj = jnp.mean(grad_unit * unit_rows, axis=-1, keepdims=True)
    return inverse * (grad_unit - mean_grad - unit_rows * mean_proj)


def nn(a, b, precision=None):
    return lax.dot_general(
        a, b, (((1,), (0,)), ((), ())), preferred_element_type=F32, precision=precision
    )


def nt(a, b, precision=None):
    return lax.dot_general(
        a, b, (((1,), (1,)), ((), ())), preferred_element_type=F32, precision=precision
    )


def tn(a, b, precision=None):
    return lax.dot_general(
        a, b, (((0,), (0,)), ((), ())), preferred_element_type=F32, precision=precision
    )


def remote(src, dst, ssem, rsem, device):
    return pltpu.make_async_remote_copy(
        src_ref=src, dst_ref=dst, send_sem=ssem, recv_sem=rsem, device_id=device, device_id_type=MESH
    )


def iota(shape, axis):
    return lax.broadcasted_iota(jnp.int32, shape, axis)


ORDER = (
    "bias0", "tw0", "E0", "bias1", "rela0", "E1", "bias2", "E2", "relb0", "bias3",
    "rela1", "mod", "aux", "E3", "rela2", "bias4", "relb1", "bias5", "proj0", "ts0",
    "rela3", "E4", "relb2", "relb3", "rela4", "relb4", "bias6", "prep", "bias7", "attend0",
    "x1.2", "x1.0", "x1.1", "x1.3", "y1.1", "y1.0", "y1.2", "E5", "E6", "y1.3",
    "E7", "z1.1", "rela5", "z1.2", "z1.3", "z1.0", "ffnA0", "rela6", "relb5", "rela7",
    "relb6", "x2.1", "x2.0", "relb7", "proj1", "attend1", "x2.3", "y2.1", "z2.1", "x2.2",
    "y2.0", "y2.3", "y2.2", "z2.3", "z2.2", "x1.4", "z2.0", "backA0", "P3", "Q3",
    "P2", "x1.6", "y1.4", "x1.5", "P1", "x1.7", "y1.6", "P0", "y1.5", "R3",
    "y1.7", "S3", "Q0", "z1.4", "ffnB0", "Q2", "z1.7", "z1.6", "x3.1", "z1.5",
    "ffnA1", "x3.2", "x2.4", "y3.2", "x2.6", "x2.5", "x2.7", "one0", "Q1", "y2.6",
    "R1", "R0", "x3.0", "y2.5", "y2.4", "z3.2", "z2.5", "R2", "z2.6", "y2.7",
    "z2.7", "z2.4", "backA1", "S1", "S0", "x4.0", "x3.3", "y3.0", "Q6", "P4",
    "y3.1", "one1", "S2", "y3.3", "z3.3", "pw0", "ffnB1", "x3.5", "x4.4", "Q5",
    "P7", "x3.6", "x4.2", "x4.1", "wff", "x4.6", "P5", "R5", "y4.0", "pw1",
    "P6", "pw2", "y3.5", "y4.4", "R4", "Q4", "S5", "x4.3", "R6", "pw3",
    "Q7", "S4", "R7", "z4.0", "y4.6", "y4.2", "x3.7", "x4.7", "watt", "pw4",
    "x4.5", "pw5", "y4.3", "S6", "S7", "y4.1", "z4.3", "y3.6", "z4.1", "z3.6",
    "x3.4", "z3.0", "pw6", "z4.4", "z3.1", "y3.7", "z4.2", "fin0", "pw7", "z3.5",
    "pwe", "z4.6", "z3.7", "y4.5", "y4.7", "y3.4", "z3.4", "z4.7", "z4.5", "fin1",
    "mg",
)


class Place:
    def __init__(self, ndp):
        self.ndp = ndp
        self.dp = dp = lax.axis_index("dp")
        self.t = t = lax.axis_index("tensor")
        self.near_t, self.skip_t, self.far_t = t + 1 - 2 * lax.rem(t, 2), lax.rem(t + 2, 4), 3 - t
        self.near, self.skip, self.far = (dp, self.near_t), (dp, self.skip_t), (dp, self.far_t)
        self.inner = (t == 1) | (t == 2)
        self.first = lax.rem(dp, 2) == 0
        self.twin = (dp + 1 - 2 * lax.rem(dp, 2), t)
        self.outer = (t == 0) | (t == 3)

    def peer(self, step):
        return lax.rem(self.dp + step, self.ndp)

    def greet(self):
        sem = pltpu.get_barrier_semaphore()
        for device in (self.near, self.skip, self.far):
            pl.semaphore_signal(sem, inc=1, device_id=device, device_id_type=MESH)

        @pl.loop(1, self.ndp)
        def _(step):
            pl.semaphore_signal(
                sem, inc=1, device_id=(self.peer(step), self.t), device_id_type=MESH
            )

    def meet(self):
        pl.semaphore_wait(pltpu.get_barrier_semaphore(), 3 + self.ndp - 1)


class Spread:
    def __init__(self, place, source, target, ssem, rsem):
        self.place, self.source, self.target, self.ssem, self.rsem = place, source, target, ssem, rsem

    def copy(self, step):
        there = self.place.peer(step)
        return remote(
            self.source(there),
            self.target.at[self.place.dp],
            self.ssem.at[step],
            self.rsem.at[self.place.dp],
            (there, self.place.t),
        )

    def arrival(self, step):
        there = self.place.peer(step)
        return remote(
            self.source(there),
            self.target.at[there],
            self.ssem.at[step],
            self.rsem.at[there],
            (there, self.place.t),
        )

    def own(self):
        here = self.place.dp
        return pltpu.make_async_copy(self.source(here), self.target.at[here], self.ssem.at[0])

    def start(self):
        self.own().start()

        @pl.loop(1, self.place.ndp)
        def _(step):
            self.copy(step).start()

    def wait(self):
        self.own().wait()

        @pl.loop(1, self.place.ndp)
        def _(step):
            self.copy(step).wait_send()
            self.arrival(step).wait_recv()


class LineSum:
    def __init__(self, place, part, in2, total, sems):
        self.place, self.part, self.in2, self.total, self.sems = place, part, in2, total, sems

    def copy(self, stage, i):
        src = (self.part, self.part, self.total)[stage].at[i]
        dst = (self.total, self.in2, self.total)[stage].at[i]
        device = (self.place.near, self.place.far, self.place.near)[stage]
        return remote(src, dst, self.sems.at[2 * stage, i], self.sems.at[2 * stage + 1, i], device)

    def start(self, i):
        @pl.when(self.place.outer)
        def _():
            self.copy(0, i).start()

    def cross(self, i):
        @pl.when(self.place.inner)
        def _():
            self.copy(0, i).wait_recv()
            self.part[i] = (self.part[i].astype(F32) + self.total[i].astype(F32)).astype(BF16)
            self.copy(1, i).start()

    def back(self, i):
        @pl.when(self.place.inner)
        def _():
            self.copy(1, i).wait_recv()
            self.total[i] = (self.part[i].astype(F32) + self.in2[i].astype(F32)).astype(BF16)
            self.copy(2, i).start()

    def finish(self, i):
        @pl.when(self.place.outer)
        def _():
            self.copy(2, i).wait_recv()

    def drain(self, i):
        @pl.when(self.place.outer)
        def _():
            self.copy(0, i).wait_send()

        @pl.when(self.place.inner)
        def _():
            self.copy(1, i).wait_send()
            self.copy(2, i).wait_send()

    def value(self, b):
        return self.total[b * PARTS : (b + 1) * PARTS].reshape(L, D).astype(F32)


def layer_kernel(
    nb, ndp,
    noise, labels, freq, table, pw, ada, act_in, cot_in, wq_in, wo_in, wgu_in, wd_in, pf,
    sg_o, out_o, in_o, wff_o, watt_o, mg_o, pw_o, aux_o,
    act, cot, wq, wo, wgu, wd, isem, kw, mod, pbuf, psem,
    bsend, own, ring, inward, across, bsem,
    qs, ks, vs, probs, gate, att, normed_t,
    part1, in1, total1, sem1,
    part2, in2, total2, sem2,
    part3, in3, total3, sem3,
    part4, in4, total4, sem4,
    norm2_t, fgrad, fgrad_t, swish, hgrad, bgrad_t, gated_s, pgrad, mgrad_mid,
    sg, gsem, acc, wff, watt, mgs, pws, aux, out_s, in_s, osem, turn, xsem,
):
    place = Place(ndp)
    place.greet()
    nch = nb * NRC
    slots = pbuf.shape[0]
    rows_per = D // ndp

    def fetch(k, slot):
        b, r = k // NRC, k % NRC
        return pltpu.make_async_copy(pf.at[b, :, pl.ds(r * RC, RC), :], pbuf.at[slot], psem.at[slot])

    for k in range(slots):
        fetch(k, k).start()
    loads = [
        pltpu.make_async_copy(src, dst, isem.at[n])
        for n, (src, dst) in enumerate(
            ((act_in, act), (wq_in, wq), (wo_in, wo), (cot_in, cot), (wgu_in, wgu), (wd_in, wd))
        )
    ]
    for load in loads:
        load.start()
    ready = set()

    def need(*numbers):
        for n in numbers:
            if n not in ready:
                ready.add(n)
                loads[n].wait()


    row, col = iota((192, 12), 0), iota((192, 12), 1)
    group, head = row // 48, lax.rem(row // 16, 3)
    owner = jnp.where(
        group == 0,
        place.far_t,
        jnp.where(group == 1, place.skip_t, jnp.where(group == 2, place.near_t, place.t)),
    )
    pick = (col == owner * 3 + head).astype(F32).astype(BF16)
    chosen = nn(pick, pw[...]).astype(BF16)
    channels = pw.shape[1]
    widen = (iota((channels, channels * 16), 1) // 16 == iota((channels, channels * 16), 0)).astype(F32)
    wide = nn(chosen, widen.astype(BF16))
    diagonal = lax.rem(iota(wide.shape, 0), 16) == lax.rem(iota(wide.shape, 1), 16)
    kw[...] = jnp.where(diagonal, wide, 0.0).astype(BF16)

    aux_spread = Spread(place, lambda j: aux.at[j], aux_o, xsem.at[0], xsem.at[1])

    def inwards(k):
        return remote(bsend.at[k], inward.at[k], bsem.at[0, k], bsem.at[1, k], place.near)

    def crossing(k):
        return remote(
            bsend.at[k, pl.ds(0, 2)], across.at[k], bsem.at[2, k], bsem.at[3, k], place.far
        )

    def outwards(k):
        return remote(bsend.at[k, 2], inward.at[k, 0], bsem.at[4, k], bsem.at[5, k], place.near)

    def bias(k):
        slot = k % slots
        fetch(k, slot).wait()
        for s in range(RC // 16):
            here = pl.ds(s * 16, 16)
            rows = pbuf[slot, :, here, :].reshape(-1, L)
            out = nn(kw[...], rows)
            three = out[:144].reshape(3, LH, 16, L)

            @pl.when(place.outer)
            def _():
                bsend[k, :, :, here, :] = three.astype(BF16)

            @pl.when(place.inner)
            def _():
                ring[k % RING, :, :, here, :] = three

            own[k, :, here, :] = out[144:].reshape(LH, 16, L)

        if k + slots < nch:
            fetch(k + slots, slot).start()
        if k == nch - 1:
            for n in range(slots):
                fetch(n, n).start()

    def send_bias(k):
        @pl.when(place.outer)
        def _():
            inwards(k).start()

    def pass_turn(_):
        @pl.when(place.outer & place.first)
        def _():
            inwards(NRC - 1).wait_send()
            pl.semaphore_signal(turn, inc=1, device_id=place.twin, device_id_type=MESH)

    def take_turn(_):
        @pl.when(place.outer & ~place.first)
        def _():
            pl.semaphore_wait(turn, 1)

    def relay(k):
        @pl.when(place.inner)
        def _():
            inwards(k).wait_recv()
            bsend[k, 0] = (ring[k % RING, 0] + inward[k, 1].astype(F32)).astype(BF16)
            bsend[k, 1] = (ring[k % RING, 1] + inward[k, 0].astype(F32)).astype(BF16)
            crossing(k).start()

    def relay_out(k):
        @pl.when(place.inner)
        def _():
            crossing(k).wait_recv()
            bsend[k, 2] = (ring[k % RING, 2] + across[k, 1].astype(F32)).astype(BF16)
            outwards(k).start()

    def modulate():
        def scoped(rows, sem):
            load = pltpu.make_async_copy(ada, rows, sem)
            load.start()
            width = DC // ndp
            conds, hots = [], []
            for b in range(nb):
                phase = (2.0 * math.pi * noise[b]) * freq[...]
                row = jnp.concatenate([jnp.cos(phase), jnp.sin(phase)], axis=1)
                for n in range(NCLASS):
                    row += table[n : n + 1, :].astype(F32) * (labels[b] == n).astype(F32)
                conds.append(row)
                hots.append((iota((1, width), 1) == labels[b]).astype(F32))
            cond = jnp.concatenate(conds, axis=0)
            sigmoid = jax.nn.sigmoid(cond)
            silu = cond * sigmoid
            factor = sigmoid * (1.0 + cond * (1.0 - sigmoid))
            hot = jnp.concatenate(hots, axis=0)
            for j in range(ndp):
                cols = slice(j * width, (j + 1) * width)
                aux[j] = jnp.concatenate([silu[:, cols], factor[:, cols], hot], axis=0)
            high = silu.astype(BF16)
            rest = silu - high.astype(F32)
            middle = rest.astype(BF16)
            low = (rest - middle.astype(F32)).astype(BF16)
            terms = jnp.concatenate([high, middle, low], axis=0)
            load.wait()
            for n in range(6):
                out = nn(terms, rows[n])
                mod[:, n, :] = out[:nb] + out[nb : 2 * nb] + out[2 * nb : 3 * nb]

        pl.run_scoped(scoped, pltpu.VMEM(ada.shape, BF16), pltpu.SemaphoreType.DMA)

    def project(b):
        need(0, 1)
        unit, _ = normalize(act[pl.ds(b * L, L)].astype(F32))
        m = mod[b]
        low = (unit * (1.0 + m[0:1]) + m[1:2]).astype(BF16)
        normed_t[:, pl.ds(b * L, L)] = low.T
        for piece in range(2):
            out = nt(low, wq[pl.ds(piece * 384, 384), :])
            for n in range(6):
                which, h = piece * 2 + n // 3, n % 3
                column = out[:, n * HD : (n + 1) * HD]
                if which == 0:
                    qs[b, h] = (column.astype(BF16).astype(F32) * 0.125).astype(BF16)
                elif which == 1:
                    ks[b, h] = column.astype(BF16)
                elif which == 2:
                    vs[b, h] = column.astype(BF16)
            if piece == 1:
                gate[b] = jax.nn.sigmoid(out[:, LW:])

    sum1 = LineSum(place, part1, in1, total1, sem1)
    sum2 = LineSum(place, part2, in2, total2, sem2)
    sum3 = LineSum(place, part3, in3, total3, sem3)
    sum4 = LineSum(place, part4, in4, total4, sem4)

    def attend(b):
        need(2)
        for k in range(b * NRC, (b + 1) * NRC):

            @pl.when(place.outer)
            def _():
                outwards(k).wait_recv()

        heads = []
        for h in range(LH):
            here = slice(b * NRC, (b + 1) * NRC)
            from_near = jnp.where(place.inner, inward[here, 2, h], inward[here, 0, h]).astype(F32)
            from_far = jnp.where(place.inner, across[here, 0, h], jnp.zeros((), BF16)).astype(F32)
            bias_rows = (own[here, h] + (from_near + from_far)).reshape(L, L)
            scores = nt(qs[b, h], ks[b, h]) + bias_rows
            e = jnp.exp(scores - jnp.max(scores, axis=-1, keepdims=True))
            p = (e * (1.0 / jnp.sum(e, axis=-1, keepdims=True))).astype(BF16)
            probs[b, h] = p
            heads.append(nn(p, vs[b, h]))
        attended = jnp.concatenate(heads, axis=1)
        att[b] = attended
        gated = (attended * gate[b]).astype(BF16)
        gated_s[pl.ds(b * L, L)] = gated
        part1[b * PARTS : (b + 1) * PARTS] = nn(gated, wo[...]).astype(BF16).reshape(PARTS, PR, D)
        for i in range(b * PARTS, (b + 1) * PARTS):
            sum1.start(i)

    def prepare():
        need(3)
        for b in range(nb):
            low = (cot[pl.ds(b * L, L)].astype(F32) * jax.nn.sigmoid(mod[b, 5:6])).astype(BF16)
            fgrad[pl.ds(b * L, L)] = low
            fgrad_t[:, pl.ds(b * L, L)] = low.T

    def middle_of(b):
        rows = act[pl.ds(b * L, L)].astype(F32)
        return rows + jax.nn.sigmoid(mod[b, 2:3]) * sum1.value(b)

    def feedforward(b):
        need(4, 5)
        here = pl.ds(b * L, L)
        unit, _ = normalize(middle_of(b))
        low = (unit * (1.0 + mod[b, 3:4]) + mod[b, 4:5]).astype(BF16)
        norm2_t[:, here] = low.T
        for f in range(3):
            tile, tile_up = pl.ds(f * 256, 256), pl.ds(D + f * 256, 256)
            g = nn(low, wgu[:, tile])
            up = nn(low, wgu[:, tile_up])
            back = nt(fgrad[here], wd[tile, :])
            s = jax.nn.sigmoid(g)
            silu = g * s
            swish[here, tile] = (silu * up).astype(BF16)
            hgrad[here, tile_up] = (back * silu).astype(BF16)
            hgrad[here, tile] = (back * up * s * (1.0 + g * (1.0 - s))).astype(BF16)
        here_parts = pl.ds(b * PARTS, PARTS)
        for d in range(3):
            tile = pl.ds(d * 256, 256)
            part2[here_parts, :, tile] = (
                nt(hgrad[here, :], wgu[tile, :]).astype(BF16).reshape(PARTS, PR, 256)
            )
        for i in range(b * PARTS, (b + 1) * PARTS):
            sum2.start(i)

    def feedforward_out(b):
        here, here_parts = pl.ds(b * L, L), pl.ds(b * PARTS, PARTS)
        for d in range(3):
            tile = pl.ds(d * 256, 256)
            part3[here_parts, :, tile] = (
                nn(swish[here, :], wd[:, tile]).astype(BF16).reshape(PARTS, PR, 256)
            )
        for i in range(b * PARTS, (b + 1) * PARTS):
            sum3.start(i)

    def put_rows(target, tile, values):
        low = values.astype(BF16)
        for j in range(ndp):
            target[j, :, tile] = low[j * rows_per : (j + 1) * rows_per]

    wff_spread = Spread(place, lambda j: wff.at[j], wff_o, xsem.at[2], xsem.at[3])
    watt_spread = Spread(place, lambda j: watt.at[j], watt_o, xsem.at[4], xsem.at[5])

    def weights_ff():
        for f in range(6):
            tile = pl.ds(f * 256, 256)
            put_rows(wff, tile, nn(norm2_t[...], hgrad[:, tile]))
        for f in range(3):
            put_rows(wff, pl.ds(2 * D + f * 256, 256), nn(fgrad_t[...], swish[:, pl.ds(f * 256, 256)]))
        wff_spread.start()

    def weights_att():
        for f in range(3):
            tile = pl.ds(f * 256, 256)
            put_rows(watt, tile, nn(normed_t[...], pgrad[:, tile]))
        put_rows(watt, pl.ds(D, LW), nn(bgrad_t[...], gated_s[...]))
        watt_spread.start()

    def share(k, n):
        source, target, device = (
            (3, 2, place.near),
            (3, 0, place.far),
            (2, 1, place.far),
            (0, 1, place.near),
            (1, 0, place.near),
        )[n]
        return remote(
            sg.at[source, k], sg.at[target, k], gsem.at[2 * n, k], gsem.at[2 * n + 1, k], device
        )

    def share_near(k):
        share(k, 0).start()

    def share_far(k):
        @pl.when(place.inner)
        def _():
            share(k, 1).start()

    def pass_far(k):
        @pl.when(place.inner)
        def _():
            share(k, 0).wait_recv()
            share(k, 2).start()

    def pass_near(k):
        @pl.when(place.inner)
        def _():
            share(k, 1).wait_recv()
            share(k, 3).start()
            share(k, 2).wait_recv()
            share(k, 4).start()

    def attend_back(b):
        here = pl.ds(b * L, L)
        m = mod[b]
        gate_one = jax.nn.sigmoid(m[2:3])
        middle = middle_of(b)
        unit, inverse = normalize(middle)
        two = sum2.value(b)
        up = cot[here].astype(F32)
        mid_grad = up + norm_back(two * (1.0 + m[3:4]), unit, inverse)
        mgrad_mid[here] = mid_grad
        low = (mid_grad * gate_one).astype(BF16)
        bgrad_t[:, here] = low.T
        mgs[b, 2:3] = (
            jnp.sum(mid_grad * sum1.value(b), axis=0, keepdims=True) * gate_one * (1.0 - gate_one)
        )
        mgs[b, 3:4] = jnp.sum(two * unit, axis=0, keepdims=True)
        mgs[b, 4:5] = jnp.sum(two, axis=0, keepdims=True)
        gated_grad = nt(low, wo[...])
        opened = gate[b]
        att_grad = (gated_grad * opened).astype(BF16)
        attended = att[b]
        pgrad[here, pl.ds(3 * LW, LW)] = (gated_grad * attended * opened * (1.0 - opened)).astype(BF16)
        product = att_grad.astype(F32) * attended
        dq, dk, dv = [], [], []
        for h in range(LH):
            cols = slice(h * HD, (h + 1) * HD)
            head_grad = att_grad[:, cols]
            delta = jnp.sum(product[:, cols], axis=-1, keepdims=True)
            p = probs[b, h]
            score_grad = (p.astype(F32) * (nt(head_grad, vs[b, h]) - delta)).astype(BF16)
            for r in range(NRC):
                sg[3, b * NRC + r, h] = score_grad[r * RC : (r + 1) * RC]
            dq.append(nn(score_grad, ks[b, h]) * 0.125)
            dk.append(tn(score_grad, qs[b, h]))
            dv.append(tn(p, head_grad))
        pgrad[here, pl.ds(0, 3 * LW)] = jnp.concatenate(dq + dk + dv, axis=1).astype(BF16)

    def project_back(b):
        here, here_parts = pl.ds(b * L, L), pl.ds(b * PARTS, PARTS)
        for d in range(3):
            tile = pl.ds(d * 256, 256)
            part4[here_parts, :, tile] = (
                nn(pgrad[here, :], wq[:, tile]).astype(BF16).reshape(PARTS, PR, 256)
            )
        for i in range(b * PARTS, (b + 1) * PARTS):
            sum4.start(i)

    def pair_weight(k):
        slot = k % slots

        @pl.when(place.outer)
        def _():
            share(k, 0).wait_recv()
            share(k, 3).wait_recv()
            share(k, 4).wait_recv()

        fetch(k, slot).wait()
        total = None
        for s in range(RC // 16):
            rows = pbuf[slot, :, pl.ds(s * 16, 16), :].reshape(-1, L)
            grads = sg[:, k, :, pl.ds(s * 16, 16), :].reshape(-1, L)
            out = nt(rows, grads)
            total = out if total is None else total + out
        if k == 0:
            acc[...] = total
        else:
            acc[...] += total
        store_sg(k).start()
        if k + slots < nch:
            fetch(k + slots, slot).start()

    def pair_weight_end():
        values = acc[...].reshape(channels, 16, 192)
        mask = iota((16, 192), 0) == lax.rem(iota((16, 192), 1), 16)
        picked = jnp.sum(jnp.where(mask[None], values, 0.0), axis=1)
        row, col = iota((16, 192), 0), iota((16, 192), 1)
        group, head = col // 48, lax.rem(col // 16, 3)
        owner = jnp.where(
            group == 0,
            place.far_t,
            jnp.where(group == 1, place.skip_t, jnp.where(group == 2, place.near_t, place.t)),
        )
        pws[...] = nt((row == owner * 3 + head).astype(F32), picked, precision=highest)

    def store_sg(k):
        return pltpu.make_async_copy(sg.at[:, k], sg_o.at[:, k], osem.at[0, k])

    def store_rows(b, n):
        source, target = ((out_s, out_o), (in_s, in_o))[n]
        here = pl.ds(b * L, L)
        return pltpu.make_async_copy(source.at[here], target.at[here], osem.at[1 + n, b])

    def finish_rows(b):
        here = pl.ds(b * L, L)
        m = mod[b]
        gate_two = jax.nn.sigmoid(m[5:6])
        ffn = sum3.value(b)
        out_s[here] = (middle_of(b) + gate_two * ffn).astype(BF16)
        mgs[b, 5:6] = (
            jnp.sum(cot[here].astype(F32) * ffn, axis=0, keepdims=True) * gate_two * (1.0 - gate_two)
        )
        unit, inverse = normalize(act[here].astype(F32))
        one = sum4.value(b)
        mgs[b, 0:1] = jnp.sum(one * unit, axis=0, keepdims=True)
        mgs[b, 1:2] = jnp.sum(one, axis=0, keepdims=True)
        in_s[here] = (mgrad_mid[here] + norm_back(one * (1.0 + m[0:1]), unit, inverse)).astype(BF16)
        for n in range(2):
            store_rows(b, n).start()

    mg_spread = Spread(place, lambda j: mgs, mg_o, xsem.at[6], xsem.at[7])
    pw_spread = Spread(place, lambda j: pws, pw_o, xsem.at[8], xsem.at[9])

    steps = {
        "bias": bias,
        "E": send_bias,
        "ts": pass_turn,
        "tw": take_turn,
        "aux": aux_spread.start,
        "rela": relay,
        "relb": relay_out,
        "mod": modulate,
        "proj": project,
        "prep": prepare,
        "attend": attend,
        "ffnA": feedforward,
        "ffnB": feedforward_out,
        "backA": attend_back,
        "one": project_back,
        "P": share_near,
        "Q": share_far,
        "R": pass_far,
        "S": pass_near,
        "pw": pair_weight,
        "wff": weights_ff,
        "watt": weights_att,
        "fin": finish_rows,
        "mg": mg_spread.start,
        "pwe": pair_weight_end,
    }
    for n, total in enumerate((sum1, sum2, sum3, sum4)):
        steps[f"x{n + 1}."] = total.cross
        steps[f"y{n + 1}."] = total.back
        steps[f"z{n + 1}."] = total.finish
    for entry in ORDER:
        name = entry.rstrip("0123456789")
        number = entry[len(name) :]
        steps[name](*([int(number)] if number else []))
        if entry == "bias0":
            place.meet()
    done = set(ORDER)
    if "pwe" in done:
        pw_spread.start()

    for k in range(nch):
        if f"E{k}" in done:

            @pl.when(place.outer & ~place.first if k == NRC - 1 and "ts0" in done else place.outer)
            def _():
                inwards(k).wait_send()

        if f"rela{k}" in done:

            @pl.when(place.inner)
            def _():
                crossing(k).wait_send()

        if f"relb{k}" in done:

            @pl.when(place.inner)
            def _():
                outwards(k).wait_send()

        if f"P{k}" in done:
            share(k, 0).wait_send()

        for n, name in ((1, "Q"), (2, "R"), (3, "S"), (4, "S")):
            if f"{name}{k}" in done:

                @pl.when(place.inner)
                def _():
                    share(k, n).wait_send()

    for a, (total, source) in enumerate(
        ((sum1, "attend"), (sum2, "ffnA"), (sum3, "ffnB"), (sum4, "one"))
    ):
        for i in range(PARTS * nb):
            if f"{source}{i // PARTS}" in done:

                @pl.when(place.outer)
                def _():
                    total.copy(0, i).wait_send()

            if f"x{a + 1}.{i}" in done:

                @pl.when(place.inner)
                def _():
                    total.copy(1, i).wait_send()

            if f"y{a + 1}.{i}" in done:

                @pl.when(place.inner)
                def _():
                    total.copy(2, i).wait_send()

    for spread, name in (
        (aux_spread, "aux"), (wff_spread, "wff"), (watt_spread, "watt"), (mg_spread, "mg"), (pw_spread, "pwe"),
    ):
        if name in done:
            spread.wait()
    for k in range(nch):
        if f"pw{k}" in done:
            store_sg(k).wait()
    for b in range(nb):
        if f"fin{b}" in done:
            for n in range(2):
                store_rows(b, n).wait()


def vmem_specs(n):
    return [pl.BlockSpec(memory_space=pltpu.VMEM)] * n


def any_specs(n):
    return [pl.BlockSpec(memory_space=pl.ANY)] * n


def layer_call(nb, ndp, noise, labels, freq, table, pw, ada, act, cot, wq, wo, wgu, wd, pf):
    nch = nb * NRC
    rows = nb * L
    rows_per = D // ndp
    channels = pf.shape[1]
    hidden = wd.shape[0]
    shapes = [
        ((4, nch, LH, RC, L), BF16),
        ((rows, D), BF16),
        ((rows, D), BF16),
        ((ndp, rows_per, 3 * hidden), BF16),
        ((ndp, rows_per, 5 * LW), BF16),
        ((ndp, nb, 6, D), F32),
        ((ndp, 16, channels), F32),
        ((ndp, 3 * nb, DC // ndp), F32),
    ]
    dma = pltpu.SemaphoreType.DMA

    def line():
        return [pltpu.VMEM((PARTS * nb, PR, D), BF16)] * 3 + [dma((6, PARTS * nb))]

    scratch = [
        pltpu.VMEM((rows, D), BF16),
        pltpu.VMEM((rows, D), BF16),
        pltpu.VMEM(wq.shape, BF16),
        pltpu.VMEM(wo.shape, BF16),
        pltpu.VMEM(wgu.shape, BF16),
        pltpu.VMEM(wd.shape, BF16),
        dma((6,)),
        pltpu.VMEM((192, channels * 16), BF16),
        pltpu.VMEM((nb, 6, D), F32),
        pltpu.VMEM((3, channels, RC, L), BF16),
        dma((3,)),
        pltpu.VMEM((nch, 3, LH, RC, L), BF16),
        pltpu.VMEM((nch, LH, RC, L), F32),
        pltpu.VMEM((RING, 3, LH, RC, L), F32),
        pltpu.VMEM((nch, 3, LH, RC, L), BF16),
        pltpu.VMEM((nch, 2, LH, RC, L), BF16),
        dma((6, nch)),
        pltpu.VMEM((nb, LH, L, HD), BF16),
        pltpu.VMEM((nb, LH, L, HD), BF16),
        pltpu.VMEM((nb, LH, L, HD), BF16),
        pltpu.VMEM((nb, LH, L, L), BF16),
        pltpu.VMEM((nb, L, LW), F32),
        pltpu.VMEM((nb, L, LW), F32),
        pltpu.VMEM((D, rows), BF16),
        *line(),
        *line(),
        *line(),
        *line(),
        pltpu.VMEM((D, rows), BF16),
        pltpu.VMEM((rows, D), BF16),
        pltpu.VMEM((D, rows), BF16),
        pltpu.VMEM((rows, hidden), BF16),
        pltpu.VMEM((rows, 2 * hidden), BF16),
        pltpu.VMEM((D, rows), BF16),
        pltpu.VMEM((rows, LW), BF16),
        pltpu.VMEM((rows, 4 * LW), BF16),
        pltpu.VMEM((rows, D), F32),
        pltpu.VMEM((4, nch, LH, RC, L), BF16),
        dma((10, nch)),
        pltpu.VMEM((channels * 16, 192), F32),
        pltpu.VMEM((ndp, rows_per, 3 * hidden), BF16),
        pltpu.VMEM((ndp, rows_per, 5 * LW), BF16),
        pltpu.VMEM((nb, 6, D), F32),
        pltpu.VMEM((16, channels), F32),
        pltpu.VMEM((ndp, 3 * nb, DC // ndp), F32),
        pltpu.VMEM((rows, D), BF16),
        pltpu.VMEM((rows, D), BF16),
        dma((3, nch)),
        pltpu.SemaphoreType.REGULAR,
        dma((10, ndp)),
    ]
    return pl.pallas_call(
        functools.partial(layer_kernel, nb, ndp),
        out_shape=[jax.ShapeDtypeStruct(*s) for s in shapes],
        in_specs=[pl.BlockSpec(memory_space=pltpu.SMEM)] * 2 + vmem_specs(3) + any_specs(8),
        out_specs=any_specs(8),
        scratch_shapes=scratch,
        compiler_params=pltpu.CompilerParams(
            collective_id=0, has_side_effects=True, vmem_limit_bytes=VMEM_LIMIT
        ),
        name="layer",
    )(noise, labels, freq, table, pw, ada, act, cot, wq, wo, wgu, wd, pf)


def ending_kernel(
    nb, ndp,
    pw, mg, aux, pwi, sg_i, ada_i, out_i, in_i, wff_i, watt_i,
    pg, out_o, in_o, ada_o, class_o, wgu_o, wd_o, wq_o, wo_o, pw_o,
    sg, ada, rows, wff, watt, obuf, osem, gsem, isem,
):
    t = lax.axis_index("tensor")
    nch = nb * NRC
    hidden = wd_o.shape[1]
    slots = obuf.shape[0]

    def load(k):
        return pltpu.make_async_copy(sg_i.at[:, k], sg.at[:, k], gsem.at[k])

    others = [
        pltpu.make_async_copy(src, dst, isem.at[n])
        for n, (src, dst) in enumerate(
            (
                (wff_i, wff),
                (watt_i, watt),
                (out_i, rows.at[0]),
                (in_i, rows.at[1]),
                (ada_i, ada),
            )
        )
    ]
    for k in range(nch):
        load(k).start()
        if k == 1:
            for copy in others:
                copy.start()
    passed = [
        pltpu.make_async_copy(rows.at[n], target, isem.at[5 + n])
        for n, target in enumerate((out_o, in_o))
    ]
    channels = pw.shape[1]
    row, col = iota((12, 192), 0), iota((12, 192), 1)
    group, head = col // 48, lax.rem(col // 16, 3)
    near_t, skip_t, far_t = t + 1 - 2 * lax.rem(t, 2), lax.rem(t + 2, 4), 3 - t
    owner = jnp.where(
        group == 0, far_t, jnp.where(group == 1, skip_t, jnp.where(group == 2, near_t, t))
    )
    pick = (row == owner * 3 + head).astype(F32).astype(BF16)
    chosen = tn(pw[...], pick).astype(BF16)
    widen = (iota((channels * 16, channels), 0) // 16 == iota((channels * 16, channels), 1)).astype(F32)
    wide = nn(widen.astype(BF16), chosen)
    diagonal = lax.rem(iota(wide.shape, 0), 16) == lax.rem(iota(wide.shape, 1), 16)
    spread = jnp.where(diagonal, wide, 0.0).astype(BF16)

    def store(k):
        b, r = k // NRC, k % NRC
        return pltpu.make_async_copy(
            obuf.at[k % slots], pg.at[b, :, pl.ds(r * RC, RC), :], osem.at[k % slots]
        )

    def pair_grad(k):
        if k >= slots:
            store(k - slots).wait()
        load(k).wait()
        for s in range(RC // 16):
            grads = sg[:, k, :, pl.ds(s * 16, 16), :].reshape(-1, L)
            obuf[k % slots, :, pl.ds(s * 16, 16), :] = (
                nn(spread, grads).reshape(channels, 16, L).astype(BF16)
            )
        store(k).start()

    def add(source, tile):
        total = source[0, :, tile].astype(F32)
        for j in range(1, ndp):
            total += source[j, :, tile].astype(F32)
        return total

    def ff_sums():
        others[0].wait()
        total = add(wff, pl.ds(0, 3 * hidden))
        wgu_o[:, 0, :] = total[:, :hidden]
        wgu_o[:, 1, :] = total[:, hidden : 2 * hidden]
        wd_o[...] = total[:, 2 * hidden :]

    def att_sums():
        others[1].wait()
        total = add(watt, pl.ds(0, 5 * LW))
        for n in range(4):
            wq_o[:, n, :] = total[:, n * LW : (n + 1) * LW]
        wo_o[...] = total[:, 4 * LW :].T
        total = pwi[0]
        for j in range(1, ndp):
            total += pwi[j]
        pw_o[...] = total[: pw_o.shape[0]]

    def pass_rows():
        for n in range(2):
            others[2 + n].wait()
            passed[n].start()

    def condition():
        def each(kind):
            return jnp.concatenate([aux[j, kind * nb : (kind + 1) * nb] for j in range(ndp)], axis=0)

        others[4].wait()
        silu, factor, hot = each(0), each(1), each(2)
        width = silu.shape[1]
        back = None
        for m in range(6):
            grads = mg[:, m, :]
            ada_o[m] = tn(silu, grads, precision=highest)
            part = nt(grads, ada[m].astype(F32), precision=highest)
            back = part if back is None else back + part
        here = lax.axis_index("dp") * width
        mine = (iota((DC, width), 0) == here + iota((DC, width), 1)).astype(F32)
        back = nn(back, mine, precision=highest)
        class_o[...] = tn(hot, back * factor, precision=highest)[:NCLASS]

    after = {0: pass_rows, 1: ff_sums, 2: att_sums, 3: condition}
    for k in range(nch):
        pair_grad(k)
        if k in after:
            after[k]()
    for k in range(max(nch - slots, 0), nch):
        store(k).wait()
    for copy in passed:
        copy.wait()


def ending_call(nb, ndp, pw, mg, aux, pwi, sg, ada, out, inputs_grad, wff, watt, pair_shape):
    rows_per = D // ndp
    hidden = wff.shape[2] // 3
    width = DC // ndp
    channels = pair_shape[1]
    dma = pltpu.SemaphoreType.DMA
    shapes = [
        (pair_shape, BF16),
        (out.shape, BF16),
        (out.shape, BF16),
        ((6, width, D), F32),
        ((NCLASS, width), F32),
        ((rows_per, 2, hidden), F32),
        ((rows_per, hidden), F32),
        ((rows_per, 4, LW), F32),
        ((LW, rows_per), F32),
        ((12, channels), F32),
    ]
    return pl.pallas_call(
        functools.partial(ending_kernel, nb, ndp),
        out_shape=[jax.ShapeDtypeStruct(*s) for s in shapes],
        in_specs=vmem_specs(4) + any_specs(6),
        out_specs=any_specs(3) + vmem_specs(7),
        scratch_shapes=[
            pltpu.VMEM(sg.shape, BF16),
            pltpu.VMEM(ada.shape, BF16),
            pltpu.VMEM((2, *out.shape), BF16),
            pltpu.VMEM(wff.shape, BF16),
            pltpu.VMEM(watt.shape, BF16),
            pltpu.VMEM((3, channels, RC, L), BF16),
            dma((3,)),
            dma((nb * NRC,)),
            dma((7,)),
        ],
        compiler_params=pltpu.CompilerParams(vmem_limit_bytes=VMEM_LIMIT),
        name="ending",
    )(pw, mg, aux, pwi, sg, ada, out, inputs_grad, wff, watt)


def shards(
    ndp,
    activations,
    noise_times,
    cath_labels,
    class_table,
    ada_weight,
    qkvg_weight,
    out_weight,
    pair_weight,
    gateup_weight,
    down_weight,
    pair_features,
    cotangent,
):
    chains = pair_features.shape[0]
    freq = jnp.asarray(np.exp(np.arange(DC // 2) * (math.log(1000.0) / (DC // 2)))[None], F32)
    ada = jnp.transpose(ada_weight, (1, 0, 2))
    wq = jnp.transpose(qkvg_weight, (1, 2, 0)).reshape(-1, D)
    wgu = gateup_weight.reshape(D, -1)
    pw = pair_weight.T
    sg, out, inputs_grad, wff, watt, mg, pwi, aux = layer_call(
        chains, ndp, noise_times, cath_labels, freq, class_table, pw, ada, activations, cotangent,
        wq, out_weight, wgu, down_weight, pair_features,
    )
    pair_grad, out, inputs_grad, ada_sum, class_sum, gateup, down, qkvg, outw, pair_sum = ending_call(
        chains, ndp, pw, mg.reshape(-1, 6, D), aux, pwi, sg, ada, out, inputs_grad, wff, watt,
        pair_features.shape,
    )
    return (
        out,
        inputs_grad,
        pair_grad,
        class_sum,
        jnp.transpose(ada_sum, (1, 0, 2)),
        qkvg,
        outw,
        pair_sum.T,
        gateup,
        down.T,
    )


def solution(mesh):
    placed = (
        P("dp", None),
        P("dp"),
        P("dp"),
        P(),
        P(),
        P(None, None, "tensor"),
        P("tensor", None),
        P("tensor", None),
        P(None, None, "tensor"),
        P("tensor", None),
        P("dp", "tensor", None, None),
        P("dp", None),
    )
    return jax.shard_map(
        functools.partial(shards, mesh.shape["dp"]),
        mesh=mesh,
        in_specs=placed,
        out_specs=(
            P("dp", None),
            P("dp", None),
            P("dp", "tensor", None, None),
            P(None, "dp"),
            P("dp", None, None),
            P("dp", None, "tensor"),
            P("tensor", "dp"),
            P("tensor", None),
            P("dp", None, "tensor"),
            P("tensor", "dp"),
        ),
        check_vma=False,
    )
```

```python
import functools
import math

import jax
import jax.numpy as jnp
import numpy as np
from jax import lax
from jax.experimental import pallas as pl
from jax.experimental.pallas import tpu as pltpu
from jax.sharding import PartitionSpec as P

D = 768
HD = 64
DC = 256
NCLASS = 4
L = 256
RC = 64
NRC = L // RC
LH = 3
LW = LH * HD
PARTS = 4
PR = L // PARTS
RING = 4
RAW = 96
MESH = pl.DeviceIdType.MESH
F32 = jnp.float32
BF16 = jnp.bfloat16
VMEM_LIMIT = 63 * 2**20

highest = lax.Precision.HIGHEST


def normalize(values):
    centred = values - jnp.mean(values, axis=-1, keepdims=True)
    inverse = lax.rsqrt(jnp.mean(centred * centred, axis=-1, keepdims=True) + 1e-05)
    return (centred * inverse, inverse)


def norm_back(grad_unit, unit_rows, inverse):
    mean_grad = jnp.mean(grad_unit, axis=-1, keepdims=True)
    mean_proj = jnp.mean(grad_unit * unit_rows, axis=-1, keepdims=True)
    return inverse * (grad_unit - mean_grad - unit_rows * mean_proj)


def nn(a, b, precision=None):
    return lax.dot_general(
        a, b, (((1,), (0,)), ((), ())), preferred_element_type=F32, precision=precision
    )


def nt(a, b, precision=None):
    return lax.dot_general(
        a, b, (((1,), (1,)), ((), ())), preferred_element_type=F32, precision=precision
    )


def tn(a, b, precision=None):
    return lax.dot_general(
        a, b, (((0,), (0,)), ((), ())), preferred_element_type=F32, precision=precision
    )


def in_terms(values):
    high = values.astype(BF16)
    rest = values - high.astype(F32)
    middle = rest.astype(BF16)
    return [high, middle, (rest - middle.astype(F32)).astype(BF16)]


def remote(src, dst, ssem, rsem, device):
    return pltpu.make_async_remote_copy(
        src_ref=src, dst_ref=dst, send_sem=ssem, recv_sem=rsem, device_id=device, device_id_type=MESH
    )


def iota(shape, axis):
    return lax.broadcasted_iota(jnp.int32, shape, axis)


ORDER = (
    "bias0", "tw0", "E0", "bias1", "rela0", "bias2", "E1", "rela1", "E2", "bias3",
    "mod", "aux", "relb0", "E3", "rela2", "bias4", "proj0", "relb2", "rela3", "ts0",
    "relb1", "relb3", "attend0", "gw", "bias5", "bias6", "E4", "x1.0", "x1.3", "x1.1",
    "y1.0", "x1.2", "y1.3", "E5", "y1.1", "prep", "y1.2", "z1.0", "z1.1", "z1.2",
    "z1.3", "ffnA0", "bias7", "rela4", "proj1", "E6", "relb4", "x2.1", "x2.0", "x2.2",
    "x2.3", "rela5", "y2.1", "y2.0", "z2.1", "y2.2", "z2.2", "y2.3", "z2.3", "z2.0",
    "backA0", "P3", "P0", "E7", "P2", "Q3", "rela6", "relb5", "relb6", "R3",
    "Q0", "R0", "S3", "S0", "rela7", "ffnB0", "x3.1", "relb7", "attend1", "x3.0",
    "P1", "x3.3", "y3.1", "x3.2", "y3.0", "y3.3", "pw0", "y3.2", "Q2", "x1.4",
    "x1.5", "one0", "x1.6", "y1.4", "x1.7", "y1.5", "R2", "x4.0", "z1.4", "y1.6",
    "z1.6", "z1.5", "y1.7", "S2", "x4.3", "y4.0", "z1.7", "y4.3", "ffnA1", "ffnB1",
    "Q1", "R1", "wff", "x4.2", "x2.6", "x2.4", "S1", "x2.5", "y4.2", "z4.2",
    "x2.7", "y2.6", "pw1", "z3.3", "x4.1", "x3.6", "y2.4", "z3.1", "y2.5", "z2.6",
    "x3.7", "z2.4", "z2.5", "y2.7", "z2.7", "backA1", "z3.2", "one1", "P6", "P4",
    "y4.1", "P5", "watt", "x4.4", "x4.5", "x4.6", "Q4", "x3.4", "Q7", "Q5",
    "Q6", "y3.4", "y4.6", "R5", "pw2", "x3.5", "R4", "z4.0", "y3.7", "z4.1",
    "P7", "y4.4", "R6", "y3.6", "pw3", "z4.3", "R7", "z3.0", "y3.5", "fin0",
    "S4", "z3.7", "x4.7", "S5", "z4.6", "pw4", "pw5", "S6", "pw6", "S7",
    "z3.6", "pw7", "y4.5", "pwe", "y4.7", "z4.5", "z3.4", "z4.7", "z4.4", "z3.5",
    "fin1", "mg",
)


class Place:
    def __init__(self, ndp):
        self.ndp = ndp
        self.dp = dp = lax.axis_index("dp")
        self.t = t = lax.axis_index("tensor")
        self.near_t, self.skip_t, self.far_t = t + 1 - 2 * lax.rem(t, 2), lax.rem(t + 2, 4), 3 - t
        self.near, self.skip, self.far = (dp, self.near_t), (dp, self.skip_t), (dp, self.far_t)
        self.inner = (t == 1) | (t == 2)
        self.first = lax.rem(dp, 2) == 0
        self.twin = (dp + 1 - 2 * lax.rem(dp, 2), t)
        self.outer = (t == 0) | (t == 3)

    def peer(self, step):
        return lax.rem(self.dp + step, self.ndp)

    def greet(self):
        sem = pltpu.get_barrier_semaphore()
        for device in (self.near, self.skip, self.far):
            pl.semaphore_signal(sem, inc=1, device_id=device, device_id_type=MESH)

        @pl.loop(1, self.ndp)
        def _(step):
            pl.semaphore_signal(
                sem, inc=1, device_id=(self.peer(step), self.t), device_id_type=MESH
            )

    def meet(self):
        pl.semaphore_wait(pltpu.get_barrier_semaphore(), 3 + self.ndp - 1)


class Spread:
    def __init__(self, place, source, target, ssem, rsem):
        self.place, self.source, self.target, self.ssem, self.rsem = place, source, target, ssem, rsem

    def copy(self, step):
        there = self.place.peer(step)
        return remote(
            self.source(there),
            self.target.at[self.place.dp],
            self.ssem.at[step],
            self.rsem.at[self.place.dp],
            (there, self.place.t),
        )

    def arrival(self, step):
        there = self.place.peer(step)
        return remote(
            self.source(there),
            self.target.at[there],
            self.ssem.at[step],
            self.rsem.at[there],
            (there, self.place.t),
        )

    def own(self):
        here = self.place.dp
        return pltpu.make_async_copy(self.source(here), self.target.at[here], self.ssem.at[0])

    def start(self):
        self.own().start()

        @pl.loop(1, self.place.ndp)
        def _(step):
            self.copy(step).start()

    def wait(self):
        self.own().wait()

        @pl.loop(1, self.place.ndp)
        def _(step):
            self.copy(step).wait_send()
            self.arrival(step).wait_recv()


class LineSum:
    def __init__(self, place, part, in2, total, sems):
        self.place, self.part, self.in2, self.total, self.sems = place, part, in2, total, sems

    def copy(self, stage, i):
        src = (self.part, self.part, self.total)[stage].at[i]
        dst = (self.total, self.in2, self.total)[stage].at[i]
        device = (self.place.near, self.place.far, self.place.near)[stage]
        return remote(src, dst, self.sems.at[2 * stage, i], self.sems.at[2 * stage + 1, i], device)

    def start(self, i):
        @pl.when(self.place.outer)
        def _():
            self.copy(0, i).start()

    def cross(self, i):
        @pl.when(self.place.inner)
        def _():
            self.copy(0, i).wait_recv()
            self.part[i] = (self.part[i].astype(F32) + self.total[i].astype(F32)).astype(BF16)
            self.copy(1, i).start()

    def back(self, i):
        @pl.when(self.place.inner)
        def _():
            self.copy(1, i).wait_recv()
            self.total[i] = (self.part[i].astype(F32) + self.in2[i].astype(F32)).astype(BF16)
            self.copy(2, i).start()

    def finish(self, i):
        @pl.when(self.place.outer)
        def _():
            self.copy(2, i).wait_recv()

    def drain(self, i):
        @pl.when(self.place.outer)
        def _():
            self.copy(0, i).wait_send()

        @pl.when(self.place.inner)
        def _():
            self.copy(1, i).wait_send()
            self.copy(2, i).wait_send()

    def value(self, b):
        return self.total[b * PARTS : (b + 1) * PARTS].reshape(L, D).astype(F32)


def layer_kernel(
    nb, ndp,
    noise, labels, freq, table, pw, ada, act_in, cot_in, wq_in, wo_in, wgu_in, wd_in, pf,
    sg_o, out_o, in_o, wff_o, watt_o, mg_o, pw_o, aux_o,
    act, cot, wq, wo, wgu, wd, isem, raw, rsem, kw, mod, pbuf, psem,
    bsend, own, ring, inward, across, bsem,
    qs, ks, vs, probs, gate, att, normed_t,
    part1, in1, total1, sem1,
    part2, in2, total2, sem2,
    part3, in3, total3, sem3,
    part4, in4, total4, sem4,
    norm2_t, fgrad, fgrad_t, swish, hgrad, bgrad_t, gated_s, pgrad, mgrad_mid,
    sg, gsem, acc, wff, watt, mgs, pws, aux, out_s, in_s, osem, turn, xsem,
):
    place = Place(ndp)
    place.greet()
    nch = nb * NRC
    slots = pbuf.shape[0]
    rows_per = D // ndp

    def fetch(k, slot):
        b, r = k // NRC, k % NRC
        return pltpu.make_async_copy(pf.at[b, :, pl.ds(r * RC, RC), :], pbuf.at[slot], psem.at[slot])

    for k in range(slots):
        fetch(k, k).start()
    loads = [
        pltpu.make_async_copy(src, dst, isem.at[n])
        for n, (src, dst) in enumerate(
            ((act_in, act), (wq_in, wq), (wo_in, wo), (cot_in, cot), (wd_in, wd))
        )
    ]
    for load in loads:
        load.start()
    ready = set()

    def need(*numbers):
        for n in numbers:
            if n not in ready:
                ready.add(n)
                loads[n].wait()


    row, col = iota((192, 12), 0), iota((192, 12), 1)
    group, head = row // 48, lax.rem(row // 16, 3)
    owner = jnp.where(
        group == 0,
        place.far_t,
        jnp.where(group == 1, place.skip_t, jnp.where(group == 2, place.near_t, place.t)),
    )
    pick = (col == owner * 3 + head).astype(F32).astype(BF16)
    chosen = nn(pick, pw[...]).astype(BF16)
    channels = pw.shape[1]
    widen = (iota((channels, channels * 16), 1) // 16 == iota((channels, channels * 16), 0)).astype(F32)
    wide = nn(chosen, widen.astype(BF16))
    diagonal = lax.rem(iota(wide.shape, 0), 16) == lax.rem(iota(wide.shape, 1), 16)
    kw[...] = jnp.where(diagonal, wide, 0.0).astype(BF16)

    aux_spread = Spread(place, lambda j: aux.at[j], aux_o, xsem.at[0], xsem.at[1])

    def inwards(k):
        return remote(bsend.at[k], inward.at[k], bsem.at[0, k], bsem.at[1, k], place.near)

    def crossing(k):
        return remote(
            bsend.at[k, pl.ds(0, 2)], across.at[k], bsem.at[2, k], bsem.at[3, k], place.far
        )

    def outwards(k):
        return remote(bsend.at[k, 2], inward.at[k, 0], bsem.at[4, k], bsem.at[5, k], place.near)

    def bias(k):
        slot = k % slots
        fetch(k, slot).wait()
        for s in range(RC // 16):
            here = pl.ds(s * 16, 16)
            rows = pbuf[slot, :, here, :].reshape(-1, L)
            out = nn(kw[...], rows)
            three = out[:144].reshape(3, LH, 16, L)

            @pl.when(place.outer)
            def _():
                bsend[k, :, :, here, :] = three.astype(BF16)

            @pl.when(place.inner)
            def _():
                ring[k % RING, :, :, here, :] = three

            own[k, :, here, :] = out[144:].reshape(LH, 16, L)

        if k + slots < nch:
            fetch(k + slots, slot).start()
        if k == nch - 1:
            for n in range(slots):
                fetch(n, n).start()

    def send_bias(k):
        @pl.when(place.outer)
        def _():
            inwards(k).start()

    def pass_turn(_):
        @pl.when(place.outer & place.first)
        def _():
            inwards(NRC - 1).wait_send()
            pl.semaphore_signal(turn, inc=1, device_id=place.twin, device_id_type=MESH)

    def take_turn(_):
        @pl.when(place.outer & ~place.first)
        def _():
            pl.semaphore_wait(turn, 1)

    def relay(k):
        @pl.when(place.inner)
        def _():
            inwards(k).wait_recv()
            bsend[k, 0] = (ring[k % RING, 0] + inward[k, 1].astype(F32)).astype(BF16)
            bsend[k, 1] = (ring[k % RING, 1] + inward[k, 0].astype(F32)).astype(BF16)
            crossing(k).start()

    def relay_out(k):
        @pl.when(place.inner)
        def _():
            crossing(k).wait_recv()
            bsend[k, 2] = (ring[k % RING, 2] + across[k, 1].astype(F32)).astype(BF16)
            outwards(k).start()

    def modulate():
        def scoped(rows, sem):
            load = pltpu.make_async_copy(ada, rows, sem)
            load.start()
            width = DC // ndp
            conds, hots = [], []
            for b in range(nb):
                phase = (2.0 * math.pi * noise[b]) * freq[...]
                row = jnp.concatenate([jnp.cos(phase), jnp.sin(phase)], axis=1)
                for n in range(NCLASS):
                    row += table[n : n + 1, :].astype(F32) * (labels[b] == n).astype(F32)
                conds.append(row)
                hots.append((iota((1, width), 1) == labels[b]).astype(F32))
            cond = jnp.concatenate(conds, axis=0)
            sigmoid = jax.nn.sigmoid(cond)
            silu = cond * sigmoid
            factor = sigmoid * (1.0 + cond * (1.0 - sigmoid))
            hot = jnp.concatenate(hots, axis=0)
            for j in range(ndp):
                cols = slice(j * width, (j + 1) * width)
                aux[j] = jnp.concatenate([silu[:, cols], factor[:, cols], hot], axis=0)
            terms = jnp.concatenate(in_terms(silu), axis=0)
            load.wait()
            for n in range(6):
                out = nn(terms, rows[n])
                mod[:, n, :] = out[:nb] + out[nb : 2 * nb] + out[2 * nb : 3 * nb]

        pl.run_scoped(scoped, pltpu.VMEM(ada.shape, BF16), pltpu.SemaphoreType.DMA)

    def project(b):
        need(0, 1)
        unit, _ = normalize(act[pl.ds(b * L, L)].astype(F32))
        m = mod[b]
        low = (unit * (1.0 + m[0:1]) + m[1:2]).astype(BF16)
        normed_t[:, pl.ds(b * L, L)] = low.T
        for piece in range(2):
            out = nt(low, wq[pl.ds(piece * 384, 384), :])
            for n in range(6):
                which, h = piece * 2 + n // 3, n % 3
                column = out[:, n * HD : (n + 1) * HD]
                if which == 0:
                    qs[b, h] = (column.astype(BF16).astype(F32) * 0.125).astype(BF16)
                elif which == 1:
                    ks[b, h] = column.astype(BF16)
                elif which == 2:
                    vs[b, h] = column.astype(BF16)
            if piece == 1:
                gate[b] = jax.nn.sigmoid(out[:, LW:])

    sum1 = LineSum(place, part1, in1, total1, sem1)
    sum2 = LineSum(place, part2, in2, total2, sem2)
    sum3 = LineSum(place, part3, in3, total3, sem3)
    sum4 = LineSum(place, part4, in4, total4, sem4)

    def attend(b):
        need(2)
        for k in range(b * NRC, (b + 1) * NRC):

            @pl.when(place.outer)
            def _():
                outwards(k).wait_recv()

        heads = []
        for h in range(LH):
            here = slice(b * NRC, (b + 1) * NRC)
            from_near = jnp.where(place.inner, inward[here, 2, h], inward[here, 0, h]).astype(F32)
            from_far = jnp.where(place.inner, across[here, 0, h], jnp.zeros((), BF16)).astype(F32)
            bias_rows = (own[here, h] + (from_near + from_far)).reshape(L, L)
            scores = nt(qs[b, h], ks[b, h]) + bias_rows
            e = jnp.exp(scores - jnp.max(scores, axis=-1, keepdims=True))
            p = (e * (1.0 / jnp.sum(e, axis=-1, keepdims=True))).astype(BF16)
            probs[b, h] = p
            heads.append(nn(p, vs[b, h]))
        attended = jnp.concatenate(heads, axis=1)
        att[b] = attended
        gated = (attended * gate[b]).astype(BF16)
        gated_s[pl.ds(b * L, L)] = gated
        part1[b * PARTS : (b + 1) * PARTS] = nn(gated, wo[...]).astype(BF16).reshape(PARTS, PR, D)
        for i in range(b * PARTS, (b + 1) * PARTS):
            sum1.start(i)

    def raw_rows(n):
        return pltpu.make_async_copy(
            wgu_in.at[pl.ds(n * RAW, RAW)], raw.at[n % 2], rsem.at[n % 2]
        )

    def split_gate_up():
        for n in range(D // RAW):
            raw_rows(n).wait()
            for piece in range(2):
                wgu[pl.ds(n * RAW, RAW), pl.ds(piece * D, D)] = raw[n % 2, :, piece, :]
            if n + 2 < D // RAW:
                raw_rows(n + 2).start()

    def prepare():
        need(3)
        for b in range(nb):
            low = (cot[pl.ds(b * L, L)].astype(F32) * jax.nn.sigmoid(mod[b, 5:6])).astype(BF16)
            fgrad[pl.ds(b * L, L)] = low
            fgrad_t[:, pl.ds(b * L, L)] = low.T

    def middle_of(b):
        rows = act[pl.ds(b * L, L)].astype(F32)
        return rows + jax.nn.sigmoid(mod[b, 2:3]) * sum1.value(b)

    def feedforward(b):
        need(4)
        here = pl.ds(b * L, L)
        unit, _ = normalize(middle_of(b))
        low = (unit * (1.0 + mod[b, 3:4]) + mod[b, 4:5]).astype(BF16)
        norm2_t[:, here] = low.T
        for f in range(3):
            tile, tile_up = pl.ds(f * 256, 256), pl.ds(D + f * 256, 256)
            g = nn(low, wgu[:, tile])
            up = nn(low, wgu[:, tile_up])
            back = nt(fgrad[here], wd[tile, :])
            s = jax.nn.sigmoid(g)
            silu = g * s
            swish[here, tile] = (silu * up).astype(BF16)
            hgrad[here, tile_up] = (back * silu).astype(BF16)
            hgrad[here, tile] = (back * up * s * (1.0 + g * (1.0 - s))).astype(BF16)
        here_parts = pl.ds(b * PARTS, PARTS)
        for d in range(3):
            tile = pl.ds(d * 256, 256)
            part2[here_parts, :, tile] = (
                nt(hgrad[here, :], wgu[tile, :]).astype(BF16).reshape(PARTS, PR, 256)
            )
        for i in range(b * PARTS, (b + 1) * PARTS):
            sum2.start(i)

    def feedforward_out(b):
        here, here_parts = pl.ds(b * L, L), pl.ds(b * PARTS, PARTS)
        for d in range(3):
            tile = pl.ds(d * 256, 256)
            part3[here_parts, :, tile] = (
                nn(swish[here, :], wd[:, tile]).astype(BF16).reshape(PARTS, PR, 256)
            )
        for i in range(b * PARTS, (b + 1) * PARTS):
            sum3.start(i)

    def put_rows(target, tile, values):
        low = values.astype(BF16)
        for j in range(ndp):
            target[j, :, tile] = low[j * rows_per : (j + 1) * rows_per]

    wff_spread = Spread(place, lambda j: wff.at[j], wff_o, xsem.at[2], xsem.at[3])
    watt_spread = Spread(place, lambda j: watt.at[j], watt_o, xsem.at[4], xsem.at[5])

    def weights_ff():
        for f in range(6):
            tile = pl.ds(f * 256, 256)
            put_rows(wff, tile, nn(norm2_t[...], hgrad[:, tile]))
        for f in range(3):
            put_rows(wff, pl.ds(2 * D + f * 256, 256), nn(fgrad_t[...], swish[:, pl.ds(f * 256, 256)]))
        wff_spread.start()

    def weights_att():
        for f in range(3):
            tile = pl.ds(f * 256, 256)
            put_rows(watt, tile, nn(normed_t[...], pgrad[:, tile]))
        put_rows(watt, pl.ds(D, LW), nn(bgrad_t[...], gated_s[...]))
        watt_spread.start()

    def share(k, n):
        source, target, device = (
            (3, 2, place.near),
            (3, 0, place.far),
            (2, 1, place.far),
            (0, 1, place.near),
            (1, 0, place.near),
        )[n]
        return remote(
            sg.at[source, k], sg.at[target, k], gsem.at[2 * n, k], gsem.at[2 * n + 1, k], device
        )

    def share_near(k):
        share(k, 0).start()

    def share_far(k):
        @pl.when(place.inner)
        def _():
            share(k, 1).start()

    def pass_far(k):
        @pl.when(place.inner)
        def _():
            share(k, 0).wait_recv()
            share(k, 2).start()

    def pass_near(k):
        @pl.when(place.inner)
        def _():
            share(k, 1).wait_recv()
            share(k, 3).start()
            share(k, 2).wait_recv()
            share(k, 4).start()

    def attend_back(b):
        here = pl.ds(b * L, L)
        m = mod[b]
        gate_one = jax.nn.sigmoid(m[2:3])
        middle = middle_of(b)
        unit, inverse = normalize(middle)
        two = sum2.value(b)
        up = cot[here].astype(F32)
        mid_grad = up + norm_back(two * (1.0 + m[3:4]), unit, inverse)
        mgrad_mid[here] = mid_grad
        low = (mid_grad * gate_one).astype(BF16)
        bgrad_t[:, here] = low.T
        mgs[b, 2:3] = (
            jnp.sum(mid_grad * sum1.value(b), axis=0, keepdims=True) * gate_one * (1.0 - gate_one)
        )
        mgs[b, 3:4] = jnp.sum(two * unit, axis=0, keepdims=True)
        mgs[b, 4:5] = jnp.sum(two, axis=0, keepdims=True)
        gated_grad = nt(low, wo[...])
        opened = gate[b]
        att_grad = (gated_grad * opened).astype(BF16)
        attended = att[b]
        pgrad[here, pl.ds(3 * LW, LW)] = (gated_grad * attended * opened * (1.0 - opened)).astype(BF16)
        product = att_grad.astype(F32) * attended
        dq, dk, dv = [], [], []
        for h in range(LH):
            cols = slice(h * HD, (h + 1) * HD)
            head_grad = att_grad[:, cols]
            delta = jnp.sum(product[:, cols], axis=-1, keepdims=True)
            p = probs[b, h]
            score_grad = (p.astype(F32) * (nt(head_grad, vs[b, h]) - delta)).astype(BF16)
            for r in range(NRC):
                sg[3, b * NRC + r, h] = score_grad[r * RC : (r + 1) * RC]
            dq.append(nn(score_grad, ks[b, h]) * 0.125)
            dk.append(tn(score_grad, qs[b, h]))
            dv.append(tn(p, head_grad))
        pgrad[here, pl.ds(0, 3 * LW)] = jnp.concatenate(dq + dk + dv, axis=1).astype(BF16)

    def project_back(b):
        here, here_parts = pl.ds(b * L, L), pl.ds(b * PARTS, PARTS)
        for d in range(3):
            tile = pl.ds(d * 256, 256)
            part4[here_parts, :, tile] = (
                nn(pgrad[here, :], wq[:, tile]).astype(BF16).reshape(PARTS, PR, 256)
            )
        for i in range(b * PARTS, (b + 1) * PARTS):
            sum4.start(i)

    def pair_weight(k):
        slot = k % slots

        @pl.when(place.outer)
        def _():
            share(k, 0).wait_recv()
            share(k, 3).wait_recv()
            share(k, 4).wait_recv()

        fetch(k, slot).wait()
        total = None
        for s in range(RC // 16):
            rows = pbuf[slot, :, pl.ds(s * 16, 16), :].reshape(-1, L)
            grads = sg[:, k, :, pl.ds(s * 16, 16), :].reshape(-1, L)
            out = nt(rows, grads)
            total = out if total is None else total + out
        if k == 0:
            acc[...] = total
        else:
            acc[...] += total
        store_sg(k).start()
        if k + slots < nch:
            fetch(k + slots, slot).start()

    def pair_weight_end():
        values = acc[...].reshape(channels, 16, 192)
        mask = iota((16, 192), 0) == lax.rem(iota((16, 192), 1), 16)
        picked = jnp.sum(jnp.where(mask[None], values, 0.0), axis=1)
        row, col = iota((16, 192), 0), iota((16, 192), 1)
        group, head = col // 48, lax.rem(col // 16, 3)
        owner = jnp.where(
            group == 0,
            place.far_t,
            jnp.where(group == 1, place.skip_t, jnp.where(group == 2, place.near_t, place.t)),
        )
        pws[...] = nt((row == owner * 3 + head).astype(F32), picked, precision=highest)

    def store_sg(k):
        return pltpu.make_async_copy(sg.at[:, k], sg_o.at[:, k], osem.at[0, k])

    def store_rows(b, n):
        source, target = ((out_s, out_o), (in_s, in_o))[n]
        here = pl.ds(b * L, L)
        return pltpu.make_async_copy(source.at[here], target.at[here], osem.at[1 + n, b])

    def finish_rows(b):
        here = pl.ds(b * L, L)
        m = mod[b]
        gate_two = jax.nn.sigmoid(m[5:6])
        ffn = sum3.value(b)
        out_s[here] = (middle_of(b) + gate_two * ffn).astype(BF16)
        mgs[b, 5:6] = (
            jnp.sum(cot[here].astype(F32) * ffn, axis=0, keepdims=True) * gate_two * (1.0 - gate_two)
        )
        unit, inverse = normalize(act[here].astype(F32))
        one = sum4.value(b)
        mgs[b, 0:1] = jnp.sum(one * unit, axis=0, keepdims=True)
        mgs[b, 1:2] = jnp.sum(one, axis=0, keepdims=True)
        in_s[here] = (mgrad_mid[here] + norm_back(one * (1.0 + m[0:1]), unit, inverse)).astype(BF16)
        for n in range(2):
            store_rows(b, n).start()

    mg_spread = Spread(place, lambda j: mgs, mg_o, xsem.at[6], xsem.at[7])
    pw_spread = Spread(place, lambda j: pws, pw_o, xsem.at[8], xsem.at[9])

    steps = {
        "bias": bias,
        "E": send_bias,
        "ts": pass_turn,
        "tw": take_turn,
        "aux": aux_spread.start,
        "rela": relay,
        "relb": relay_out,
        "mod": modulate,
        "proj": project,
        "prep": prepare,
        "gw": split_gate_up,
        "attend": attend,
        "ffnA": feedforward,
        "ffnB": feedforward_out,
        "backA": attend_back,
        "one": project_back,
        "P": share_near,
        "Q": share_far,
        "R": pass_far,
        "S": pass_near,
        "pw": pair_weight,
        "wff": weights_ff,
        "watt": weights_att,
        "fin": finish_rows,
        "mg": mg_spread.start,
        "pwe": pair_weight_end,
    }
    for n, total in enumerate((sum1, sum2, sum3, sum4)):
        steps[f"x{n + 1}."] = total.cross
        steps[f"y{n + 1}."] = total.back
        steps[f"z{n + 1}."] = total.finish
    for entry in ORDER:
        if entry == "end":
            break
        name = entry.rstrip("0123456789")
        number = entry[len(name) :]
        steps[name](*([int(number)] if number else []))
        if entry == "bias0":
            place.meet()
            for n in range(2):
                raw_rows(n).start()
    done = set(ORDER)
    if "pwe" in done:
        pw_spread.start()

    for k in range(nch):
        if f"E{k}" in done:

            @pl.when(place.outer & ~place.first if k == NRC - 1 and "ts0" in done else place.outer)
            def _():
                inwards(k).wait_send()

        if f"rela{k}" in done:

            @pl.when(place.inner)
            def _():
                crossing(k).wait_send()

        if f"relb{k}" in done:

            @pl.when(place.inner)
            def _():
                outwards(k).wait_send()

        if f"P{k}" in done:
            share(k, 0).wait_send()

        for n, name in ((1, "Q"), (2, "R"), (3, "S"), (4, "S")):
            if f"{name}{k}" in done:

                @pl.when(place.inner)
                def _():
                    share(k, n).wait_send()

    for a, (total, source) in enumerate(
        ((sum1, "attend"), (sum2, "ffnA"), (sum3, "ffnB"), (sum4, "one"))
    ):
        for i in range(PARTS * nb):
            if f"{source}{i // PARTS}" in done:

                @pl.when(place.outer)
                def _():
                    total.copy(0, i).wait_send()

            if f"x{a + 1}.{i}" in done:

                @pl.when(place.inner)
                def _():
                    total.copy(1, i).wait_send()

            if f"y{a + 1}.{i}" in done:

                @pl.when(place.inner)
                def _():
                    total.copy(2, i).wait_send()

    for spread, name in (
        (aux_spread, "aux"), (wff_spread, "wff"), (watt_spread, "watt"), (mg_spread, "mg"), (pw_spread, "pwe"),
    ):
        if name in done:
            spread.wait()
    for k in range(nch):
        if f"pw{k}" in done:
            store_sg(k).wait()
    for b in range(nb):
        if f"fin{b}" in done:
            for n in range(2):
                store_rows(b, n).wait()


def vmem_specs(n):
    return [pl.BlockSpec(memory_space=pltpu.VMEM)] * n


def any_specs(n):
    return [pl.BlockSpec(memory_space=pl.ANY)] * n


def layer_call(nb, ndp, noise, labels, freq, table, pw, ada, act, cot, wq, wo, wgu, wd, pf):
    nch = nb * NRC
    rows = nb * L
    rows_per = D // ndp
    channels = pf.shape[1]
    hidden = wd.shape[0]
    shapes = [
        ((4, nch, LH, RC, L), BF16),
        ((rows, D), BF16),
        ((rows, D), BF16),
        ((ndp, rows_per, 3 * hidden), BF16),
        ((ndp, rows_per, 5 * LW), BF16),
        ((ndp, nb, 6, D), F32),
        ((ndp, 16, channels), F32),
        ((ndp, 3 * nb, DC // ndp), F32),
    ]
    dma = pltpu.SemaphoreType.DMA

    def line():
        return [pltpu.VMEM((PARTS * nb, PR, D), BF16)] * 3 + [dma((6, PARTS * nb))]

    scratch = [
        pltpu.VMEM((rows, D), BF16),
        pltpu.VMEM((rows, D), BF16),
        pltpu.VMEM(wq.shape, BF16),
        pltpu.VMEM(wo.shape, BF16),
        pltpu.VMEM((D, 2 * hidden), BF16),
        pltpu.VMEM(wd.shape, BF16),
        dma((5,)),
        pltpu.VMEM((2, RAW, 2, hidden), BF16),
        dma((2,)),
        pltpu.VMEM((192, channels * 16), BF16),
        pltpu.VMEM((nb, 6, D), F32),
        pltpu.VMEM((3, channels, RC, L), BF16),
        dma((3,)),
        pltpu.VMEM((nch, 3, LH, RC, L), BF16),
        pltpu.VMEM((nch, LH, RC, L), F32),
        pltpu.VMEM((RING, 3, LH, RC, L), F32),
        pltpu.VMEM((nch, 3, LH, RC, L), BF16),
        pltpu.VMEM((nch, 2, LH, RC, L), BF16),
        dma((6, nch)),
        pltpu.VMEM((nb, LH, L, HD), BF16),
        pltpu.VMEM((nb, LH, L, HD), BF16),
        pltpu.VMEM((nb, LH, L, HD), BF16),
        pltpu.VMEM((nb, LH, L, L), BF16),
        pltpu.VMEM((nb, L, LW), F32),
        pltpu.VMEM((nb, L, LW), F32),
        pltpu.VMEM((D, rows), BF16),
        *line(),
        *line(),
        *line(),
        *line(),
        pltpu.VMEM((D, rows), BF16),
        pltpu.VMEM((rows, D), BF16),
        pltpu.VMEM((D, rows), BF16),
        pltpu.VMEM((rows, hidden), BF16),
        pltpu.VMEM((rows, 2 * hidden), BF16),
        pltpu.VMEM((D, rows), BF16),
        pltpu.VMEM((rows, LW), BF16),
        pltpu.VMEM((rows, 4 * LW), BF16),
        pltpu.VMEM((rows, D), F32),
        pltpu.VMEM((4, nch, LH, RC, L), BF16),
        dma((10, nch)),
        pltpu.VMEM((channels * 16, 192), F32),
        pltpu.VMEM((ndp, rows_per, 3 * hidden), BF16),
        pltpu.VMEM((ndp, rows_per, 5 * LW), BF16),
        pltpu.VMEM((nb, 6, D), F32),
        pltpu.VMEM((16, channels), F32),
        pltpu.VMEM((ndp, 3 * nb, DC // ndp), F32),
        pltpu.VMEM((rows, D), BF16),
        pltpu.VMEM((rows, D), BF16),
        dma((3, nch)),
        pltpu.SemaphoreType.REGULAR,
        dma((10, ndp)),
    ]
    return pl.pallas_call(
        functools.partial(layer_kernel, nb, ndp),
        out_shape=[jax.ShapeDtypeStruct(*s) for s in shapes],
        in_specs=[pl.BlockSpec(memory_space=pltpu.SMEM)] * 2 + vmem_specs(3) + any_specs(8),
        out_specs=any_specs(8),
        scratch_shapes=scratch,
        compiler_params=pltpu.CompilerParams(
            collective_id=0, has_side_effects=True, vmem_limit_bytes=VMEM_LIMIT
        ),
        name="layer",
    )(noise, labels, freq, table, pw, ada, act, cot, wq, wo, wgu, wd, pf)


def ending_kernel(
    nb, ndp,
    pw, mg, aux, pwi, sg_i, ada_i, out_i, in_i, wff_i, watt_i,
    pg, out_o, in_o, ada_o, class_o, wgu_o, wd_o, wq_o, wo_o, pw_o,
    sg, ada, rows, wff, watt, obuf, osem, gsem, isem,
):
    t = lax.axis_index("tensor")
    nch = nb * NRC
    hidden = wd_o.shape[1]
    slots = obuf.shape[0]

    def load(k):
        return pltpu.make_async_copy(sg_i.at[:, k], sg.at[:, k], gsem.at[k])

    others = [
        pltpu.make_async_copy(src, dst, isem.at[n])
        for n, (src, dst) in enumerate(
            (
                (wff_i, wff),
                (watt_i, watt),
                (out_i, rows.at[0]),
                (in_i, rows.at[1]),
                (ada_i, ada),
            )
        )
    ]
    for k in range(nch):
        load(k).start()
        if k == 1:
            for copy in others:
                copy.start()
    passed = [
        pltpu.make_async_copy(rows.at[n], target, isem.at[5 + n])
        for n, target in enumerate((out_o, in_o))
    ]
    channels = pw.shape[1]
    row, col = iota((12, 192), 0), iota((12, 192), 1)
    group, head = col // 48, lax.rem(col // 16, 3)
    near_t, skip_t, far_t = t + 1 - 2 * lax.rem(t, 2), lax.rem(t + 2, 4), 3 - t
    owner = jnp.where(
        group == 0, far_t, jnp.where(group == 1, skip_t, jnp.where(group == 2, near_t, t))
    )
    pick = (row == owner * 3 + head).astype(F32).astype(BF16)
    chosen = tn(pw[...], pick).astype(BF16)
    widen = (iota((channels * 16, channels), 0) // 16 == iota((channels * 16, channels), 1)).astype(F32)
    wide = nn(widen.astype(BF16), chosen)
    diagonal = lax.rem(iota(wide.shape, 0), 16) == lax.rem(iota(wide.shape, 1), 16)
    spread = jnp.where(diagonal, wide, 0.0).astype(BF16)

    def store(k):
        b, r = k // NRC, k % NRC
        return pltpu.make_async_copy(
            obuf.at[k % slots], pg.at[b, :, pl.ds(r * RC, RC), :], osem.at[k % slots]
        )

    def pair_grad(k):
        if k >= slots:
            store(k - slots).wait()
        load(k).wait()
        for s in range(RC // 16):
            grads = sg[:, k, :, pl.ds(s * 16, 16), :].reshape(-1, L)
            obuf[k % slots, :, pl.ds(s * 16, 16), :] = (
                nn(spread, grads).reshape(channels, 16, L).astype(BF16)
            )
        store(k).start()

    def add(source, tile):
        total = source[0, :, tile].astype(F32)
        for j in range(1, ndp):
            total += source[j, :, tile].astype(F32)
        return total

    def ff_sums():
        others[0].wait()
        total = add(wff, pl.ds(0, 3 * hidden))
        wgu_o[:, 0, :] = total[:, :hidden]
        wgu_o[:, 1, :] = total[:, hidden : 2 * hidden]
        wd_o[...] = total[:, 2 * hidden :]

    def att_sums():
        others[1].wait()
        total = add(watt, pl.ds(0, 5 * LW))
        for n in range(4):
            wq_o[:, n, :] = total[:, n * LW : (n + 1) * LW]
        wo_o[...] = total[:, 4 * LW :].T
        total = pwi[0]
        for j in range(1, ndp):
            total += pwi[j]
        pw_o[...] = total[: pw_o.shape[0]]

    def pass_rows():
        for n in range(2):
            others[2 + n].wait()
            passed[n].start()

    def condition():
        def each(kind):
            return jnp.concatenate([aux[j, kind * nb : (kind + 1) * nb] for j in range(ndp)], axis=0)

        others[4].wait()
        silu, factor, hot = each(0), each(1), each(2)
        width = silu.shape[1]
        total = None
        for m in range(6):
            grads = mg[:, m, :]
            ada_o[m] = tn(silu, grads, precision=highest)
            part = nt(jnp.concatenate(in_terms(grads), axis=0), ada[m])
            total = part if total is None else total + part
        rows = total.shape[0] // 3
        back = total[:rows] + total[rows : 2 * rows] + total[2 * rows :]
        here = lax.axis_index("dp") * width
        mine = (iota((DC, width), 0) == here + iota((DC, width), 1)).astype(F32)
        back = nn(back, mine, precision=highest)
        class_o[...] = tn(hot, back * factor, precision=highest)[:NCLASS]

    after = {0: pass_rows, 1: ff_sums, 2: att_sums, 3: condition}
    for k in range(nch):
        pair_grad(k)
        if k in after:
            after[k]()
    for k in range(max(nch - slots, 0), nch):
        store(k).wait()
    for copy in passed:
        copy.wait()


def ending_call(nb, ndp, pw, mg, aux, pwi, sg, ada, out, inputs_grad, wff, watt, pair_shape):
    rows_per = D // ndp
    hidden = wff.shape[2] // 3
    width = DC // ndp
    channels = pair_shape[1]
    dma = pltpu.SemaphoreType.DMA
    shapes = [
        (pair_shape, BF16),
        (out.shape, BF16),
        (out.shape, BF16),
        ((6, width, D), F32),
        ((NCLASS, width), F32),
        ((rows_per, 2, hidden), F32),
        ((rows_per, hidden), F32),
        ((rows_per, 4, LW), F32),
        ((LW, rows_per), F32),
        ((12, channels), F32),
    ]
    return pl.pallas_call(
        functools.partial(ending_kernel, nb, ndp),
        out_shape=[jax.ShapeDtypeStruct(*s) for s in shapes],
        in_specs=vmem_specs(4) + any_specs(6),
        out_specs=any_specs(3) + vmem_specs(7),
        scratch_shapes=[
            pltpu.VMEM(sg.shape, BF16),
            pltpu.VMEM(ada.shape, BF16),
            pltpu.VMEM((2, *out.shape), BF16),
            pltpu.VMEM(wff.shape, BF16),
            pltpu.VMEM(watt.shape, BF16),
            pltpu.VMEM((3, channels, RC, L), BF16),
            dma((3,)),
            dma((nb * NRC,)),
            dma((7,)),
        ],
        compiler_params=pltpu.CompilerParams(vmem_limit_bytes=VMEM_LIMIT),
        name="ending",
    )(pw, mg, aux, pwi, sg, ada, out, inputs_grad, wff, watt)


def shards(
    ndp,
    activations,
    noise_times,
    cath_labels,
    class_table,
    ada_weight,
    qkvg_weight,
    out_weight,
    pair_weight,
    gateup_weight,
    down_weight,
    pair_features,
    cotangent,
):
    chains = pair_features.shape[0]
    freq = jnp.asarray(np.exp(np.arange(DC // 2) * (math.log(1000.0) / (DC // 2)))[None], F32)
    ada = jnp.transpose(ada_weight, (1, 0, 2))
    wq = jnp.transpose(qkvg_weight, (1, 2, 0)).reshape(-1, D)
    pw = pair_weight.T
    sg, out, inputs_grad, wff, watt, mg, pwi, aux = layer_call(
        chains, ndp, noise_times, cath_labels, freq, class_table, pw, ada, activations, cotangent,
        wq, out_weight, gateup_weight, down_weight, pair_features,
    )
    pair_grad, out, inputs_grad, ada_sum, class_sum, gateup, down, qkvg, outw, pair_sum = ending_call(
        chains, ndp, pw, mg.reshape(-1, 6, D), aux, pwi, sg, ada, out, inputs_grad, wff, watt,
        pair_features.shape,
    )
    return (
        out,
        inputs_grad,
        pair_grad,
        class_sum,
        jnp.transpose(ada_sum, (1, 0, 2)),
        qkvg,
        outw,
        pair_sum.T,
        gateup,
        down.T,
    )


def solution(mesh):
    placed = (
        P("dp", None),
        P("dp"),
        P("dp"),
        P(),
        P(),
        P(None, None, "tensor"),
        P("tensor", None),
        P("tensor", None),
        P(None, None, "tensor"),
        P("tensor", None),
        P("dp", "tensor", None, None),
        P("dp", None),
    )
    return jax.shard_map(
        functools.partial(shards, mesh.shape["dp"]),
        mesh=mesh,
        in_specs=placed,
        out_specs=(
            P("dp", None),
            P("dp", None),
            P("dp", "tensor", None, None),
            P(None, "dp"),
            P("dp", None, None),
            P("dp", None, "tensor"),
            P("tensor", "dp"),
            P("tensor", None),
            P("dp", None, "tensor"),
            P("tensor", "dp"),
        ),
        check_vma=False,
    )
```

```python
import functools
import math

import jax
import jax.numpy as jnp
import numpy as np
from jax import lax
from jax.experimental import pallas as pl
from jax.experimental.pallas import tpu as pltpu
from jax.sharding import PartitionSpec as P

D = 768
HD = 64
DC = 256
NCLASS = 4
L = 256
RC = 64
NRC = L // RC
LH = 3
LW = LH * HD
PARTS = 4
PR = L // PARTS
RING = 4
RAW = 96
MESH = pl.DeviceIdType.MESH
F32 = jnp.float32
BF16 = jnp.bfloat16
VMEM_LIMIT = 63 * 2**20

highest = lax.Precision.HIGHEST


def normalize(values):
    centred = values - jnp.mean(values, axis=-1, keepdims=True)
    inverse = lax.rsqrt(jnp.mean(centred * centred, axis=-1, keepdims=True) + 1e-05)
    return (centred * inverse, inverse)


def norm_back(grad_unit, unit_rows, inverse):
    mean_grad = jnp.mean(grad_unit, axis=-1, keepdims=True)
    mean_proj = jnp.mean(grad_unit * unit_rows, axis=-1, keepdims=True)
    return inverse * (grad_unit - mean_grad - unit_rows * mean_proj)


def nn(a, b, precision=None):
    return lax.dot_general(
        a, b, (((1,), (0,)), ((), ())), preferred_element_type=F32, precision=precision
    )


def nt(a, b, precision=None):
    return lax.dot_general(
        a, b, (((1,), (1,)), ((), ())), preferred_element_type=F32, precision=precision
    )


def tn(a, b, precision=None):
    return lax.dot_general(
        a, b, (((0,), (0,)), ((), ())), preferred_element_type=F32, precision=precision
    )


def in_terms(values):
    high = values.astype(BF16)
    rest = values - high.astype(F32)
    middle = rest.astype(BF16)
    return [high, middle, (rest - middle.astype(F32)).astype(BF16)]


def remote(src, dst, ssem, rsem, device):
    return pltpu.make_async_remote_copy(
        src_ref=src, dst_ref=dst, send_sem=ssem, recv_sem=rsem, device_id=device, device_id_type=MESH
    )


def iota(shape, axis):
    return lax.broadcasted_iota(jnp.int32, shape, axis)


(
    BIAS, SEND, SEND_NEAR, RELAY, RELAY_OUT, PASS_TURN,
    TAKE_TURN, MODULATE, AUX, PROJECT, PREPARE, SPLIT,
    ATTEND, FEED, FEED_OUT, ATTEND_BACK, PROJECT_BACK, SHARE_NEAR,
    SHARE_FAR, PASS_FAR, PASS_NEAR, PAIR, PAIR_END, WEIGHTS_FF,
    WEIGHTS_ATT, FINISH, GRADS,
) = range(27)
CROSS1, CROSS2, CROSS3, CROSS4 = range(27, 31)
BACK1, BACK2, BACK3, BACK4 = range(31, 35)
DONE1, DONE2, DONE3, DONE4 = range(35, 39)
ORDER = (
    (BIAS, 0), (TAKE_TURN, 0), (SEND, 0), (BIAS, 1), (SEND, 1), (RELAY, 0),
    (BIAS, 2), (SEND, 2), (BIAS, 3), (SEND, 3), (SEND_NEAR, 1), (SEND_NEAR, 3),
    (SEND_NEAR, 0), (RELAY, 1), (PASS_TURN, 0), (RELAY, 2), (RELAY, 3), (MODULATE, 0),
    (AUX, 0), (PROJECT, 1), (RELAY_OUT, 0), (RELAY_OUT, 2), (BIAS, 4), (PREPARE, 0),
    (SEND_NEAR, 2), (RELAY_OUT, 3), (RELAY_OUT, 1), (PROJECT, 0), (SPLIT, 0), (ATTEND, 0),
    (BIAS, 5), (CROSS1, 0), (CROSS1, 2), (CROSS1, 1), (SEND, 4), (CROSS1, 3),
    (BACK1, 0), (RELAY, 4), (BACK1, 1), (SEND, 5), (BACK1, 2), (RELAY, 5),
    (DONE1, 0), (BACK1, 3), (DONE1, 2), (BIAS, 6), (DONE1, 1), (DONE1, 3),
    (RELAY_OUT, 4), (RELAY_OUT, 5), (FEED, 0), (CROSS2, 0), (SEND, 6), (BIAS, 7),
    (CROSS2, 2), (SEND, 7), (SEND_NEAR, 4), (CROSS2, 3), (CROSS2, 1), (BACK2, 0),
    (RELAY, 6), (BACK2, 2), (DONE2, 0), (BACK2, 3), (RELAY, 7), (DONE2, 2),
    (BACK2, 1), (DONE2, 1), (DONE2, 3), (ATTEND_BACK, 0), (SHARE_NEAR, 0), (SHARE_FAR, 1),
    (SHARE_FAR, 2), (SHARE_NEAR, 1), (SEND_NEAR, 6), (SEND_NEAR, 5), (SHARE_NEAR, 3), (SHARE_NEAR, 2),
    (RELAY_OUT, 6), (RELAY_OUT, 7), (PASS_FAR, 0), (PASS_FAR, 1), (SHARE_FAR, 3), (SHARE_FAR, 0),
    (PASS_NEAR, 1), (PASS_FAR, 2), (SEND_NEAR, 7), (PASS_FAR, 3), (ATTEND, 1), (CROSS1, 4),
    (PASS_NEAR, 0), (PASS_NEAR, 2), (CROSS1, 6), (CROSS1, 5), (CROSS1, 7), (FEED_OUT, 0),
    (PASS_NEAR, 3), (BACK1, 4), (CROSS3, 1), (BACK1, 6), (BACK1, 5), (CROSS3, 0),
    (DONE1, 5), (PAIR, 0), (BACK1, 7), (CROSS3, 3), (BACK3, 1), (DONE1, 6),
    (CROSS3, 2), (DONE1, 4), (DONE1, 7), (BACK3, 3), (BACK3, 0), (FEED, 1),
    (PROJECT_BACK, 0), (CROSS2, 4), (PAIR, 1), (FEED_OUT, 1), (CROSS2, 7), (CROSS2, 5),
    (CROSS2, 6), (BACK2, 4), (WEIGHTS_FF, 0), (CROSS4, 1), (BACK2, 7), (CROSS4, 2),
    (PAIR, 2), (CROSS4, 3), (BACK2, 6), (CROSS4, 0), (CROSS3, 5), (BACK3, 2),
    (BACK4, 2), (CROSS3, 4), (BACK4, 3), (DONE3, 0), (DONE2, 6), (DONE2, 7),
    (BACK4, 1), (BACK2, 5), (DONE2, 5), (BACK4, 0), (CROSS3, 7), (DONE2, 4),
    (ATTEND_BACK, 1), (PAIR, 3), (PROJECT_BACK, 1), (BACK3, 5), (DONE3, 1), (DONE3, 5),
    (BACK3, 4), (WEIGHTS_ATT, 0), (SHARE_NEAR, 6), (SHARE_NEAR, 5), (SHARE_NEAR, 4), (CROSS4, 5),
    (SHARE_FAR, 4), (DONE4, 0), (CROSS4, 6), (DONE4, 3), (DONE3, 3), (DONE3, 4),
    (PASS_FAR, 6), (PASS_FAR, 4), (SHARE_FAR, 5), (PASS_FAR, 5), (CROSS4, 7), (SHARE_FAR, 6),
    (DONE4, 1), (CROSS3, 6), (PASS_NEAR, 5), (SHARE_NEAR, 7), (PASS_NEAR, 4), (DONE3, 2),
    (DONE4, 2), (SHARE_FAR, 7), (BACK3, 7), (PAIR, 4), (PAIR, 5), (PASS_FAR, 7),
    (BACK4, 6), (CROSS4, 4), (PASS_NEAR, 6), (BACK3, 6), (FINISH, 0), (PAIR, 6),
    (DONE3, 7), (BACK4, 5), (PASS_NEAR, 7), (DONE4, 6), (PAIR, 7), (DONE4, 5),
    (DONE3, 6), (PAIR_END, 0), (BACK4, 4), (BACK4, 7), (DONE4, 4), (DONE4, 7),
    (FINISH, 1), (GRADS, 0),
)


class Place:
    def __init__(self, ndp):
        self.ndp = ndp
        self.dp = dp = lax.axis_index("dp")
        self.t = t = lax.axis_index("tensor")
        self.near_t, self.skip_t, self.far_t = t + 1 - 2 * lax.rem(t, 2), lax.rem(t + 2, 4), 3 - t
        self.near, self.skip, self.far = (dp, self.near_t), (dp, self.skip_t), (dp, self.far_t)
        self.inner = (t == 1) | (t == 2)
        self.first = lax.rem(dp, 2) == 0
        self.twin = (dp + 1 - 2 * lax.rem(dp, 2), t)
        self.outer = (t == 0) | (t == 3)

    def peer(self, step):
        return lax.rem(self.dp + step, self.ndp)

    def greet(self):
        sem = pltpu.get_barrier_semaphore()
        for device in (self.near, self.skip, self.far):
            pl.semaphore_signal(sem, inc=1, device_id=device, device_id_type=MESH)

        @pl.loop(1, self.ndp)
        def _(step):
            pl.semaphore_signal(
                sem, inc=1, device_id=(self.peer(step), self.t), device_id_type=MESH
            )

    def meet(self):
        pl.semaphore_wait(pltpu.get_barrier_semaphore(), 3 + self.ndp - 1)


class Spread:
    def __init__(self, place, source, target, ssem, rsem):
        self.place, self.source, self.target, self.ssem, self.rsem = place, source, target, ssem, rsem

    def copy(self, step):
        there = self.place.peer(step)
        return remote(
            self.source(there),
            self.target.at[self.place.dp],
            self.ssem.at[step],
            self.rsem.at[self.place.dp],
            (there, self.place.t),
        )

    def arrival(self, step):
        there = self.place.peer(step)
        return remote(
            self.source(there),
            self.target.at[there],
            self.ssem.at[step],
            self.rsem.at[there],
            (there, self.place.t),
        )

    def own(self):
        here = self.place.dp
        return pltpu.make_async_copy(self.source(here), self.target.at[here], self.ssem.at[0])

    def start(self):
        self.own().start()

        @pl.loop(1, self.place.ndp)
        def _(step):
            self.copy(step).start()

    def wait(self):
        self.own().wait()

        @pl.loop(1, self.place.ndp)
        def _(step):
            self.copy(step).wait_send()
            self.arrival(step).wait_recv()


class LineSum:
    def __init__(self, place, part, in2, total, sems):
        self.place, self.part, self.in2, self.total, self.sems = place, part, in2, total, sems

    def copy(self, stage, i):
        src = (self.part, self.part, self.total)[stage].at[i]
        dst = (self.total, self.in2, self.total)[stage].at[i]
        device = (self.place.near, self.place.far, self.place.near)[stage]
        return remote(src, dst, self.sems.at[2 * stage, i], self.sems.at[2 * stage + 1, i], device)

    def start(self, i):
        @pl.when(self.place.outer)
        def _():
            self.copy(0, i).start()

    def cross(self, i):
        @pl.when(self.place.inner)
        def _():
            self.copy(0, i).wait_recv()
            self.part[i] = (self.part[i].astype(F32) + self.total[i].astype(F32)).astype(BF16)
            self.copy(1, i).start()

    def back(self, i):
        @pl.when(self.place.inner)
        def _():
            self.copy(1, i).wait_recv()
            self.total[i] = (self.part[i].astype(F32) + self.in2[i].astype(F32)).astype(BF16)
            self.copy(2, i).start()

    def finish(self, i):
        @pl.when(self.place.outer)
        def _():
            self.copy(2, i).wait_recv()

    def drain(self, i):
        @pl.when(self.place.outer)
        def _():
            self.copy(0, i).wait_send()

        @pl.when(self.place.inner)
        def _():
            self.copy(1, i).wait_send()
            self.copy(2, i).wait_send()

    def value(self, b):
        return self.total[b * PARTS : (b + 1) * PARTS].reshape(L, D).astype(F32)


def layer_kernel(
    nb, ndp,
    noise, labels, freq, table, pw, ada, act_in, cot_in, wq_in, wo_in, wgu_in, wd_in, pf,
    sg_o, out_o, in_o, wff_o, watt_o, mg_o, pw_o, aux_o,
    act, cot, wq, wo, wgu, wd, isem, raw, rsem, kw, mod, pbuf, psem,
    bsend, own, ring, inward, across, bsem,
    qs, ks, vs, probs, gate, att, normed_t,
    part1, in1, total1, sem1,
    part2, in2, total2, sem2,
    part3, in3, total3, sem3,
    part4, in4, total4, sem4,
    norm2_t, fgrad, fgrad_t, swish, hgrad, bgrad_t, gated_s, pgrad, mgrad_mid,
    sg, gsem, acc, wff, watt, mgs, pws, aux, out_s, in_s, osem, turn, xsem,
):
    place = Place(ndp)
    place.greet()
    nch = nb * NRC
    slots = pbuf.shape[0]
    rows_per = D // ndp

    def fetch(k, slot):
        b, r = k // NRC, k % NRC
        return pltpu.make_async_copy(pf.at[b, :, pl.ds(r * RC, RC), :], pbuf.at[slot], psem.at[slot])

    fetch(0, 0).start()
    loads = [
        pltpu.make_async_copy(src, dst, isem.at[n])
        for n, (src, dst) in enumerate(
            ((act_in, act), (wq_in, wq), (wo_in, wo), (cot_in, cot), (wd_in, wd))
        )
    ]
    ready = set()

    def need(*numbers):
        for n in numbers:
            if n not in ready:
                ready.add(n)
                loads[n].wait()


    row, col = iota((192, 12), 0), iota((192, 12), 1)
    group, head = row // 48, lax.rem(row // 16, 3)
    owner = jnp.where(
        group == 0,
        place.far_t,
        jnp.where(group == 1, place.skip_t, jnp.where(group == 2, place.near_t, place.t)),
    )
    pick = (col == owner * 3 + head).astype(F32).astype(BF16)
    chosen = nn(pick, pw[...]).astype(BF16)
    channels = pw.shape[1]
    widen = (iota((channels, channels * 16), 1) // 16 == iota((channels, channels * 16), 0)).astype(F32)
    wide = nn(chosen, widen.astype(BF16))
    diagonal = lax.rem(iota(wide.shape, 0), 16) == lax.rem(iota(wide.shape, 1), 16)
    kw[...] = jnp.where(diagonal, wide, 0.0).astype(BF16)

    aux_spread = Spread(place, lambda j: aux.at[j], aux_o, xsem.at[0], xsem.at[1])

    def inwards(k):
        two = pl.ds(0, 2)
        return remote(bsend.at[k, two], inward.at[k, two], bsem.at[0, k], bsem.at[1, k], place.near)

    def to_near(k):
        return remote(bsend.at[k, 2], inward.at[k, 2], bsem.at[6, k], bsem.at[7, k], place.near)

    def crossing(k):
        return remote(
            bsend.at[k, pl.ds(0, 2)], across.at[k], bsem.at[2, k], bsem.at[3, k], place.far
        )

    def outwards(k):
        return remote(bsend.at[k, 2], inward.at[k, 0], bsem.at[4, k], bsem.at[5, k], place.near)

    def bias(k):
        slot = k % slots
        fetch(k, slot).wait()
        if k == 0:
            for n in range(1, slots):
                fetch(n, n).start()
            for load in loads:
                load.start()
        for s in range(RC // 16):
            here = pl.ds(s * 16, 16)
            rows = pbuf[slot, :, here, :].reshape(-1, L)
            out = nn(kw[...], rows)
            three = out[:144].reshape(3, LH, 16, L)

            @pl.when(place.outer)
            def _():
                bsend[k, :, :, here, :] = three.astype(BF16)

            @pl.when(place.inner)
            def _():
                ring[k % RING, :, :, here, :] = three

            own[k, :, here, :] = out[144:].reshape(LH, 16, L)

        if k + slots < nch:
            fetch(k + slots, slot).start()
        if k == nch - 1:
            for n in range(slots):
                fetch(n, n).start()

    def send_bias(k):
        @pl.when(place.outer)
        def _():
            inwards(k).start()

    def send_near(k):
        @pl.when(place.outer)
        def _():
            to_near(k).start()

    def pass_turn(_):
        @pl.when(place.outer & place.first)
        def _():
            inwards(NRC - 1).wait_send()
            pl.semaphore_signal(turn, inc=1, device_id=place.twin, device_id_type=MESH)

    def take_turn(_):
        @pl.when(place.outer & ~place.first)
        def _():
            pl.semaphore_wait(turn, 1)

    def relay(k):
        @pl.when(place.inner)
        def _():
            inwards(k).wait_recv()
            bsend[k, 0] = (ring[k % RING, 0] + inward[k, 1].astype(F32)).astype(BF16)
            bsend[k, 1] = (ring[k % RING, 1] + inward[k, 0].astype(F32)).astype(BF16)
            crossing(k).start()

    def relay_out(k):
        @pl.when(place.inner)
        def _():
            crossing(k).wait_recv()
            bsend[k, 2] = (ring[k % RING, 2] + across[k, 1].astype(F32)).astype(BF16)
            outwards(k).start()

    def modulate():
        def scoped(rows, sem):
            load = pltpu.make_async_copy(ada, rows, sem)
            load.start()
            width = DC // ndp
            conds, hots = [], []
            for b in range(nb):
                phase = (2.0 * math.pi * noise[b]) * freq[...]
                row = jnp.concatenate([jnp.cos(phase), jnp.sin(phase)], axis=1)
                for n in range(NCLASS):
                    row += table[n : n + 1, :].astype(F32) * (labels[b] == n).astype(F32)
                conds.append(row)
                hots.append((iota((1, width), 1) == labels[b]).astype(F32))
            cond = jnp.concatenate(conds, axis=0)
            sigmoid = jax.nn.sigmoid(cond)
            silu = cond * sigmoid
            factor = sigmoid * (1.0 + cond * (1.0 - sigmoid))
            hot = jnp.concatenate(hots, axis=0)
            for j in range(ndp):
                cols = slice(j * width, (j + 1) * width)
                aux[j] = jnp.concatenate([silu[:, cols], factor[:, cols], hot], axis=0)
            terms = jnp.concatenate(in_terms(silu), axis=0)
            load.wait()
            for n in range(6):
                out = nn(terms, rows[n])
                mod[:, n, :] = out[:nb] + out[nb : 2 * nb] + out[2 * nb : 3 * nb]

        pl.run_scoped(scoped, pltpu.VMEM(ada.shape, BF16), pltpu.SemaphoreType.DMA)

    def project(b):
        need(0, 1)
        unit, _ = normalize(act[pl.ds(b * L, L)].astype(F32))
        m = mod[b]
        low = (unit * (1.0 + m[0:1]) + m[1:2]).astype(BF16)
        normed_t[:, pl.ds(b * L, L)] = low.T
        for piece in range(2):
            out = nt(low, wq[pl.ds(piece * 384, 384), :])
            for n in range(6):
                which, h = piece * 2 + n // 3, n % 3
                column = out[:, n * HD : (n + 1) * HD]
                if which == 0:
                    qs[b, h] = (column.astype(BF16).astype(F32) * 0.125).astype(BF16)
                elif which == 1:
                    ks[b, h] = column.astype(BF16)
                elif which == 2:
                    vs[b, h] = column.astype(BF16)
            if piece == 1:
                gate[b] = jax.nn.sigmoid(out[:, LW:])

    sum1 = LineSum(place, part1, in1, total1, sem1)
    sum2 = LineSum(place, part2, in2, total2, sem2)
    sum3 = LineSum(place, part3, in3, total3, sem3)
    sum4 = LineSum(place, part4, in4, total4, sem4)

    def attend(b):
        need(2)
        for k in range(b * NRC, (b + 1) * NRC):

            @pl.when(place.outer)
            def _():
                outwards(k).wait_recv()

            @pl.when(place.inner)
            def _():
                to_near(k).wait_recv()

        heads = []
        for h in range(LH):
            here = slice(b * NRC, (b + 1) * NRC)
            from_near = jnp.where(place.inner, inward[here, 2, h], inward[here, 0, h]).astype(F32)
            from_far = jnp.where(place.inner, across[here, 0, h], jnp.zeros((), BF16)).astype(F32)
            bias_rows = (own[here, h] + (from_near + from_far)).reshape(L, L)
            scores = nt(qs[b, h], ks[b, h]) + bias_rows
            e = jnp.exp(scores - jnp.max(scores, axis=-1, keepdims=True))
            p = (e * (1.0 / jnp.sum(e, axis=-1, keepdims=True))).astype(BF16)
            probs[b, h] = p
            heads.append(nn(p, vs[b, h]))
        attended = jnp.concatenate(heads, axis=1)
        att[b] = attended
        gated = (attended * gate[b]).astype(BF16)
        gated_s[pl.ds(b * L, L)] = gated
        part1[b * PARTS : (b + 1) * PARTS] = nn(gated, wo[...]).astype(BF16).reshape(PARTS, PR, D)
        for i in range(b * PARTS, (b + 1) * PARTS):
            sum1.start(i)

    def raw_rows(n):
        return pltpu.make_async_copy(
            wgu_in.at[pl.ds(n * RAW, RAW)], raw.at[n % 2], rsem.at[n % 2]
        )

    def split_gate_up():
        for n in range(D // RAW):
            raw_rows(n).wait()
            for piece in range(2):
                wgu[pl.ds(n * RAW, RAW), pl.ds(piece * D, D)] = raw[n % 2, :, piece, :]
            if n + 2 < D // RAW:
                raw_rows(n + 2).start()

    def prepare():
        need(3)
        for b in range(nb):
            low = (cot[pl.ds(b * L, L)].astype(F32) * jax.nn.sigmoid(mod[b, 5:6])).astype(BF16)
            fgrad[pl.ds(b * L, L)] = low
            fgrad_t[:, pl.ds(b * L, L)] = low.T

    def middle_of(b):
        rows = act[pl.ds(b * L, L)].astype(F32)
        return rows + jax.nn.sigmoid(mod[b, 2:3]) * sum1.value(b)

    def feedforward(b):
        need(4)
        here = pl.ds(b * L, L)
        unit, _ = normalize(middle_of(b))
        low = (unit * (1.0 + mod[b, 3:4]) + mod[b, 4:5]).astype(BF16)
        norm2_t[:, here] = low.T
        for f in range(3):
            tile, tile_up = pl.ds(f * 256, 256), pl.ds(D + f * 256, 256)
            g = nn(low, wgu[:, tile])
            up = nn(low, wgu[:, tile_up])
            back = nt(fgrad[here], wd[tile, :])
            s = jax.nn.sigmoid(g)
            silu = g * s
            swish[here, tile] = (silu * up).astype(BF16)
            hgrad[here, tile_up] = (back * silu).astype(BF16)
            hgrad[here, tile] = (back * up * s * (1.0 + g * (1.0 - s))).astype(BF16)
        here_parts = pl.ds(b * PARTS, PARTS)
        for d in range(3):
            tile = pl.ds(d * 256, 256)
            part2[here_parts, :, tile] = (
                nt(hgrad[here, :], wgu[tile, :]).astype(BF16).reshape(PARTS, PR, 256)
            )
        for i in range(b * PARTS, (b + 1) * PARTS):
            sum2.start(i)

    def feedforward_out(b):
        here, here_parts = pl.ds(b * L, L), pl.ds(b * PARTS, PARTS)
        for d in range(3):
            tile = pl.ds(d * 256, 256)
            part3[here_parts, :, tile] = (
                nn(swish[here, :], wd[:, tile]).astype(BF16).reshape(PARTS, PR, 256)
            )
        for i in range(b * PARTS, (b + 1) * PARTS):
            sum3.start(i)

    def put_rows(target, tile, values):
        low = values.astype(BF16)
        for j in range(ndp):
            target[j, :, tile] = low[j * rows_per : (j + 1) * rows_per]

    wff_spread = Spread(place, lambda j: wff.at[j], wff_o, xsem.at[2], xsem.at[3])
    watt_spread = Spread(place, lambda j: watt.at[j], watt_o, xsem.at[4], xsem.at[5])

    def weights_ff():
        for f in range(6):
            tile = pl.ds(f * 256, 256)
            put_rows(wff, tile, nn(norm2_t[...], hgrad[:, tile]))
        for f in range(3):
            put_rows(wff, pl.ds(2 * D + f * 256, 256), nn(fgrad_t[...], swish[:, pl.ds(f * 256, 256)]))
        wff_spread.start()

    def weights_att():
        for f in range(3):
            tile = pl.ds(f * 256, 256)
            put_rows(watt, tile, nn(normed_t[...], pgrad[:, tile]))
        put_rows(watt, pl.ds(D, LW), nn(bgrad_t[...], gated_s[...]))
        watt_spread.start()

    def share(k, n):
        source, target, device = (
            (3, 2, place.near),
            (3, 0, place.far),
            (2, 1, place.far),
            (0, 1, place.near),
            (1, 0, place.near),
        )[n]
        return remote(
            sg.at[source, k], sg.at[target, k], gsem.at[2 * n, k], gsem.at[2 * n + 1, k], device
        )

    def share_near(k):
        share(k, 0).start()

    def share_far(k):
        @pl.when(place.inner)
        def _():
            share(k, 1).start()

    def pass_far(k):
        @pl.when(place.inner)
        def _():
            share(k, 0).wait_recv()
            share(k, 2).start()

    def pass_near(k):
        @pl.when(place.inner)
        def _():
            share(k, 1).wait_recv()
            share(k, 3).start()
            share(k, 2).wait_recv()
            share(k, 4).start()

    def attend_back(b):
        here = pl.ds(b * L, L)
        m = mod[b]
        gate_one = jax.nn.sigmoid(m[2:3])
        middle = middle_of(b)
        unit, inverse = normalize(middle)
        two = sum2.value(b)
        up = cot[here].astype(F32)
        mid_grad = up + norm_back(two * (1.0 + m[3:4]), unit, inverse)
        mgrad_mid[here] = mid_grad
        low = (mid_grad * gate_one).astype(BF16)
        bgrad_t[:, here] = low.T
        mgs[b, 2:3] = (
            jnp.sum(mid_grad * sum1.value(b), axis=0, keepdims=True) * gate_one * (1.0 - gate_one)
        )
        mgs[b, 3:4] = jnp.sum(two * unit, axis=0, keepdims=True)
        mgs[b, 4:5] = jnp.sum(two, axis=0, keepdims=True)
        gated_grad = nt(low, wo[...])
        opened = gate[b]
        att_grad = (gated_grad * opened).astype(BF16)
        attended = att[b]
        pgrad[here, pl.ds(3 * LW, LW)] = (gated_grad * attended * opened * (1.0 - opened)).astype(BF16)
        product = att_grad.astype(F32) * attended
        dq, dk, dv = [], [], []
        for h in range(LH):
            cols = slice(h * HD, (h + 1) * HD)
            head_grad = att_grad[:, cols]
            delta = jnp.sum(product[:, cols], axis=-1, keepdims=True)
            p = probs[b, h]
            score_grad = (p.astype(F32) * (nt(head_grad, vs[b, h]) - delta)).astype(BF16)
            for r in range(NRC):
                sg[3, b * NRC + r, h] = score_grad[r * RC : (r + 1) * RC]
            dq.append(nn(score_grad, ks[b, h]) * 0.125)
            dk.append(tn(score_grad, qs[b, h]))
            dv.append(tn(p, head_grad))
        pgrad[here, pl.ds(0, 3 * LW)] = jnp.concatenate(dq + dk + dv, axis=1).astype(BF16)

    def project_back(b):
        here, here_parts = pl.ds(b * L, L), pl.ds(b * PARTS, PARTS)
        for d in range(3):
            tile = pl.ds(d * 256, 256)
            part4[here_parts, :, tile] = (
                nn(pgrad[here, :], wq[:, tile]).astype(BF16).reshape(PARTS, PR, 256)
            )
        for i in range(b * PARTS, (b + 1) * PARTS):
            sum4.start(i)

    def pair_weight(k):
        slot = k % slots

        @pl.when(place.outer)
        def _():
            share(k, 0).wait_recv()
            share(k, 3).wait_recv()
            share(k, 4).wait_recv()

        fetch(k, slot).wait()
        total = None
        for s in range(RC // 16):
            rows = pbuf[slot, :, pl.ds(s * 16, 16), :].reshape(-1, L)
            grads = sg[:, k, :, pl.ds(s * 16, 16), :].reshape(-1, L)
            out = nt(rows, grads)
            total = out if total is None else total + out
        if k == 0:
            acc[...] = total
        else:
            acc[...] += total
        store_sg(k).start()
        if k + slots < nch:
            fetch(k + slots, slot).start()

    def pair_weight_end():
        values = acc[...].reshape(channels, 16, 192)
        mask = iota((16, 192), 0) == lax.rem(iota((16, 192), 1), 16)
        picked = jnp.sum(jnp.where(mask[None], values, 0.0), axis=1)
        row, col = iota((16, 192), 0), iota((16, 192), 1)
        group, head = col // 48, lax.rem(col // 16, 3)
        owner = jnp.where(
            group == 0,
            place.far_t,
            jnp.where(group == 1, place.skip_t, jnp.where(group == 2, place.near_t, place.t)),
        )
        pws[...] = nt((row == owner * 3 + head).astype(F32), picked, precision=highest)
        pw_spread.start()

    def store_sg(k):
        return pltpu.make_async_copy(sg.at[:, k], sg_o.at[:, k], osem.at[0, k])

    def store_rows(b, n):
        source, target = ((out_s, out_o), (in_s, in_o))[n]
        here = pl.ds(b * L, L)
        return pltpu.make_async_copy(source.at[here], target.at[here], osem.at[1 + n, b])

    def finish_rows(b):
        here = pl.ds(b * L, L)
        m = mod[b]
        gate_two = jax.nn.sigmoid(m[5:6])
        ffn = sum3.value(b)
        out_s[here] = (middle_of(b) + gate_two * ffn).astype(BF16)
        mgs[b, 5:6] = (
            jnp.sum(cot[here].astype(F32) * ffn, axis=0, keepdims=True) * gate_two * (1.0 - gate_two)
        )
        unit, inverse = normalize(act[here].astype(F32))
        one = sum4.value(b)
        mgs[b, 0:1] = jnp.sum(one * unit, axis=0, keepdims=True)
        mgs[b, 1:2] = jnp.sum(one, axis=0, keepdims=True)
        in_s[here] = (mgrad_mid[here] + norm_back(one * (1.0 + m[0:1]), unit, inverse)).astype(BF16)
        for n in range(2):
            store_rows(b, n).start()

    mg_spread = Spread(place, lambda j: mgs, mg_o, xsem.at[6], xsem.at[7])
    pw_spread = Spread(place, lambda j: pws, pw_o, xsem.at[8], xsem.at[9])

    sums = (sum1, sum2, sum3, sum4)
    steps = (
        bias,
        send_bias,
        send_near,
        relay,
        relay_out,
        pass_turn,
        take_turn,
        lambda _: modulate(),
        lambda _: aux_spread.start(),
        project,
        lambda _: prepare(),
        lambda _: split_gate_up(),
        attend,
        feedforward,
        feedforward_out,
        attend_back,
        project_back,
        share_near,
        share_far,
        pass_far,
        pass_near,
        pair_weight,
        lambda _: pair_weight_end(),
        lambda _: weights_ff(),
        lambda _: weights_att(),
        finish_rows,
        lambda _: mg_spread.start(),
        *(total.cross for total in sums),
        *(total.back for total in sums),
        *(total.finish for total in sums),
    )
    for kind, number in ORDER:
        steps[kind](number)
        if (kind, number) == (BIAS, 0):
            place.meet()
            for n in range(2):
                raw_rows(n).start()

    for k in range(nch):

        @pl.when(place.outer & ~place.first if k == NRC - 1 else place.outer)
        def _():
            inwards(k).wait_send()

        @pl.when(place.outer)
        def _():
            to_near(k).wait_send()

        @pl.when(place.inner)
        def _():
            crossing(k).wait_send()
            outwards(k).wait_send()
            for n in range(1, 5):
                share(k, n).wait_send()

        share(k, 0).wait_send()
    for total in sums:
        for i in range(PARTS * nb):
            total.drain(i)
    for spread in (aux_spread, wff_spread, watt_spread, mg_spread, pw_spread):
        spread.wait()
    for k in range(nch):
        store_sg(k).wait()
    for b in range(nb):
        for n in range(2):
            store_rows(b, n).wait()


def vmem_specs(n):
    return [pl.BlockSpec(memory_space=pltpu.VMEM)] * n


def any_specs(n):
    return [pl.BlockSpec(memory_space=pl.ANY)] * n


def layer_call(nb, ndp, noise, labels, freq, table, pw, ada, act, cot, wq, wo, wgu, wd, pf):
    nch = nb * NRC
    rows = nb * L
    rows_per = D // ndp
    channels = pf.shape[1]
    hidden = wd.shape[0]
    shapes = [
        ((4, nch, LH, RC, L), BF16),
        ((rows, D), BF16),
        ((rows, D), BF16),
        ((ndp, rows_per, 3 * hidden), BF16),
        ((ndp, rows_per, 5 * LW), BF16),
        ((ndp, nb, 6, D), F32),
        ((ndp, 16, channels), F32),
        ((ndp, 3 * nb, DC // ndp), F32),
    ]
    dma = pltpu.SemaphoreType.DMA

    def line():
        return [pltpu.VMEM((PARTS * nb, PR, D), BF16)] * 3 + [dma((6, PARTS * nb))]

    scratch = [
        pltpu.VMEM((rows, D), BF16),
        pltpu.VMEM((rows, D), BF16),
        pltpu.VMEM(wq.shape, BF16),
        pltpu.VMEM(wo.shape, BF16),
        pltpu.VMEM((D, 2 * hidden), BF16),
        pltpu.VMEM(wd.shape, BF16),
        dma((5,)),
        pltpu.VMEM((2, RAW, 2, hidden), BF16),
        dma((2,)),
        pltpu.VMEM((192, channels * 16), BF16),
        pltpu.VMEM((nb, 6, D), F32),
        pltpu.VMEM((3, channels, RC, L), BF16),
        dma((3,)),
        pltpu.VMEM((nch, 3, LH, RC, L), BF16),
        pltpu.VMEM((nch, LH, RC, L), F32),
        pltpu.VMEM((RING, 3, LH, RC, L), F32),
        pltpu.VMEM((nch, 3, LH, RC, L), BF16),
        pltpu.VMEM((nch, 2, LH, RC, L), BF16),
        dma((8, nch)),
        pltpu.VMEM((nb, LH, L, HD), BF16),
        pltpu.VMEM((nb, LH, L, HD), BF16),
        pltpu.VMEM((nb, LH, L, HD), BF16),
        pltpu.VMEM((nb, LH, L, L), BF16),
        pltpu.VMEM((nb, L, LW), F32),
        pltpu.VMEM((nb, L, LW), F32),
        pltpu.VMEM((D, rows), BF16),
        *line(),
        *line(),
        *line(),
        *line(),
        pltpu.VMEM((D, rows), BF16),
        pltpu.VMEM((rows, D), BF16),
        pltpu.VMEM((D, rows), BF16),
        pltpu.VMEM((rows, hidden), BF16),
        pltpu.VMEM((rows, 2 * hidden), BF16),
        pltpu.VMEM((D, rows), BF16),
        pltpu.VMEM((rows, LW), BF16),
        pltpu.VMEM((rows, 4 * LW), BF16),
        pltpu.VMEM((rows, D), F32),
        pltpu.VMEM((4, nch, LH, RC, L), BF16),
        dma((10, nch)),
        pltpu.VMEM((channels * 16, 192), F32),
        pltpu.VMEM((ndp, rows_per, 3 * hidden), BF16),
        pltpu.VMEM((ndp, rows_per, 5 * LW), BF16),
        pltpu.VMEM((nb, 6, D), F32),
        pltpu.VMEM((16, channels), F32),
        pltpu.VMEM((ndp, 3 * nb, DC // ndp), F32),
        pltpu.VMEM((rows, D), BF16),
        pltpu.VMEM((rows, D), BF16),
        dma((3, nch)),
        pltpu.SemaphoreType.REGULAR,
        dma((10, ndp)),
    ]
    return pl.pallas_call(
        functools.partial(layer_kernel, nb, ndp),
        out_shape=[jax.ShapeDtypeStruct(*s) for s in shapes],
        in_specs=[pl.BlockSpec(memory_space=pltpu.SMEM)] * 2 + vmem_specs(3) + any_specs(8),
        out_specs=any_specs(8),
        scratch_shapes=scratch,
        compiler_params=pltpu.CompilerParams(
            collective_id=0, has_side_effects=True, vmem_limit_bytes=VMEM_LIMIT
        ),
        name="layer",
    )(noise, labels, freq, table, pw, ada, act, cot, wq, wo, wgu, wd, pf)


def ending_kernel(
    nb, ndp,
    pw, mg, aux, pwi, sg_i, ada_i, out_i, in_i, wff_i, watt_i,
    pg, out_o, in_o, ada_o, class_o, wgu_o, wd_o, wq_o, wo_o, pw_o,
    sg, ada, rows, wff, watt, obuf, osem, gsem, isem,
):
    t = lax.axis_index("tensor")
    nch = nb * NRC
    hidden = wd_o.shape[1]
    slots = obuf.shape[0]

    def load(k):
        return pltpu.make_async_copy(sg_i.at[:, k], sg.at[:, k], gsem.at[k])

    others = [
        pltpu.make_async_copy(src, dst, isem.at[n])
        for n, (src, dst) in enumerate(
            (
                (wff_i, wff),
                (watt_i, watt),
                (out_i, rows.at[0]),
                (in_i, rows.at[1]),
                (ada_i, ada),
            )
        )
    ]
    for k in range(nch):
        load(k).start()
        if k == 1:
            for copy in others:
                copy.start()
    passed = [
        pltpu.make_async_copy(rows.at[n], target, isem.at[5 + n])
        for n, target in enumerate((out_o, in_o))
    ]
    channels = pw.shape[1]
    row, col = iota((12, 192), 0), iota((12, 192), 1)
    group, head = col // 48, lax.rem(col // 16, 3)
    near_t, skip_t, far_t = t + 1 - 2 * lax.rem(t, 2), lax.rem(t + 2, 4), 3 - t
    owner = jnp.where(
        group == 0, far_t, jnp.where(group == 1, skip_t, jnp.where(group == 2, near_t, t))
    )
    pick = (row == owner * 3 + head).astype(F32).astype(BF16)
    chosen = tn(pw[...], pick).astype(BF16)
    widen = (iota((channels * 16, channels), 0) // 16 == iota((channels * 16, channels), 1)).astype(F32)
    wide = nn(widen.astype(BF16), chosen)
    diagonal = lax.rem(iota(wide.shape, 0), 16) == lax.rem(iota(wide.shape, 1), 16)
    spread = jnp.where(diagonal, wide, 0.0).astype(BF16)

    def store(k):
        b, r = k // NRC, k % NRC
        return pltpu.make_async_copy(
            obuf.at[k % slots], pg.at[b, :, pl.ds(r * RC, RC), :], osem.at[k % slots]
        )

    def pair_grad(k):
        if k >= slots:
            store(k - slots).wait()
        load(k).wait()
        for s in range(RC // 16):
            grads = sg[:, k, :, pl.ds(s * 16, 16), :].reshape(-1, L)
            obuf[k % slots, :, pl.ds(s * 16, 16), :] = (
                nn(spread, grads).reshape(channels, 16, L).astype(BF16)
            )
        store(k).start()

    def add(source, tile):
        total = source[0, :, tile].astype(F32)
        for j in range(1, ndp):
            total += source[j, :, tile].astype(F32)
        return total

    def ff_sums():
        others[0].wait()
        total = add(wff, pl.ds(0, 3 * hidden))
        wgu_o[:, 0, :] = total[:, :hidden]
        wgu_o[:, 1, :] = total[:, hidden : 2 * hidden]
        wd_o[...] = total[:, 2 * hidden :]

    def att_sums():
        others[1].wait()
        total = add(watt, pl.ds(0, 5 * LW))
        for n in range(4):
            wq_o[:, n, :] = total[:, n * LW : (n + 1) * LW]
        wo_o[...] = total[:, 4 * LW :].T
        total = pwi[0]
        for j in range(1, ndp):
            total += pwi[j]
        pw_o[...] = total[: pw_o.shape[0]]

    def pass_rows():
        for n in range(2):
            others[2 + n].wait()
            passed[n].start()

    def condition():
        def each(kind):
            return jnp.concatenate([aux[j, kind * nb : (kind + 1) * nb] for j in range(ndp)], axis=0)

        others[4].wait()
        silu, factor, hot = each(0), each(1), each(2)
        width = silu.shape[1]
        total = None
        for m in range(6):
            grads = mg[:, m, :]
            ada_o[m] = tn(silu, grads, precision=highest)
            part = nt(jnp.concatenate(in_terms(grads), axis=0), ada[m])
            total = part if total is None else total + part
        rows = total.shape[0] // 3
        back = total[:rows] + total[rows : 2 * rows] + total[2 * rows :]
        here = lax.axis_index("dp") * width
        mine = (iota((DC, width), 0) == here + iota((DC, width), 1)).astype(F32)
        back = nn(back, mine, precision=highest)
        class_o[...] = tn(hot, back * factor, precision=highest)[:NCLASS]

    after = {0: pass_rows, 1: ff_sums, 2: att_sums, 3: condition}
    for k in range(nch):
        pair_grad(k)
        if k in after:
            after[k]()
    for k in range(max(nch - slots, 0), nch):
        store(k).wait()
    for copy in passed:
        copy.wait()


def ending_call(nb, ndp, pw, mg, aux, pwi, sg, ada, out, inputs_grad, wff, watt, pair_shape):
    rows_per = D // ndp
    hidden = wff.shape[2] // 3
    width = DC // ndp
    channels = pair_shape[1]
    dma = pltpu.SemaphoreType.DMA
    shapes = [
        (pair_shape, BF16),
        (out.shape, BF16),
        (out.shape, BF16),
        ((6, width, D), F32),
        ((NCLASS, width), F32),
        ((rows_per, 2, hidden), F32),
        ((rows_per, hidden), F32),
        ((rows_per, 4, LW), F32),
        ((LW, rows_per), F32),
        ((12, channels), F32),
    ]
    return pl.pallas_call(
        functools.partial(ending_kernel, nb, ndp),
        out_shape=[jax.ShapeDtypeStruct(*s) for s in shapes],
        in_specs=vmem_specs(4) + any_specs(6),
        out_specs=any_specs(3) + vmem_specs(7),
        scratch_shapes=[
            pltpu.VMEM(sg.shape, BF16),
            pltpu.VMEM(ada.shape, BF16),
            pltpu.VMEM((2, *out.shape), BF16),
            pltpu.VMEM(wff.shape, BF16),
            pltpu.VMEM(watt.shape, BF16),
            pltpu.VMEM((3, channels, RC, L), BF16),
            dma((3,)),
            dma((nb * NRC,)),
            dma((7,)),
        ],
        compiler_params=pltpu.CompilerParams(vmem_limit_bytes=VMEM_LIMIT),
        name="ending",
    )(pw, mg, aux, pwi, sg, ada, out, inputs_grad, wff, watt)


def shards(
    ndp,
    activations,
    noise_times,
    cath_labels,
    class_table,
    ada_weight,
    qkvg_weight,
    out_weight,
    pair_weight,
    gateup_weight,
    down_weight,
    pair_features,
    cotangent,
):
    chains = pair_features.shape[0]
    freq = jnp.asarray(np.exp(np.arange(DC // 2) * (math.log(1000.0) / (DC // 2)))[None], F32)
    ada = jnp.transpose(ada_weight, (1, 0, 2))
    wq = jnp.transpose(qkvg_weight, (1, 2, 0)).reshape(-1, D)
    pw = pair_weight.T
    sg, out, inputs_grad, wff, watt, mg, pwi, aux = layer_call(
        chains, ndp, noise_times, cath_labels, freq, class_table, pw, ada, activations, cotangent,
        wq, out_weight, gateup_weight, down_weight, pair_features,
    )
    pair_grad, out, inputs_grad, ada_sum, class_sum, gateup, down, qkvg, outw, pair_sum = ending_call(
        chains, ndp, pw, mg.reshape(-1, 6, D), aux, pwi, sg, ada, out, inputs_grad, wff, watt,
        pair_features.shape,
    )
    return (
        out,
        inputs_grad,
        pair_grad,
        class_sum,
        jnp.transpose(ada_sum, (1, 0, 2)),
        qkvg,
        outw,
        pair_sum.T,
        gateup,
        down.T,
    )


def solution(mesh):
    placed = (
        P("dp", None),
        P("dp"),
        P("dp"),
        P(),
        P(),
        P(None, None, "tensor"),
        P("tensor", None),
        P("tensor", None),
        P(None, None, "tensor"),
        P("tensor", None),
        P("dp", "tensor", None, None),
        P("dp", None),
    )
    return jax.shard_map(
        functools.partial(shards, mesh.shape["dp"]),
        mesh=mesh,
        in_specs=placed,
        out_specs=(
            P("dp", None),
            P("dp", None),
            P("dp", "tensor", None, None),
            P(None, "dp"),
            P("dp", None, None),
            P("dp", None, "tensor"),
            P("tensor", "dp"),
            P("tensor", None),
            P("dp", None, "tensor"),
            P("tensor", "dp"),
        ),
        check_vma=False,
    )
```

```python
import functools
import math

import jax
import jax.numpy as jnp
import numpy as np
from jax import lax
from jax.experimental import pallas as pl
from jax.experimental.pallas import tpu as pltpu
from jax.sharding import PartitionSpec as P

D = 768
HD = 64
DC = 256
NCLASS = 4
L = 256
RC = 64
NRC = L // RC
LH = 3
LW = LH * HD
PARTS = 4
PR = L // PARTS
RING = 4
RAW = 96
MESH = pl.DeviceIdType.MESH
F32 = jnp.float32
BF16 = jnp.bfloat16
VMEM_LIMIT = 63 * 2**20

highest = lax.Precision.HIGHEST


def normalize(values):
    centred = values - jnp.mean(values, axis=-1, keepdims=True)
    inverse = lax.rsqrt(jnp.mean(centred * centred, axis=-1, keepdims=True) + 1e-05)
    return (centred * inverse, inverse)


def norm_back(grad_unit, unit_rows, inverse):
    mean_grad = jnp.mean(grad_unit, axis=-1, keepdims=True)
    mean_proj = jnp.mean(grad_unit * unit_rows, axis=-1, keepdims=True)
    return inverse * (grad_unit - mean_grad - unit_rows * mean_proj)


def nn(a, b, precision=None):
    return lax.dot_general(
        a, b, (((1,), (0,)), ((), ())), preferred_element_type=F32, precision=precision
    )


def nt(a, b, precision=None):
    return lax.dot_general(
        a, b, (((1,), (1,)), ((), ())), preferred_element_type=F32, precision=precision
    )


def tn(a, b, precision=None):
    return lax.dot_general(
        a, b, (((0,), (0,)), ((), ())), preferred_element_type=F32, precision=precision
    )


def in_terms(values):
    high = values.astype(BF16)
    rest = values - high.astype(F32)
    middle = rest.astype(BF16)
    return [high, middle, (rest - middle.astype(F32)).astype(BF16)]


def remote(src, dst, ssem, rsem, device):
    return pltpu.make_async_remote_copy(
        src_ref=src, dst_ref=dst, send_sem=ssem, recv_sem=rsem, device_id=device, device_id_type=MESH
    )


def iota(shape, axis):
    return lax.broadcasted_iota(jnp.int32, shape, axis)


(
    BIAS, SEND, SEND_NEAR, RELAY, RELAY_OUT, PASS_TURN,
    TAKE_TURN, MODULATE, AUX, PROJECT, PREPARE, SPLIT,
    ATTEND, FEED, FEED_OUT, ATTEND_BACK, PROJECT_BACK, SHARE_NEAR,
    SHARE_FAR, PASS_FAR, PASS_NEAR, PAIR, PAIR_END, WEIGHTS_FF,
    WEIGHTS_ATT, FINISH, GRADS,
) = range(27)
CROSS1, CROSS2, CROSS3, CROSS4 = range(27, 31)
BACK1, BACK2, BACK3, BACK4 = range(31, 35)
DONE1, DONE2, DONE3, DONE4 = range(35, 39)
ORDER = (
    (BIAS, 0), (TAKE_TURN, 0), (SEND, 0), (BIAS, 1), (SEND, 1), (RELAY, 0),
    (BIAS, 2), (SEND, 2), (BIAS, 3), (SEND, 3), (SEND_NEAR, 1), (SEND_NEAR, 3),
    (SEND_NEAR, 0), (RELAY, 1), (PASS_TURN, 0), (RELAY, 2), (RELAY, 3), (MODULATE, 0),
    (AUX, 0), (PROJECT, 1), (RELAY_OUT, 0), (RELAY_OUT, 2), (BIAS, 4), (PREPARE, 0),
    (SEND_NEAR, 2), (RELAY_OUT, 3), (RELAY_OUT, 1), (PROJECT, 0), (SPLIT, 0), (ATTEND, 0),
    (BIAS, 5), (CROSS1, 0), (CROSS1, 2), (CROSS1, 1), (SEND, 4), (CROSS1, 3),
    (BACK1, 0), (RELAY, 4), (BACK1, 1), (SEND, 5), (BACK1, 2), (RELAY, 5),
    (DONE1, 0), (BACK1, 3), (DONE1, 2), (BIAS, 6), (DONE1, 1), (DONE1, 3),
    (RELAY_OUT, 4), (RELAY_OUT, 5), (FEED, 0), (CROSS2, 0), (SEND, 6), (BIAS, 7),
    (CROSS2, 2), (SEND, 7), (SEND_NEAR, 4), (CROSS2, 3), (CROSS2, 1), (BACK2, 0),
    (RELAY, 6), (BACK2, 2), (DONE2, 0), (BACK2, 3), (RELAY, 7), (DONE2, 2),
    (BACK2, 1), (DONE2, 1), (DONE2, 3), (ATTEND_BACK, 0), (SHARE_NEAR, 0), (SHARE_FAR, 1),
    (SHARE_FAR, 2), (SHARE_NEAR, 1), (SEND_NEAR, 6), (SEND_NEAR, 5), (SHARE_NEAR, 3), (SHARE_NEAR, 2),
    (RELAY_OUT, 6), (RELAY_OUT, 7), (PASS_FAR, 0), (PASS_FAR, 1), (SHARE_FAR, 3), (SHARE_FAR, 0),
    (PASS_NEAR, 1), (PASS_FAR, 2), (SEND_NEAR, 7), (PASS_FAR, 3), (ATTEND, 1), (CROSS1, 4),
    (PASS_NEAR, 0), (PASS_NEAR, 2), (CROSS1, 6), (CROSS1, 5), (CROSS1, 7), (FEED_OUT, 0),
    (PASS_NEAR, 3), (BACK1, 4), (CROSS3, 1), (BACK1, 6), (BACK1, 5), (CROSS3, 0),
    (DONE1, 5), (PAIR, 0), (BACK1, 7), (CROSS3, 3), (BACK3, 1), (DONE1, 6),
    (CROSS3, 2), (DONE1, 4), (DONE1, 7), (BACK3, 3), (BACK3, 0), (FEED, 1),
    (PROJECT_BACK, 0), (CROSS2, 4), (PAIR, 1), (FEED_OUT, 1), (CROSS2, 7), (CROSS2, 5),
    (CROSS2, 6), (BACK2, 4), (WEIGHTS_FF, 0), (CROSS4, 1), (BACK2, 7), (CROSS4, 2),
    (PAIR, 2), (CROSS4, 3), (BACK2, 6), (CROSS4, 0), (CROSS3, 5), (BACK3, 2),
    (BACK4, 2), (CROSS3, 4), (BACK4, 3), (DONE3, 0), (DONE2, 6), (DONE2, 7),
    (BACK4, 1), (BACK2, 5), (DONE2, 5), (BACK4, 0), (CROSS3, 7), (DONE2, 4),
    (ATTEND_BACK, 1), (PAIR, 3), (PROJECT_BACK, 1), (BACK3, 5), (DONE3, 1), (DONE3, 5),
    (BACK3, 4), (WEIGHTS_ATT, 0), (SHARE_NEAR, 6), (SHARE_NEAR, 5), (SHARE_NEAR, 4), (CROSS4, 5),
    (SHARE_FAR, 4), (DONE4, 0), (CROSS4, 6), (DONE4, 3), (DONE3, 3), (DONE3, 4),
    (PASS_FAR, 6), (PASS_FAR, 4), (SHARE_FAR, 5), (PASS_FAR, 5), (CROSS4, 7), (SHARE_FAR, 6),
    (DONE4, 1), (CROSS3, 6), (PASS_NEAR, 5), (SHARE_NEAR, 7), (PASS_NEAR, 4), (DONE3, 2),
    (DONE4, 2), (SHARE_FAR, 7), (BACK3, 7), (PAIR, 4), (PAIR, 5), (PASS_FAR, 7),
    (BACK4, 6), (CROSS4, 4), (PASS_NEAR, 6), (BACK3, 6), (FINISH, 0), (PAIR, 6),
    (DONE3, 7), (BACK4, 5), (PASS_NEAR, 7), (DONE4, 6), (PAIR, 7), (DONE4, 5),
    (DONE3, 6), (PAIR_END, 0), (BACK4, 4), (BACK4, 7), (DONE4, 4), (DONE4, 7),
    (FINISH, 1), (GRADS, 0),
)


class Place:
    def __init__(self, ndp):
        self.ndp = ndp
        self.dp = dp = lax.axis_index("dp")
        self.t = t = lax.axis_index("tensor")
        self.near_t, self.skip_t, self.far_t = t + 1 - 2 * lax.rem(t, 2), lax.rem(t + 2, 4), 3 - t
        self.near, self.skip, self.far = (dp, self.near_t), (dp, self.skip_t), (dp, self.far_t)
        self.inner = (t == 1) | (t == 2)
        self.first = lax.rem(dp, 2) == 0
        self.twin = (dp + 1 - 2 * lax.rem(dp, 2), t)
        self.outer = (t == 0) | (t == 3)

    def peer(self, step):
        return lax.rem(self.dp + step, self.ndp)

    def greet(self):
        sem = pltpu.get_barrier_semaphore()
        for device in (self.near, self.skip, self.far):
            pl.semaphore_signal(sem, inc=1, device_id=device, device_id_type=MESH)

        @pl.loop(1, self.ndp)
        def _(step):
            pl.semaphore_signal(
                sem, inc=1, device_id=(self.peer(step), self.t), device_id_type=MESH
            )

    def meet(self):
        pl.semaphore_wait(pltpu.get_barrier_semaphore(), 3 + self.ndp - 1)


class Spread:
    def __init__(self, place, source, target, ssem, rsem):
        self.place, self.source, self.target, self.ssem, self.rsem = place, source, target, ssem, rsem

    def copy(self, step):
        there = self.place.peer(step)
        return remote(
            self.source(there),
            self.target.at[self.place.dp],
            self.ssem.at[step],
            self.rsem.at[self.place.dp],
            (there, self.place.t),
        )

    def arrival(self, step):
        there = self.place.peer(step)
        return remote(
            self.source(there),
            self.target.at[there],
            self.ssem.at[step],
            self.rsem.at[there],
            (there, self.place.t),
        )

    def own(self):
        here = self.place.dp
        return pltpu.make_async_copy(self.source(here), self.target.at[here], self.ssem.at[0])

    def start(self):
        self.own().start()

        @pl.loop(1, self.place.ndp)
        def _(step):
            self.copy(step).start()

    def wait(self):
        self.own().wait()

        @pl.loop(1, self.place.ndp)
        def _(step):
            self.copy(step).wait_send()
            self.arrival(step).wait_recv()


class LineSum:
    def __init__(self, place, part, in2, total, sems):
        self.place, self.part, self.in2, self.total, self.sems = place, part, in2, total, sems

    def copy(self, stage, i):
        src = (self.part, self.part, self.total)[stage].at[i]
        dst = (self.total, self.in2, self.total)[stage].at[i]
        device = (self.place.near, self.place.far, self.place.near)[stage]
        return remote(src, dst, self.sems.at[2 * stage, i], self.sems.at[2 * stage + 1, i], device)

    def start(self, i):
        @pl.when(self.place.outer)
        def _():
            self.copy(0, i).start()

    def cross(self, i):
        @pl.when(self.place.inner)
        def _():
            self.copy(0, i).wait_recv()
            self.part[i] = (self.part[i].astype(F32) + self.total[i].astype(F32)).astype(BF16)
            self.copy(1, i).start()

    def back(self, i):
        @pl.when(self.place.inner)
        def _():
            self.copy(1, i).wait_recv()
            self.total[i] = (self.part[i].astype(F32) + self.in2[i].astype(F32)).astype(BF16)
            self.copy(2, i).start()

    def finish(self, i):
        @pl.when(self.place.outer)
        def _():
            self.copy(2, i).wait_recv()

    def drain(self, i):
        @pl.when(self.place.outer)
        def _():
            self.copy(0, i).wait_send()

        @pl.when(self.place.inner)
        def _():
            self.copy(1, i).wait_send()
            self.copy(2, i).wait_send()

    def value(self, b):
        return self.total[b * PARTS : (b + 1) * PARTS].reshape(L, D).astype(F32)


def layer_kernel(
    nb, ndp,
    noise, labels, freq, table, pw, ada, act_in, cot_in, wq_in, wo_in, wgu_in, wd_in, pf,
    sg_o, out_o, in_o, wff_o, watt_o, mg_o, pw_o, aux_o,
    act, cot, wq, wo, wgu, wd, isem, raw, rsem, kw, mod, pbuf, psem,
    bsend, own, ring, inward, across, bsem,
    qs, ks, vs, probs, gate, att, normed_t,
    part1, in1, total1, sem1,
    part2, in2, total2, sem2,
    part3, in3, total3, sem3,
    part4, in4, total4, sem4,
    norm2_t, fgrad, fgrad_t, swish, hgrad, bgrad_t, gated_s, pgrad, mgrad_mid,
    sg, gsem, acc, wff, watt, mgs, pws, aux, out_s, in_s, osem, turn, xsem,
):
    place = Place(ndp)
    place.greet()
    nch = nb * NRC
    slots = pbuf.shape[0]
    rows_per = D // ndp

    def fetch(k, slot):
        b, r = k // NRC, k % NRC
        return pltpu.make_async_copy(pf.at[b, :, pl.ds(r * RC, RC), :], pbuf.at[slot], psem.at[slot])

    fetch(0, 0).start()
    loads = [
        pltpu.make_async_copy(src, dst, isem.at[n])
        for n, (src, dst) in enumerate(
            ((act_in, act), (wq_in, wq), (wo_in, wo), (cot_in, cot), (wd_in, wd))
        )
    ]
    ready = set()

    def need(*numbers):
        for n in numbers:
            if n not in ready:
                ready.add(n)
                loads[n].wait()


    row, col = iota((192, 12), 0), iota((192, 12), 1)
    group, head = row // 48, lax.rem(row // 16, 3)
    owner = jnp.where(
        group == 0,
        place.far_t,
        jnp.where(group == 1, place.skip_t, jnp.where(group == 2, place.near_t, place.t)),
    )
    pick = (col == owner * 3 + head).astype(F32).astype(BF16)
    chosen = nn(pick, pw[...]).astype(BF16)
    channels = pw.shape[1]
    widen = (iota((channels, channels * 16), 1) // 16 == iota((channels, channels * 16), 0)).astype(F32)
    wide = nn(chosen, widen.astype(BF16))
    diagonal = lax.rem(iota(wide.shape, 0), 16) == lax.rem(iota(wide.shape, 1), 16)
    kw[...] = jnp.where(diagonal, wide, 0.0).astype(BF16)

    aux_spread = Spread(place, lambda j: aux.at[j], aux_o, xsem.at[0], xsem.at[1])

    def inwards(k):
        two = pl.ds(0, 2)
        return remote(bsend.at[k, two], inward.at[k, two], bsem.at[0, k], bsem.at[1, k], place.near)

    def to_near(k):
        return remote(bsend.at[k, 2], inward.at[k, 2], bsem.at[6, k], bsem.at[7, k], place.near)

    def crossing(k):
        return remote(
            bsend.at[k, pl.ds(0, 2)], across.at[k], bsem.at[2, k], bsem.at[3, k], place.far
        )

    def outwards(k):
        return remote(bsend.at[k, 2], inward.at[k, 0], bsem.at[4, k], bsem.at[5, k], place.near)

    def bias(k):
        slot = k % slots
        fetch(k, slot).wait()
        if k == 0:
            for n in range(1, slots):
                fetch(n, n).start()
            for load in loads:
                load.start()
        for s in range(RC // 16):
            here = pl.ds(s * 16, 16)
            rows = pbuf[slot, :, here, :].reshape(-1, L)
            out = nn(kw[...], rows)
            three = out[:144].reshape(3, LH, 16, L)

            @pl.when(place.outer)
            def _():
                bsend[k, :, :, here, :] = three.astype(BF16)

            @pl.when(place.inner)
            def _():
                ring[k % RING, :, :, here, :] = three

            own[k, :, here, :] = out[144:].reshape(LH, 16, L)

        if k + slots < nch:
            fetch(k + slots, slot).start()
        if k == nch - 1:
            for n in range(slots):
                fetch(n, n).start()

    def send_bias(k):
        @pl.when(place.outer)
        def _():
            inwards(k).start()

    def send_near(k):
        @pl.when(place.outer)
        def _():
            to_near(k).start()

    def pass_turn(_):
        @pl.when(place.outer & place.first)
        def _():
            inwards(NRC - 1).wait_send()
            pl.semaphore_signal(turn, inc=1, device_id=place.twin, device_id_type=MESH)

    def take_turn(_):
        @pl.when(place.outer & ~place.first)
        def _():
            pl.semaphore_wait(turn, 1)

    def relay(k):
        @pl.when(place.inner)
        def _():
            inwards(k).wait_recv()
            bsend[k, 0] = (ring[k % RING, 0] + inward[k, 1].astype(F32)).astype(BF16)
            bsend[k, 1] = (ring[k % RING, 1] + inward[k, 0].astype(F32)).astype(BF16)
            crossing(k).start()

    def relay_out(k):
        @pl.when(place.inner)
        def _():
            crossing(k).wait_recv()
            bsend[k, 2] = (ring[k % RING, 2] + across[k, 1].astype(F32)).astype(BF16)
            outwards(k).start()

    def modulate():
        def scoped(rows, sem):
            load = pltpu.make_async_copy(ada, rows, sem)
            load.start()
            width = DC // ndp
            conds, hots = [], []
            for b in range(nb):
                phase = (2.0 * math.pi * noise[b]) * freq[...]
                row = jnp.concatenate([jnp.cos(phase), jnp.sin(phase)], axis=1)
                for n in range(NCLASS):
                    row += table[n : n + 1, :].astype(F32) * (labels[b] == n).astype(F32)
                conds.append(row)
                hots.append((iota((1, width), 1) == labels[b]).astype(F32))
            cond = jnp.concatenate(conds, axis=0)
            sigmoid = jax.nn.sigmoid(cond)
            silu = cond * sigmoid
            factor = sigmoid * (1.0 + cond * (1.0 - sigmoid))
            hot = jnp.concatenate(hots, axis=0)
            for j in range(ndp):
                cols = slice(j * width, (j + 1) * width)
                aux[j] = jnp.concatenate([silu[:, cols], factor[:, cols], hot], axis=0)
            terms = jnp.concatenate(in_terms(silu), axis=0)
            load.wait()
            for n in range(6):
                out = nn(terms, rows[n])
                mod[:, n, :] = out[:nb] + out[nb : 2 * nb] + out[2 * nb : 3 * nb]

        pl.run_scoped(scoped, pltpu.VMEM(ada.shape, BF16), pltpu.SemaphoreType.DMA)

    def project(b):
        need(0, 1)
        unit, _ = normalize(act[pl.ds(b * L, L)].astype(F32))
        m = mod[b]
        low = (unit * (1.0 + m[0:1]) + m[1:2]).astype(BF16)
        normed_t[:, pl.ds(b * L, L)] = low.T
        for piece in range(2):
            out = nt(low, wq[pl.ds(piece * 384, 384), :])
            for n in range(6):
                which, h = piece * 2 + n // 3, n % 3
                column = out[:, n * HD : (n + 1) * HD]
                if which == 0:
                    qs[b, h] = (column.astype(BF16).astype(F32) * 0.125).astype(BF16)
                elif which == 1:
                    ks[b, h] = column.astype(BF16)
                elif which == 2:
                    vs[b, h] = column.astype(BF16)
            if piece == 1:
                gate[b] = jax.nn.sigmoid(out[:, LW:])

    sum1 = LineSum(place, part1, in1, total1, sem1)
    sum2 = LineSum(place, part2, in2, total2, sem2)
    sum3 = LineSum(place, part3, in3, total3, sem3)
    sum4 = LineSum(place, part4, in4, total4, sem4)

    def attend(b):
        need(2)
        for k in range(b * NRC, (b + 1) * NRC):

            @pl.when(place.outer)
            def _():
                outwards(k).wait_recv()

            @pl.when(place.inner)
            def _():
                to_near(k).wait_recv()

        heads = []
        for h in range(LH):
            here = slice(b * NRC, (b + 1) * NRC)
            from_near = jnp.where(place.inner, inward[here, 2, h], inward[here, 0, h]).astype(F32)
            from_far = jnp.where(place.inner, across[here, 0, h], jnp.zeros((), BF16)).astype(F32)
            bias_rows = (own[here, h] + (from_near + from_far)).reshape(L, L)
            scores = nt(qs[b, h], ks[b, h]) + bias_rows
            e = jnp.exp(scores - jnp.max(scores, axis=-1, keepdims=True))
            p = (e * (1.0 / jnp.sum(e, axis=-1, keepdims=True))).astype(BF16)
            probs[b, h] = p
            heads.append(nn(p, vs[b, h]))
        attended = jnp.concatenate(heads, axis=1)
        att[b] = attended
        gated = (attended * gate[b]).astype(BF16)
        gated_s[pl.ds(b * L, L)] = gated
        part1[b * PARTS : (b + 1) * PARTS] = nn(gated, wo[...]).astype(BF16).reshape(PARTS, PR, D)
        for i in range(b * PARTS, (b + 1) * PARTS):
            sum1.start(i)

    def raw_rows(n):
        return pltpu.make_async_copy(
            wgu_in.at[pl.ds(n * RAW, RAW)], raw.at[n % 2], rsem.at[n % 2]
        )

    def split_gate_up():
        for n in range(D // RAW):
            raw_rows(n).wait()
            for piece in range(2):
                wgu[pl.ds(n * RAW, RAW), pl.ds(piece * D, D)] = raw[n % 2, :, piece, :]
            if n + 2 < D // RAW:
                raw_rows(n + 2).start()

    def prepare():
        need(3)
        for b in range(nb):
            low = (cot[pl.ds(b * L, L)].astype(F32) * jax.nn.sigmoid(mod[b, 5:6])).astype(BF16)
            fgrad[pl.ds(b * L, L)] = low
            fgrad_t[:, pl.ds(b * L, L)] = low.T

    def middle_of(b):
        rows = act[pl.ds(b * L, L)].astype(F32)
        return rows + jax.nn.sigmoid(mod[b, 2:3]) * sum1.value(b)

    def feedforward(b):
        need(4)
        here = pl.ds(b * L, L)
        unit, _ = normalize(middle_of(b))
        low = (unit * (1.0 + mod[b, 3:4]) + mod[b, 4:5]).astype(BF16)
        norm2_t[:, here] = low.T
        for f in range(3):
            tile, tile_up = pl.ds(f * 256, 256), pl.ds(D + f * 256, 256)
            g = nn(low, wgu[:, tile])
            up = nn(low, wgu[:, tile_up])
            back = nt(fgrad[here], wd[tile, :])
            s = jax.nn.sigmoid(g)
            silu = g * s
            swish[here, tile] = (silu * up).astype(BF16)
            hgrad[here, tile_up] = (back * silu).astype(BF16)
            hgrad[here, tile] = (back * up * s * (1.0 + g * (1.0 - s))).astype(BF16)
        here_parts = pl.ds(b * PARTS, PARTS)
        for d in range(3):
            tile = pl.ds(d * 256, 256)
            part2[here_parts, :, tile] = (
                nt(hgrad[here, :], wgu[tile, :]).astype(BF16).reshape(PARTS, PR, 256)
            )
        for i in range(b * PARTS, (b + 1) * PARTS):
            sum2.start(i)

    def feedforward_out(b):
        here, here_parts = pl.ds(b * L, L), pl.ds(b * PARTS, PARTS)
        for d in range(3):
            tile = pl.ds(d * 256, 256)
            part3[here_parts, :, tile] = (
                nn(swish[here, :], wd[:, tile]).astype(BF16).reshape(PARTS, PR, 256)
            )
        for i in range(b * PARTS, (b + 1) * PARTS):
            sum3.start(i)

    def put_rows(target, tile, values):
        low = values.astype(BF16)
        for j in range(ndp):
            target[j, :, tile] = low[j * rows_per : (j + 1) * rows_per]

    wff_spread = Spread(place, lambda j: wff.at[j], wff_o, xsem.at[2], xsem.at[3])
    watt_spread = Spread(place, lambda j: watt.at[j], watt_o, xsem.at[4], xsem.at[5])

    def weights_ff():
        for f in range(6):
            tile = pl.ds(f * 256, 256)
            put_rows(wff, tile, nn(norm2_t[...], hgrad[:, tile]))
        for f in range(3):
            put_rows(wff, pl.ds(2 * D + f * 256, 256), nn(fgrad_t[...], swish[:, pl.ds(f * 256, 256)]))
        wff_spread.start()

    def weights_att():
        for f in range(3):
            tile = pl.ds(f * 256, 256)
            put_rows(watt, tile, nn(normed_t[...], pgrad[:, tile]))
        put_rows(watt, pl.ds(D, LW), nn(bgrad_t[...], gated_s[...]))
        watt_spread.start()

    def share(k, n):
        source, target, device = (
            (3, 2, place.near),
            (3, 0, place.far),
            (2, 1, place.far),
            (0, 1, place.near),
            (1, 0, place.near),
        )[n]
        return remote(
            sg.at[source, k], sg.at[target, k], gsem.at[2 * n, k], gsem.at[2 * n + 1, k], device
        )

    def share_near(k):
        share(k, 0).start()

    def share_far(k):
        @pl.when(place.inner)
        def _():
            share(k, 1).start()

    def pass_far(k):
        @pl.when(place.inner)
        def _():
            share(k, 0).wait_recv()
            share(k, 2).start()

    def pass_near(k):
        @pl.when(place.inner)
        def _():
            share(k, 1).wait_recv()
            share(k, 3).start()
            share(k, 2).wait_recv()
            share(k, 4).start()

    def attend_back(b):
        here = pl.ds(b * L, L)
        m = mod[b]
        gate_one = jax.nn.sigmoid(m[2:3])
        middle = middle_of(b)
        unit, inverse = normalize(middle)
        two = sum2.value(b)
        up = cot[here].astype(F32)
        mid_grad = up + norm_back(two * (1.0 + m[3:4]), unit, inverse)
        mgrad_mid[here] = mid_grad
        low = (mid_grad * gate_one).astype(BF16)
        bgrad_t[:, here] = low.T
        mgs[b, 2:3] = (
            jnp.sum(mid_grad * sum1.value(b), axis=0, keepdims=True) * gate_one * (1.0 - gate_one)
        )
        mgs[b, 3:4] = jnp.sum(two * unit, axis=0, keepdims=True)
        mgs[b, 4:5] = jnp.sum(two, axis=0, keepdims=True)
        gated_grad = nt(low, wo[...])
        opened = gate[b]
        att_grad = (gated_grad * opened).astype(BF16)
        attended = att[b]
        pgrad[here, pl.ds(3 * LW, LW)] = (gated_grad * attended * opened * (1.0 - opened)).astype(BF16)
        product = att_grad.astype(F32) * attended
        dq, dk, dv = [], [], []
        for h in range(LH):
            cols = slice(h * HD, (h + 1) * HD)
            head_grad = att_grad[:, cols]
            delta = jnp.sum(product[:, cols], axis=-1, keepdims=True)
            p = probs[b, h]
            score_grad = (p.astype(F32) * (nt(head_grad, vs[b, h]) - delta)).astype(BF16)
            for r in range(NRC):
                sg[3, b * NRC + r, h] = score_grad[r * RC : (r + 1) * RC]
            dq.append(nn(score_grad, ks[b, h]) * 0.125)
            dk.append(tn(score_grad, qs[b, h]))
            dv.append(tn(p, head_grad))
        pgrad[here, pl.ds(0, 3 * LW)] = jnp.concatenate(dq + dk + dv, axis=1).astype(BF16)

    def project_back(b):
        here, here_parts = pl.ds(b * L, L), pl.ds(b * PARTS, PARTS)
        for d in range(3):
            tile = pl.ds(d * 256, 256)
            part4[here_parts, :, tile] = (
                nn(pgrad[here, :], wq[:, tile]).astype(BF16).reshape(PARTS, PR, 256)
            )
        for i in range(b * PARTS, (b + 1) * PARTS):
            sum4.start(i)

    def pair_weight(k):
        slot = k % slots

        @pl.when(place.outer)
        def _():
            share(k, 0).wait_recv()
            share(k, 3).wait_recv()
            share(k, 4).wait_recv()

        fetch(k, slot).wait()
        total = None
        for s in range(RC // 16):
            rows = pbuf[slot, :, pl.ds(s * 16, 16), :].reshape(-1, L)
            grads = sg[:, k, :, pl.ds(s * 16, 16), :].reshape(-1, L)
            out = nt(rows, grads)
            total = out if total is None else total + out
        if k == 0:
            acc[...] = total
        else:
            acc[...] += total
        store_sg(k).start()
        if k + slots < nch:
            fetch(k + slots, slot).start()

    def pair_weight_end():
        values = acc[...].reshape(channels, 16, 192)
        mask = iota((16, 192), 0) == lax.rem(iota((16, 192), 1), 16)
        picked = jnp.sum(jnp.where(mask[None], values, 0.0), axis=1)
        row, col = iota((16, 192), 0), iota((16, 192), 1)
        group, head = col // 48, lax.rem(col // 16, 3)
        owner = jnp.where(
            group == 0,
            place.far_t,
            jnp.where(group == 1, place.skip_t, jnp.where(group == 2, place.near_t, place.t)),
        )
        pws[...] = nt((row == owner * 3 + head).astype(F32), picked, precision=highest)
        pw_spread.start()

    def store_sg(k):
        return pltpu.make_async_copy(sg.at[:, k], sg_o.at[:, k], osem.at[0, k])

    def store_rows(b, n):
        source, target = ((out_s, out_o), (in_s, in_o))[n]
        here = pl.ds(b * L, L)
        return pltpu.make_async_copy(source.at[here], target.at[here], osem.at[1 + n, b])

    def finish_rows(b):
        here = pl.ds(b * L, L)
        m = mod[b]
        gate_two = jax.nn.sigmoid(m[5:6])
        ffn = sum3.value(b)
        out_s[here] = (middle_of(b) + gate_two * ffn).astype(BF16)
        mgs[b, 5:6] = (
            jnp.sum(cot[here].astype(F32) * ffn, axis=0, keepdims=True) * gate_two * (1.0 - gate_two)
        )
        unit, inverse = normalize(act[here].astype(F32))
        one = sum4.value(b)
        mgs[b, 0:1] = jnp.sum(one * unit, axis=0, keepdims=True)
        mgs[b, 1:2] = jnp.sum(one, axis=0, keepdims=True)
        in_s[here] = (mgrad_mid[here] + norm_back(one * (1.0 + m[0:1]), unit, inverse)).astype(BF16)
        for n in range(2):
            store_rows(b, n).start()

    mg_spread = Spread(place, lambda j: mgs, mg_o, xsem.at[6], xsem.at[7])
    pw_spread = Spread(place, lambda j: pws, pw_o, xsem.at[8], xsem.at[9])

    sums = (sum1, sum2, sum3, sum4)
    steps = (
        bias,
        send_bias,
        send_near,
        relay,
        relay_out,
        pass_turn,
        take_turn,
        lambda _: modulate(),
        lambda _: aux_spread.start(),
        project,
        lambda _: prepare(),
        lambda _: split_gate_up(),
        attend,
        feedforward,
        feedforward_out,
        attend_back,
        project_back,
        share_near,
        share_far,
        pass_far,
        pass_near,
        pair_weight,
        lambda _: pair_weight_end(),
        lambda _: weights_ff(),
        lambda _: weights_att(),
        finish_rows,
        lambda _: mg_spread.start(),
        *(total.cross for total in sums),
        *(total.back for total in sums),
        *(total.finish for total in sums),
    )
    for kind, number in ORDER:
        steps[kind](number)
        if (kind, number) == (BIAS, 0):
            place.meet()
            for n in range(2):
                raw_rows(n).start()

    for k in range(nch):

        @pl.when(place.outer & ~place.first if k == NRC - 1 else place.outer)
        def _():
            inwards(k).wait_send()

        @pl.when(place.outer)
        def _():
            to_near(k).wait_send()

        @pl.when(place.inner)
        def _():
            crossing(k).wait_send()
            outwards(k).wait_send()
            for n in range(1, 5):
                share(k, n).wait_send()

        share(k, 0).wait_send()
    for total in sums:
        for i in range(PARTS * nb):
            total.drain(i)
    for spread in (aux_spread, wff_spread, watt_spread, mg_spread, pw_spread):
        spread.wait()
    for k in range(nch):
        store_sg(k).wait()
    for b in range(nb):
        for n in range(2):
            store_rows(b, n).wait()


def vmem_specs(n):
    return [pl.BlockSpec(memory_space=pltpu.VMEM)] * n


def any_specs(n):
    return [pl.BlockSpec(memory_space=pl.ANY)] * n


def layer_call(nb, ndp, noise, labels, freq, table, pw, ada, act, cot, wq, wo, wgu, wd, pf):
    nch = nb * NRC
    rows = nb * L
    rows_per = D // ndp
    channels = pf.shape[1]
    hidden = wd.shape[0]
    shapes = [
        ((4, nch, LH, RC, L), BF16),
        ((rows, D), BF16),
        ((rows, D), BF16),
        ((ndp, rows_per, 3 * hidden), BF16),
        ((ndp, rows_per, 5 * LW), BF16),
        ((ndp, nb, 6, D), F32),
        ((ndp, 16, channels), F32),
        ((ndp, 3 * nb, DC // ndp), F32),
    ]
    dma = pltpu.SemaphoreType.DMA

    def line():
        return [pltpu.VMEM((PARTS * nb, PR, D), BF16)] * 3 + [dma((6, PARTS * nb))]

    scratch = [
        pltpu.VMEM((rows, D), BF16),
        pltpu.VMEM((rows, D), BF16),
        pltpu.VMEM(wq.shape, BF16),
        pltpu.VMEM(wo.shape, BF16),
        pltpu.VMEM((D, 2 * hidden), BF16),
        pltpu.VMEM(wd.shape, BF16),
        dma((5,)),
        pltpu.VMEM((2, RAW, 2, hidden), BF16),
        dma((2,)),
        pltpu.VMEM((192, channels * 16), BF16),
        pltpu.VMEM((nb, 6, D), F32),
        pltpu.VMEM((3, channels, RC, L), BF16),
        dma((3,)),
        pltpu.VMEM((nch, 3, LH, RC, L), BF16),
        pltpu.VMEM((nch, LH, RC, L), F32),
        pltpu.VMEM((RING, 3, LH, RC, L), F32),
        pltpu.VMEM((nch, 3, LH, RC, L), BF16),
        pltpu.VMEM((nch, 2, LH, RC, L), BF16),
        dma((8, nch)),
        pltpu.VMEM((nb, LH, L, HD), BF16),
        pltpu.VMEM((nb, LH, L, HD), BF16),
        pltpu.VMEM((nb, LH, L, HD), BF16),
        pltpu.VMEM((nb, LH, L, L), BF16),
        pltpu.VMEM((nb, L, LW), F32),
        pltpu.VMEM((nb, L, LW), F32),
        pltpu.VMEM((D, rows), BF16),
        *line(),
        *line(),
        *line(),
        *line(),
        pltpu.VMEM((D, rows), BF16),
        pltpu.VMEM((rows, D), BF16),
        pltpu.VMEM((D, rows), BF16),
        pltpu.VMEM((rows, hidden), BF16),
        pltpu.VMEM((rows, 2 * hidden), BF16),
        pltpu.VMEM((D, rows), BF16),
        pltpu.VMEM((rows, LW), BF16),
        pltpu.VMEM((rows, 4 * LW), BF16),
        pltpu.VMEM((rows, D), F32),
        pltpu.VMEM((4, nch, LH, RC, L), BF16),
        dma((10, nch)),
        pltpu.VMEM((channels * 16, 192), F32),
        pltpu.VMEM((ndp, rows_per, 3 * hidden), BF16),
        pltpu.VMEM((ndp, rows_per, 5 * LW), BF16),
        pltpu.VMEM((nb, 6, D), F32),
        pltpu.VMEM((16, channels), F32),
        pltpu.VMEM((ndp, 3 * nb, DC // ndp), F32),
        pltpu.VMEM((rows, D), BF16),
        pltpu.VMEM((rows, D), BF16),
        dma((3, nch)),
        pltpu.SemaphoreType.REGULAR,
        dma((10, ndp)),
    ]
    return pl.pallas_call(
        functools.partial(layer_kernel, nb, ndp),
        out_shape=[jax.ShapeDtypeStruct(*s) for s in shapes],
        in_specs=[pl.BlockSpec(memory_space=pltpu.SMEM)] * 2 + vmem_specs(3) + any_specs(8),
        out_specs=any_specs(8),
        scratch_shapes=scratch,
        compiler_params=pltpu.CompilerParams(
            collective_id=0, has_side_effects=True, vmem_limit_bytes=VMEM_LIMIT
        ),
        name="layer",
    )(noise, labels, freq, table, pw, ada, act, cot, wq, wo, wgu, wd, pf)


def ending_kernel(
    nb, ndp,
    pw, mg, aux, pwi, sg_i, ada_i, out_i, in_i, wff_i, watt_i,
    pg, out_o, in_o, ada_o, class_o, wgu_o, wd_o, wq_o, wo_o, pw_o,
    sg, ada, rows, wff, watt, obuf, osem, gsem, isem,
):
    t = lax.axis_index("tensor")
    nch = nb * NRC
    hidden = wd_o.shape[1]
    slots = obuf.shape[0]

    def load(k):
        return pltpu.make_async_copy(sg_i.at[:, k], sg.at[:, k], gsem.at[k])

    others = [
        pltpu.make_async_copy(src, dst, isem.at[n])
        for n, (src, dst) in enumerate(
            (
                (wff_i, wff),
                (watt_i, watt),
                (out_i, rows.at[0]),
                (in_i, rows.at[1]),
                (ada_i, ada),
            )
        )
    ]
    for k in range(nch):
        load(k).start()
        if k == 1:
            for copy in others:
                copy.start()
    passed = [
        pltpu.make_async_copy(rows.at[n], target, isem.at[5 + n])
        for n, target in enumerate((out_o, in_o))
    ]
    channels = pw.shape[1]
    row, col = iota((12, 192), 0), iota((12, 192), 1)
    group, head = col // 48, lax.rem(col // 16, 3)
    near_t, skip_t, far_t = t + 1 - 2 * lax.rem(t, 2), lax.rem(t + 2, 4), 3 - t
    owner = jnp.where(
        group == 0, far_t, jnp.where(group == 1, skip_t, jnp.where(group == 2, near_t, t))
    )
    pick = (row == owner * 3 + head).astype(F32).astype(BF16)
    chosen = tn(pw[...], pick).astype(BF16)
    widen = (iota((channels * 16, channels), 0) // 16 == iota((channels * 16, channels), 1)).astype(F32)
    wide = nn(widen.astype(BF16), chosen)
    diagonal = lax.rem(iota(wide.shape, 0), 16) == lax.rem(iota(wide.shape, 1), 16)
    spread = jnp.where(diagonal, wide, 0.0).astype(BF16)

    def store(k):
        b, r = k // NRC, k % NRC
        return pltpu.make_async_copy(
            obuf.at[k % slots], pg.at[b, :, pl.ds(r * RC, RC), :], osem.at[k % slots]
        )

    def pair_grad(k):
        if k >= slots:
            store(k - slots).wait()
        load(k).wait()
        for s in range(RC // 16):
            grads = sg[:, k, :, pl.ds(s * 16, 16), :].reshape(-1, L)
            obuf[k % slots, :, pl.ds(s * 16, 16), :] = (
                nn(spread, grads).reshape(channels, 16, L).astype(BF16)
            )
        store(k).start()

    def add(source, tile):
        total = source[0, :, tile].astype(F32)
        for j in range(1, ndp):
            total += source[j, :, tile].astype(F32)
        return total

    def ff_sums():
        others[0].wait()
        total = add(wff, pl.ds(0, 3 * hidden))
        wgu_o[:, 0, :] = total[:, :hidden]
        wgu_o[:, 1, :] = total[:, hidden : 2 * hidden]
        wd_o[...] = total[:, 2 * hidden :]

    def att_sums():
        others[1].wait()
        total = add(watt, pl.ds(0, 5 * LW))
        for n in range(4):
            wq_o[:, n, :] = total[:, n * LW : (n + 1) * LW]
        wo_o[...] = total[:, 4 * LW :].T
        total = pwi[0]
        for j in range(1, ndp):
            total += pwi[j]
        pw_o[...] = total[: pw_o.shape[0]]

    def pass_rows():
        for n in range(2):
            others[2 + n].wait()
            passed[n].start()

    def condition():
        def each(kind):
            return jnp.concatenate([aux[j, kind * nb : (kind + 1) * nb] for j in range(ndp)], axis=0)

        others[4].wait()
        silu, factor, hot = each(0), each(1), each(2)
        width = silu.shape[1]
        total = None
        for m in range(6):
            grads = mg[:, m, :]
            ada_o[m] = tn(silu, grads, precision=highest)
            part = nt(jnp.concatenate(in_terms(grads), axis=0), ada[m])
            total = part if total is None else total + part
        rows = total.shape[0] // 3
        back = total[:rows] + total[rows : 2 * rows] + total[2 * rows :]
        here = lax.axis_index("dp") * width
        mine = (iota((DC, width), 0) == here + iota((DC, width), 1)).astype(F32)
        back = nn(back, mine, precision=highest)
        class_o[...] = tn(hot, back * factor, precision=highest)[:NCLASS]

    after = {1: pass_rows, 5: ff_sums, 6: att_sums, 7: condition}
    for k in range(nch):
        pair_grad(k)
        if k in after:
            after[k]()
    for k in range(max(nch - slots, 0), nch):
        store(k).wait()
    for copy in passed:
        copy.wait()


def ending_call(nb, ndp, pw, mg, aux, pwi, sg, ada, out, inputs_grad, wff, watt, pair_shape):
    rows_per = D // ndp
    hidden = wff.shape[2] // 3
    width = DC // ndp
    channels = pair_shape[1]
    dma = pltpu.SemaphoreType.DMA
    shapes = [
        (pair_shape, BF16),
        (out.shape, BF16),
        (out.shape, BF16),
        ((6, width, D), F32),
        ((NCLASS, width), F32),
        ((rows_per, 2, hidden), F32),
        ((rows_per, hidden), F32),
        ((rows_per, 4, LW), F32),
        ((LW, rows_per), F32),
        ((12, channels), F32),
    ]
    return pl.pallas_call(
        functools.partial(ending_kernel, nb, ndp),
        out_shape=[jax.ShapeDtypeStruct(*s) for s in shapes],
        in_specs=vmem_specs(4) + any_specs(6),
        out_specs=any_specs(3) + vmem_specs(7),
        scratch_shapes=[
            pltpu.VMEM(sg.shape, BF16),
            pltpu.VMEM(ada.shape, BF16),
            pltpu.VMEM((2, *out.shape), BF16),
            pltpu.VMEM(wff.shape, BF16),
            pltpu.VMEM(watt.shape, BF16),
            pltpu.VMEM((nb * NRC, channels, RC, L), BF16),
            dma((nb * NRC,)),
            dma((nb * NRC,)),
            dma((7,)),
        ],
        compiler_params=pltpu.CompilerParams(vmem_limit_bytes=VMEM_LIMIT),
        name="ending",
    )(pw, mg, aux, pwi, sg, ada, out, inputs_grad, wff, watt)


def shards(
    ndp,
    activations,
    noise_times,
    cath_labels,
    class_table,
    ada_weight,
    qkvg_weight,
    out_weight,
    pair_weight,
    gateup_weight,
    down_weight,
    pair_features,
    cotangent,
):
    chains = pair_features.shape[0]
    freq = jnp.asarray(np.exp(np.arange(DC // 2) * (math.log(1000.0) / (DC // 2)))[None], F32)
    ada = jnp.transpose(ada_weight, (1, 0, 2))
    wq = jnp.transpose(qkvg_weight, (1, 2, 0)).reshape(-1, D)
    pw = pair_weight.T
    sg, out, inputs_grad, wff, watt, mg, pwi, aux = layer_call(
        chains, ndp, noise_times, cath_labels, freq, class_table, pw, ada, activations, cotangent,
        wq, out_weight, gateup_weight, down_weight, pair_features,
    )
    pair_grad, out, inputs_grad, ada_sum, class_sum, gateup, down, qkvg, outw, pair_sum = ending_call(
        chains, ndp, pw, mg.reshape(-1, 6, D), aux, pwi, sg, ada, out, inputs_grad, wff, watt,
        pair_features.shape,
    )
    return (
        out,
        inputs_grad,
        pair_grad,
        class_sum,
        jnp.transpose(ada_sum, (1, 0, 2)),
        qkvg,
        outw,
        pair_sum.T,
        gateup,
        down.T,
    )


def solution(mesh):
    placed = (
        P("dp", None),
        P("dp"),
        P("dp"),
        P(),
        P(),
        P(None, None, "tensor"),
        P("tensor", None),
        P("tensor", None),
        P(None, None, "tensor"),
        P("tensor", None),
        P("dp", "tensor", None, None),
        P("dp", None),
    )
    return jax.shard_map(
        functools.partial(shards, mesh.shape["dp"]),
        mesh=mesh,
        in_specs=placed,
        out_specs=(
            P("dp", None),
            P("dp", None),
            P("dp", "tensor", None, None),
            P(None, "dp"),
            P("dp", None, None),
            P("dp", None, "tensor"),
            P("tensor", "dp"),
            P("tensor", None),
            P("dp", None, "tensor"),
            P("tensor", "dp"),
        ),
        check_vma=False,
    )
```
